256 devices in a mesh: row: 16 (over z_lo, y), col: 4 (over x), dp: 4 (over z_hi, core).
Axes of the slice: x: 4, y: 4, z: 8 (z_hi: 2, z_lo: 4; z = z_hi * 4 + z_lo), core: 2. Of those that a mesh axis runs over, the one named last changes fastest.
Arguments:
- image: bfloat16 [4, 256, 384, 512], P('dp', None, 'row', 'col'), may hold values from -6 to 6
- labels: int32 [4, 16, 8], P('dp', 'row', 'col'), may hold values from 0 to 7
- weights: float32 [141312], replicated, may hold values from -0.375 to 0.375
- momentum: float32 [141312], P(('row', 'col', 'dp')), may hold values from -0.006 to 0.006
Outputs:
- new_weights: float32 [141312], P(('row', 'col', 'dp'))
- new_momentum: float32 [141312], P(('row', 'col', 'dp'))
- update: float32 [141312], P(('row', 'col', 'dp'))
- loss: float32 [], replicated
The draws below stay inside these ranges and needn't reach their ends.
All inputs are finite; a program needn't handle non-finite values. Where the reference program divides by a largest or mean magnitude, that divisor is 1e-20 or more.
Results may differ from the reference program's by a relative error of at most 0.0011.
Values may be sent and summed in bfloat16 or wider, within the bound.
No kernel may reach another device: no remote copies, remote signals or barrier semaphores. Data moves between devices by JAX's collectives and lax.ppermute only.
A program may use at most 64 MiB of HBM per device.

```python
import jax
import jax.numpy as jnp
from jax import lax

C = 256
MID = 64
CLASSES = 8
TILE_ROWS = 24
TILE_COLS = 64
SLIDES = 4
NR = 384
NC = 512
PARAM = 141312
NTILES = 512


def set_ends(values, rng, smallest, largest):
    dims = values.shape
    place = [jax.random.randint(jax.random.fold_in(rng, axis), (), 0, dims[axis]) for axis in range(len(dims))]
    values = values.at[tuple(place)].set(smallest)
    longest = dims.index(max(dims))
    place[longest] = (place[longest] + 1) % dims[longest]
    return values.at[tuple(place)].set(largest)


def block_levels(own_key, extent, pieces, low, largest):
    loudness, own = 1.0, jax.random.fold_in(own_key, 6)
    for dim, shards_of in pieces:
        steps = jnp.exp(jax.random.uniform(jax.random.fold_in(own, dim), (shards_of,), jnp.float32, low / len(pieces), largest / len(pieces)))
        loudness = loudness * jnp.repeat(steps, extent[dim] // shards_of).reshape([-1 if axis == dim else 1 for axis in range(len(extent))])
    return loudness


def scatter_about(own_key, dims, spread, most, split=(), kind=jnp.bfloat16):
    drawn = jax.random.normal(own_key, dims, jnp.float32) * spread
    if len(split) > 0:
        drawn = block_levels(own_key, dims, split, -0.22, 0.18) * drawn
    return jnp.clip(drawn, min=-most, max=most).astype(kind)


def setup_inputs(seed: int = 0) -> dict:
    seeds = jax.random.split(jax.random.key(seed), 5)
    image = scatter_about(seeds[0], (SLIDES, C, NR, NC), 1.0, 6.0, ((0, 4), (2, 16), (3, 4)))
    labels = set_ends(jax.random.randint(seeds[1], (SLIDES, NR // TILE_ROWS, NC // TILE_COLS), 0, CLASSES), jax.random.fold_in(seeds[1], 1), 0, CLASSES - 1).astype(jnp.int32)
    weights = scatter_about(seeds[2], (PARAM,), C ** -0.5, 0.375, (), jnp.float32)
    momentum = scatter_about(seeds[3], (PARAM,), 0.001, 0.006, ((0, 256),), jnp.float32)
    return dict(image=image, labels=labels, weights=weights, momentum=momentum)


beta_one = 0.9
beta_two = 0.99
learn_rate = 0.0001
weight_decay = 0.1


def product(spec, left, right):
    return jnp.einsum(spec, left.astype(jnp.float32), right.astype(jnp.float32), precision=lax.Precision.HIGHEST)


def unpack(weights):
    offset = 0
    blocks_list = []
    for number in range(2):
        w_in = weights[offset:offset + C * MID].reshape(C, MID)
        offset = offset + C * MID
        w_mid = weights[offset:offset + 9 * MID * MID].reshape(9, MID, MID)
        offset = offset + 9 * MID * MID
        w_out = weights[offset:offset + MID * C].reshape(MID, C)
        offset = offset + MID * C
        blocks_list.append((w_in.astype(jnp.bfloat16), w_mid.astype(jnp.bfloat16), w_out.astype(jnp.bfloat16)))
    head = weights[offset:].reshape(C, CLASSES)
    return blocks_list, head


def border(field):
    return jnp.pad(field, ((0, 0), (1, 1), (1, 1)))


def conv_taps(w_mid, padded, height, width):
    total = jnp.zeros((w_mid.shape[2], height, width), jnp.float32)
    for position in range(9):
        shift_row = position // 3
        shift_col = position % 3
        total = total + product('io,ihw->ohw', w_mid[position], padded[:, shift_row:shift_row + height, shift_col:shift_col + width])
    return total


def slide_terms(slide, label_grid, blocks_list, head):
    height, width = slide.shape[1], slide.shape[2]
    stored = []
    inputs = slide
    for w_in, w_mid, w_out in blocks_list:
        h_first = jnp.maximum(product('io,ihw->ohw', w_in, inputs), 0.0).astype(jnp.bfloat16)
        padded = border(h_first)
        h_second = jnp.maximum(conv_taps(w_mid, padded, height, width), 0.0).astype(jnp.bfloat16)
        output = jnp.maximum(product('io,ihw->ohw', w_out, h_second) + inputs.astype(jnp.float32), 0.0).astype(jnp.bfloat16)
        stored.append((inputs, padded, h_second, output))
        inputs = output
    tiles_a = height // TILE_ROWS
    tiles_b = width // TILE_COLS
    pooled = jnp.mean(inputs.astype(jnp.float32).reshape(C, tiles_a, TILE_ROWS, tiles_b, TILE_COLS), axis=(2, 4))
    logits = product('cab,ck->abk', pooled, head)
    highest = jnp.max(logits, axis=-1, keepdims=True)
    logsum = jnp.log(jnp.sum(jnp.exp(logits - highest), axis=-1, keepdims=True)) + highest
    onehot = (label_grid[:, :, None] == jnp.arange(CLASSES, dtype=jnp.int32)).astype(jnp.float32)
    loss_sum = jnp.sum(logsum[:, :, 0] - jnp.sum(onehot * logits, axis=-1))
    dlogits = (jnp.exp(logits - logsum) - onehot) / NTILES
    grad_head = product('cab,abk->ck', pooled, dlogits)
    dpooled = product('abk,ck->cab', dlogits, head) / (TILE_ROWS * TILE_COLS)
    upstream = jnp.broadcast_to(dpooled[:, :, None, :, None], (C, tiles_a, TILE_ROWS, tiles_b, TILE_COLS)).reshape(C, height, width).astype(jnp.bfloat16)
    grads = [None, None]
    for number in (1, 0):
        w_in, w_mid, w_out = blocks_list[number]
        inputs, padded, h_second, output = stored[number]
        d_sum = jnp.where(output > 0, upstream, jnp.zeros_like(upstream)).astype(jnp.bfloat16)
        grad_out = product('ihw,ohw->io', h_second, d_sum)
        d_second = product('io,ohw->ihw', w_out, d_sum)
        d_second = jnp.where(h_second > 0, d_second, 0.0).astype(jnp.bfloat16)
        grad_mid = jnp.stack([product('ihw,ohw->io', padded[:, position // 3:position // 3 + height, position % 3:position % 3 + width], d_second) for position in range(9)])
        spread_back = border(d_second)
        d_first = jnp.zeros((MID, height, width), jnp.float32)
        for position in range(9):
            shift_row = 2 - position // 3
            shift_col = 2 - position % 3
            d_first = d_first + product('io,ohw->ihw', w_mid[position], spread_back[:, shift_row:shift_row + height, shift_col:shift_col + width])
        h_first = padded[:, 1:-1, 1:-1]
        d_first = jnp.where(h_first > 0, d_first, 0.0).astype(jnp.bfloat16)
        grad_in = product('ihw,ohw->io', inputs, d_first)
        if number == 1:
            upstream = (product('io,ohw->ihw', w_in, d_first) + d_sum.astype(jnp.float32)).astype(jnp.bfloat16)
        grads[number] = jnp.concatenate([grad_in.ravel(), grad_mid.ravel(), grad_out.ravel()])
    flat = jnp.concatenate([grads[0], grads[1], grad_head.ravel()])
    return flat, loss_sum


def reference(image, labels, weights, momentum):
    blocks_list, head = unpack(weights)

    def per_slide(pair):
        return slide_terms(pair[0], pair[1], blocks_list, head)

    flats, losses = lax.map(per_slide, (image, labels))
    grad = jnp.sum(flats, axis=0)
    loss = jnp.sum(losses) / NTILES
    mixed = beta_one * momentum + (1.0 - beta_one) * grad
    scale_tau = jnp.mean(jnp.abs(mixed)) + 1e-6
    update = mixed / (jnp.abs(mixed) + scale_tau)
    new_weights = weights - learn_rate * (update + weight_decay * weights)
    new_momentum = beta_two * momentum + (1.0 - beta_two) * grad
    return new_weights, new_momentum, update, loss
```

```python
import numpy as np
import jax
import jax.numpy as jnp
from jax import lax
from jax.experimental import pallas as pl
from jax.experimental.pallas import tpu as pltpu
from jax.sharding import PartitionSpec as P

C = 256
MID = 64
CLASSES = 8
TILE_ROWS = 24
TILE_COLS = 64
NTILES = 512
PARAM = 141312
SHARE = 552

HALO = 2
ROWS = TILE_ROWS + 2 * HALO
COLS = 2 * TILE_COLS + 2 * HALO
PIX = ROWS * COLS
LANES = 3840
GUARD = 256
WIDE = LANES + 2 * GUARD
CHUNK = 768

BF = jnp.bfloat16
F32 = jnp.float32

RINGS = {
    "y": ("row", 16, 4, 1),
    "z": ("row", 16, 4, 4),
    "x": ("col", 4, 4, 1),
    "core": ("dp", 4, 2, 1),
    "far": ("dp", 4, 2, 2),
}


def rotation(ring, step):
    _, size, group, stride = RINGS[ring]
    pairs = []
    for source in range(size):
        place = (source // stride) % group
        pairs.append((source, source + (((place + step) % group) - place) * stride))
    return pairs


def place_in(ring):
    axis, _, group, stride = RINGS[ring]
    return (lax.axis_index(axis) // stride) % group


def paired_sum(own, got):
    if len(got) == 1:
        return own + got[0]
    return (own + got[1]) + (got[0] + got[2])


def ring_sum(value, ring):
    axis, _, group, _ = RINGS[ring]
    got = [lax.ppermute(value, axis, rotation(ring, k)) for k in range(1, group)]
    return paired_sum(value, got)


def ring_scatter(value, ring):
    axis, _, group, _ = RINGS[ring]
    place = place_in(ring)
    got = [
        lax.ppermute(
            lax.dynamic_index_in_dim(value, (place + k) % group, 0, keepdims=False),
            axis,
            rotation(ring, k),
        )
        for k in range(1, group)
    ]
    own = lax.dynamic_index_in_dim(value, place, 0, keepdims=False)
    return paired_sum(own, got)


def unpack(weights):
    offset = 0
    blocks_list = []
    for number in range(2):
        w_in = weights[offset : offset + C * MID].reshape(C, MID)
        offset = offset + C * MID
        w_mid = weights[offset : offset + 9 * MID * MID].reshape(3, 3, MID, MID)
        offset = offset + 9 * MID * MID
        w_out = weights[offset : offset + MID * C].reshape(MID, C)
        offset = offset + MID * C
        blocks_list.append((w_in.astype(BF), w_mid.astype(BF), w_out.astype(BF)))
    head = weights[offset:].reshape(C, CLASSES)
    return (blocks_list, head)


def nn(left, right):
    return lax.dot_general(left, right, (((1,), (0,)), ((), ())), preferred_element_type=F32)


def nt(left, right):
    return lax.dot_general(left, right, (((1,), (1,)), ((), ())), preferred_element_type=F32)


CHUNKS = [(start, CHUNK) for start in range(0, LANES, CHUNK)]


def shifted(ref, rows, start, size, shift):
    first = GUARD + start + shift
    low = first // 128 * 128
    high = -(-(first + size) // 128) * 128
    return ref[rows, low:high][:, first - low : first - low + size]


def kernel(
    labels,
    x_ref,
    mask_ref,
    win_t1,
    wf1,
    wb1,
    wout_t1,
    wout1,
    win_t2,
    wf2,
    wb2,
    wout_t2,
    wout2,
    win2,
    head_ref,
    flat_ref,
    loss_ref,
    h1a,
    h1b,
    hs1,
    hs2,
    wide,
    h2a,
    h2b,
    y1,
    y2,
    dg2,
    ds,
    dg1,
    dz,
    tall,
):
    everything = slice(None)
    for ref in (h1a, h1b, dg2, wide):
        ref[:, :GUARD] = jnp.zeros((ref.shape[0], GUARD), ref.dtype)
        ref[:, GUARD + LANES :] = jnp.zeros((ref.shape[0], GUARD), ref.dtype)

    def forward(inputs, win_t, wf, wout_t, h1, hs, h2, output, masked):
        for start, size in CHUNKS:
            lanes = slice(start, start + size)
            value = jnp.maximum(nn(win_t[...], inputs[:, lanes]), 0.0)
            if masked:
                value = value * mask_ref[2:3, lanes]
            h1[:, GUARD + start : GUARD + start + size] = value.astype(BF)
        for start, size in CHUNKS:
            lanes = slice(start, start + size)
            for s in range(3):
                hs[s * MID : (s + 1) * MID, lanes] = shifted(h1, everything, start, size, s - 1)
            wide[:, GUARD + start : GUARD + start + size] = nn(wf[...], hs[:, lanes])
        for start, size in CHUNKS:
            lanes = slice(start, start + size)
            total = sum(
                shifted(wide, slice(r * MID, (r + 1) * MID), start, size, (r - 1) * COLS)
                for r in range(3)
            )
            value = jnp.maximum(total, 0.0).astype(BF)
            h2[:, lanes] = value
            output[:, lanes] = jnp.maximum(
                nn(wout_t[...], value) + inputs[:, lanes].astype(F32), 0.0
            ).astype(BF)

    forward(x_ref, win_t1, wf1, wout_t1, h1a, hs1, h2a, y1, False)
    forward(y1, win_t2, wf2, wout_t2, h1b, hs2, h2b, y2, True)

    tile_masks = mask_ref[0:8, :]
    pooled = nt(y2[...], tile_masks.astype(BF)) * (1.0 / (TILE_ROWS * TILE_COLS))
    head = head_ref[...]
    classes = lax.broadcasted_iota(jnp.int32, (1, CLASSES), 1)
    loss = jnp.zeros((1, 1), F32)
    grad_head = jnp.zeros((C, CLASSES), F32)
    spread = []
    for tile in range(2):
        column = pooled[:, tile : tile + 1]
        logits = jnp.sum(column * head, axis=0, keepdims=True)
        highest = jnp.max(logits, axis=1, keepdims=True)
        logsum = jnp.log(jnp.sum(jnp.exp(logits - highest), axis=1, keepdims=True)) + highest
        onehot = (classes == labels[tile]).astype(F32)
        loss = loss + logsum - jnp.sum(onehot * logits, axis=1, keepdims=True)
        dlogits = (jnp.exp(logits - logsum) - onehot) * (1.0 / NTILES)
        grad_head = grad_head + column * dlogits
        dpooled = jnp.sum(head * dlogits, axis=1, keepdims=True) / (TILE_ROWS * TILE_COLS)
        spread.append(dpooled.astype(BF).astype(F32))
    loss_ref[...] = jnp.broadcast_to(loss, (8, 128))

    for start, size in CHUNKS:
        lanes = slice(start, start + size)
        upstream = spread[0] * mask_ref[0:1, lanes] + spread[1] * mask_ref[1:2, lanes]
        dz[:, lanes] = jnp.where(y2[:, lanes].astype(F32) > 0, upstream, 0.0).astype(BF)

    def pack_tall(value, row):
        count = value.shape[0]
        tall[0:count, :] = value
        half = count // 2
        flat_ref[row : row + half, 0:MID] = tall[pl.ds(0, half, stride=2), :]
        flat_ref[row : row + half, MID:] = tall[pl.ds(1, half, stride=2), :]

    def backward(inputs, wb, wout, h1, hs, h2, row, then):
        grad_out = nt(h2[...], dz[...])
        flat_ref[pl.ds(row + 416, MID, stride=2), :] = grad_out[:, :128]
        flat_ref[pl.ds(row + 417, MID, stride=2), :] = grad_out[:, 128:]
        for start, size in CHUNKS:
            lanes = slice(start, start + size)
            value = nn(wout[...], dz[:, lanes])
            value = jnp.where(h2[:, lanes].astype(F32) > 0, value, 0.0)
            dg2[:, GUARD + start : GUARD + start + size] = value.astype(BF)
        for start, size in CHUNKS:
            lanes = slice(start, start + size)
            for r in range(3):
                ds[r * MID : (r + 1) * MID, lanes] = shifted(
                    dg2, everything, start, size, (1 - r) * COLS
                )
            wide[:, GUARD + start : GUARD + start + size] = nn(wb[...], ds[:, lanes])
        grad_mid = nt(hs[...], ds[...])
        for r in range(3):
            pack_tall(grad_mid[:, r * MID : (r + 1) * MID], row + 128 + r * 96)
        for start, size in CHUNKS:
            lanes = slice(start, start + size)
            total = sum(
                shifted(wide, slice(s * MID, (s + 1) * MID), start, size, 1 - s) for s in range(3)
            )
            kept = h1[:, GUARD + start : GUARD + start + size].astype(F32) > 0
            value = jnp.where(kept, total, 0.0).astype(BF)
            dg1[:, lanes] = value
            if then is not None:
                then(lanes, value)
        pack_tall(nt(inputs[...], dg1[...]), row)

    def to_first(lanes, value):
        total = nn(win2[...], value) + dz[:, lanes].astype(F32)
        dz[:, lanes] = jnp.where(y1[:, lanes].astype(F32) > 0, total, 0.0).astype(BF)

    backward(y1, wb2, wout2, h1b, hs2, h2b, 544, to_first)
    backward(x_ref, wb1, wout1, h1a, hs1, h2a, 0, None)
    tall[:, 0:CLASSES] = grad_head
    for j in range(16):
        flat_ref[1088:1104, j * CLASSES : (j + 1) * CLASSES] = tall[
            pl.ds(j, 16, stride=16), 0:CLASSES
        ]


def compute(labels, x_flat, masks, blocks_list, head):
    (win1, wmid1, wout1), (win2, wmid2, wout2) = blocks_list
    wf = [w.transpose(0, 3, 1, 2).reshape(3 * MID, 3 * MID) for w in (wmid1, wmid2)]
    wb = [w.transpose(1, 2, 0, 3).reshape(3 * MID, 3 * MID) for w in (wmid1, wmid2)]
    vmem = pl.BlockSpec(memory_space=pltpu.VMEM)
    smem = pl.BlockSpec(memory_space=pltpu.SMEM)
    return pl.pallas_call(
        kernel,
        out_shape=(
            jax.ShapeDtypeStruct((PARAM // 128, 128), F32),
            jax.ShapeDtypeStruct((8, 128), F32),
        ),
        in_specs=[smem] + [vmem] * 14,
        out_specs=(vmem, vmem),
        scratch_shapes=[
            pltpu.VMEM((MID, WIDE), BF),
            pltpu.VMEM((MID, WIDE), BF),
            pltpu.VMEM((3 * MID, LANES), BF),
            pltpu.VMEM((3 * MID, LANES), BF),
            pltpu.VMEM((3 * MID, WIDE), F32),
            pltpu.VMEM((MID, LANES), BF),
            pltpu.VMEM((MID, LANES), BF),
            pltpu.VMEM((C, LANES), BF),
            pltpu.VMEM((C, LANES), BF),
            pltpu.VMEM((MID, WIDE), BF),
            pltpu.VMEM((3 * MID, LANES), BF),
            pltpu.VMEM((MID, LANES), BF),
            pltpu.VMEM((C, LANES), BF),
            pltpu.VMEM((C, MID), F32),
        ],
        compiler_params=pltpu.CompilerParams(vmem_limit_bytes=48 * 1024 * 1024),
    )(
        labels,
        x_flat,
        masks,
        win1.T,
        wf[0],
        wb[0],
        wout1.T,
        wout1,
        win2.T,
        wf[1],
        wb[1],
        wout2.T,
        wout2,
        win2,
        head,
    )


def neighbours(low_part, high_part, axis):
    count = lax.axis_size(axis)
    up = [(i, i + 1) for i in range(count - 1)]
    down = [(target, source) for source, target in up]
    return lax.ppermute(high_part, axis, up), lax.ppermute(low_part, axis, down)


def extended(inputs):
    height, width = inputs.shape[1:]
    left, right = neighbours(
        inputs[:, :, :HALO].reshape(C, -1), inputs[:, :, width - HALO :].reshape(C, -1), "col"
    )
    wide = jnp.concatenate(
        [left.reshape(C, height, HALO), inputs, right.reshape(C, height, HALO)], axis=2
    )
    top, bottom = neighbours(
        wide[:, :HALO].reshape(C, -1), wide[:, height - HALO :].reshape(C, -1), "row"
    )
    body = wide.reshape(C, -1)
    return jnp.concatenate([top, body, bottom, jnp.zeros((C, LANES - PIX), BF)], axis=1)


def make_masks():
    pixel = np.arange(LANES)
    r, c = pixel // COLS - HALO, pixel % COLS - HALO
    inside = (pixel < PIX) & (r >= 0) & (r < TILE_ROWS)
    tiles = [inside & (c >= t * TILE_COLS) & (c < (t + 1) * TILE_COLS) for t in range(2)]
    near = (pixel < PIX) & (r >= -1) & (r <= TILE_ROWS) & (c >= -1) & (c <= 2 * TILE_COLS)
    row, col = lax.axis_index("row"), lax.axis_index("col")
    rows, cols = lax.axis_size("row"), lax.axis_size("col")
    image = (
        jnp.asarray(near)
        & (jnp.asarray(r >= 0) | (row > 0))
        & (jnp.asarray(r < TILE_ROWS) | (row < rows - 1))
        & (jnp.asarray(c >= 0) | (col > 0))
        & (jnp.asarray(c < 2 * TILE_COLS) | (col < cols - 1))
    )
    lines = [jnp.asarray(tiles[0], F32), jnp.asarray(tiles[1], F32), image.astype(F32)]
    return jnp.stack(lines + [jnp.zeros((LANES,), F32)] * 5)


def local(image, labels, weights, momentum):
    blocks_list, head = unpack(weights)
    flat, loss_part = compute(
        labels.reshape(2), extended(image[0]), make_masks(), blocks_list, head
    )

    parts = flat.reshape(16, 4, 2, 2, SHARE).transpose(3, 1, 2, 0, 4)
    loss_column = jnp.broadcast_to(loss_part[0, 0], (2, 4, 2, 16, 1))
    parts = jnp.concatenate([parts, loss_column], axis=-1).reshape(2, 4, 32, SHARE + 1)
    parts = ring_scatter(ring_scatter(parts, "core"), "x")
    mine = place_in("far") * 16 + lax.axis_index("row")
    at_home = (jnp.arange(32) == mine)[:, None]
    parts = parts + jnp.where(at_home, 9.0 * jnp.pad(momentum, (0, 1))[None], 0.0)
    for ring in ("y", "z", "far"):
        parts = ring_sum(parts, ring)
    magnitude = jnp.full((8, 128), jnp.sum(jnp.abs(parts[:, :SHARE])))
    for ring in ("core", "x"):
        magnitude = ring_sum(magnitude, ring)
    scale_tau = 0.1 * magnitude[0, 0] / PARAM + 1e-06
    own = lax.dynamic_index_in_dim(parts, mine, 0, keepdims=False)
    loss = own[SHARE] / NTILES
    own = own[:SHARE]
    mixed = 0.1 * own
    update = mixed / (jnp.abs(mixed) + scale_tau)
    start = (lax.axis_index("row") * 16 + lax.axis_index("col") * 4 + lax.axis_index("dp")) * SHARE
    weight_share = lax.dynamic_slice_in_dim(weights, start, SHARE, 0)
    new_weights = weight_share - 0.0001 * (update + 0.1 * weight_share)
    new_momentum = 0.9 * momentum + 0.01 * own
    return (new_weights, new_momentum, update, loss)


def solution(mesh):
    in_specs = (P("dp", None, "row", "col"), P("dp", "row", "col"), P(), P(("row", "col", "dp")))
    out_specs = (P(("row", "col", "dp")), P(("row", "col", "dp")), P(("row", "col", "dp")), P())
    return jax.shard_map(local, mesh=mesh, in_specs=in_specs, out_specs=out_specs, check_vma=False)
```

```python
import numpy as np
import jax
import jax.numpy as jnp
from jax import lax
from jax.experimental import pallas as pl
from jax.experimental.pallas import tpu as pltpu
from jax.sharding import PartitionSpec as P

C = 256
MID = 64
CLASSES = 8
TILE_ROWS = 24
TILE_COLS = 64
NTILES = 512
PARAM = 141312
SHARE = 552

HALO = 2
ROWS = TILE_ROWS + 2 * HALO
COLS = 2 * TILE_COLS + 2 * HALO
PIX = ROWS * COLS
LANES = 3840
GUARD = 256
WIDE = LANES + 2 * GUARD
CHUNK = 768

BF = jnp.bfloat16
F32 = jnp.float32

SHARES = 32
PAD = 640


def exchange(size, partner):
    return [(source, partner(source)) for source in range(size)]


def neighbours(size, odd, wrap=False):
    pairs = []
    for low in range(1 if odd else 0, size - 1, 2):
        pairs += [(low, low + 1), (low + 1, low)]
    if odd and wrap:
        pairs += [(0, size - 1), (size - 1, 0)]
    return pairs


def along_z(partner):
    pairs = []
    for row in range(16):
        for dp in range(4):
            z = partner(dp // 2 * 4 + row // 4)
            pairs.append((row * 4 + dp, (z % 4 * 4 + row % 4) * 4 + z // 4 * 2 + dp % 2))
    return pairs


def z_near(z):
    return (3, 2, 1, 0, 7, 6, 5, 4)[z]


CORE = ("dp", [exchange(4, lambda i: i ^ 1)])
X_RING = ("col", [exchange(4, lambda i, k=k: i ^ k) for k in (1, 3, 2)])
Y_RING = ("row", [exchange(16, lambda i, k=k: i ^ k) for k in (1, 3, 2)])
Z_PAIR = (("row", "dp"), [along_z(lambda z: z ^ 1)])
Z_RING = (
    ("row", "dp"),
    [along_z(z_near), along_z(lambda z: 7 - z), along_z(lambda z: z_near(7 - z))],
)


def received(values, stage):
    axis, exchanges = stage
    return [lax.ppermute(value, axis, pairs) for value, pairs in zip(values, exchanges)]


def paired_sum(own, got):
    if len(got) == 1:
        return own + got[0]
    return (own + got[0]) + (got[1] + got[2])


def stage_sum(value, stage):
    return paired_sum(value, received([value] * len(stage[1]), stage))


def unpack(weights):
    offset = 0
    blocks_list = []
    for number in range(2):
        w_in = weights[offset : offset + C * MID].reshape(C, MID)
        offset = offset + C * MID
        w_mid = weights[offset : offset + 9 * MID * MID].reshape(3, 3, MID, MID)
        offset = offset + 9 * MID * MID
        w_out = weights[offset : offset + MID * C].reshape(MID, C)
        offset = offset + MID * C
        blocks_list.append((w_in.astype(BF), w_mid.astype(BF), w_out.astype(BF)))
    head = weights[offset:].reshape(C, CLASSES)
    return (blocks_list, head)


def nn(left, right):
    return lax.dot_general(left, right, (((1,), (0,)), ((), ())), preferred_element_type=F32)


def nt(left, right):
    return lax.dot_general(left, right, (((1,), (1,)), ((), ())), preferred_element_type=F32)


CHUNKS = [(start, CHUNK) for start in range(0, LANES, CHUNK)]


def shifted(ref, rows, start, size, shift):
    first = GUARD + start + shift
    low = first // 128 * 128
    high = -(-(first + size) // 128) * 128
    return ref[rows, low:high][:, first - low : first - low + size]


def split_kernel(image_ref, own_ref, edge_ref, tall, select):
    tall[...] = image_ref[...].astype(F32).reshape(C * TILE_ROWS, 128)
    lane = lax.broadcasted_iota(jnp.int32, (128, 128), 1)
    col = lax.broadcasted_iota(jnp.int32, (128, 128), 0)
    for r in range(TILE_ROWS):
        own_ref[:, r * 128 : (r + 1) * 128] = tall[pl.ds(r, C, stride=TILE_ROWS), :].astype(BF)
        wanted = jnp.where(col < HALO, col + 64, jnp.where(col >= 126, col - 126, -1000))
        select[r * 128 : (r + 1) * 128, :] = (lane - 2 * r == wanted).astype(F32).astype(BF)
    edge_ref[...] = nn(own_ref[...], select[...]).astype(BF)


def rim_kernel(place, own_ref, even_ref, odd_ref, rim_ref, up_ref, down_ref):
    row, col = place[0], place[1]
    lane = lax.broadcasted_iota(jnp.int32, (C, 128), 1)
    odd_col = lax.rem(col, 2)
    from_even = even_ref[...].astype(F32)
    from_odd = odd_ref[...].astype(F32)
    by_even = (lane < 64).astype(jnp.int32) == odd_col
    outside = ((lane < 64) & (col == 0)) | ((lane >= 64) & (col == 3))
    rim = jnp.where(outside, 0.0, jnp.where(by_even, from_even, from_odd)).astype(BF)
    rim_ref[...] = rim
    odd_row = lax.rem(row, 2)
    high = (TILE_ROWS - HALO) * 128
    first = pl.multiple_of((1 - odd_row) * high, 128)
    second = pl.multiple_of(odd_row * high, 128)
    up_ref[:, 0:256] = own_ref[:, pl.ds(first, 256)]
    up_ref[:, 256:384] = rim
    down_ref[:, 0:256] = own_ref[:, pl.ds(second, 256)]
    down_ref[:, 256:384] = rim


def kernel(
    labels,
    place,
    own_ref,
    rim_ref,
    even_ref,
    odd_ref,
    mask_ref,
    momentum_ref,
    win_t1,
    wf1,
    wb1,
    wout_t1,
    wout1,
    win_t2,
    wf2,
    wb2,
    wout_t2,
    wout2,
    win2,
    head_ref,
    keep_ref,
    send_ref,
    flat_ref,
    parts,
    x_ref,
    h1a,
    h1b,
    hs1,
    hs2,
    wide,
    h2a,
    h2b,
    y1,
    y2,
    dg2,
    ds,
    dg1,
    dz,
    tall,
):
    everything = slice(None)
    for ref in (h1a, h1b, dg2, wide):
        ref[:, :GUARD] = jnp.zeros((ref.shape[0], GUARD), ref.dtype)
        ref[:, GUARD + LANES :] = jnp.zeros((ref.shape[0], GUARD), ref.dtype)

    odd_row = lax.rem(place[0], 2) == 1
    above = jnp.where(odd_row, even_ref[...].astype(F32), odd_ref[...].astype(F32)).astype(BF)
    below = jnp.where(odd_row, odd_ref[...].astype(F32), even_ref[...].astype(F32)).astype(BF)
    for start, size in CHUNKS:
        lanes = slice(start, start + size)
        source = lax.broadcasted_iota(jnp.int32, (128, size), 0).astype(F32)
        placed = [(source == mask_ref[k : k + 1, lanes]).astype(F32).astype(BF) for k in (3, 4, 5)]
        value = nn(rim_ref[...], placed[0])
        if start == 0:
            value = value + nn(above[:, 256:], placed[1])
        if start + size == LANES:
            value = value + nn(below[:, 256:], placed[2])
        x_ref[:, lanes] = value.astype(BF)
    for r in range(ROWS):
        if r < HALO:
            line = above[:, r * 128 : (r + 1) * 128]
        elif r < ROWS - HALO:
            line = own_ref[:, (r - HALO) * 128 : (r - HALO + 1) * 128]
        else:
            line = below[:, (r - ROWS + HALO) * 128 : (r - ROWS + HALO + 1) * 128]
        x_ref[:, r * COLS + HALO : r * COLS + HALO + 128] = line

    def forward(inputs, win_t, wf, wout_t, h1, hs, h2, output, masked):
        for start, size in CHUNKS:
            lanes = slice(start, start + size)
            value = jnp.maximum(nn(win_t[...], inputs[:, lanes]), 0.0)
            if masked:
                value = value * mask_ref[2:3, lanes]
            h1[:, GUARD + start : GUARD + start + size] = value.astype(BF)
        for start, size in CHUNKS:
            lanes = slice(start, start + size)
            for s in range(3):
                hs[s * MID : (s + 1) * MID, lanes] = shifted(h1, everything, start, size, s - 1)
            wide[:, GUARD + start : GUARD + start + size] = nn(wf[...], hs[:, lanes])
        for start, size in CHUNKS:
            lanes = slice(start, start + size)
            total = sum(
                shifted(wide, slice(r * MID, (r + 1) * MID), start, size, (r - 1) * COLS)
                for r in range(3)
            )
            value = jnp.maximum(total, 0.0).astype(BF)
            h2[:, lanes] = value
            output[:, lanes] = jnp.maximum(
                nn(wout_t[...], value) + inputs[:, lanes].astype(F32), 0.0
            ).astype(BF)

    forward(x_ref, win_t1, wf1, wout_t1, h1a, hs1, h2a, y1, False)
    forward(y1, win_t2, wf2, wout_t2, h1b, hs2, h2b, y2, True)

    tile_masks = mask_ref[0:8, :]
    pooled = nt(y2[...], tile_masks.astype(BF)) * (1.0 / (TILE_ROWS * TILE_COLS))
    head = head_ref[...]
    classes = lax.broadcasted_iota(jnp.int32, (1, CLASSES), 1)
    loss = jnp.zeros((1, 1), F32)
    grad_head = jnp.zeros((C, CLASSES), F32)
    spread = []
    for tile in range(2):
        column = pooled[:, tile : tile + 1]
        logits = jnp.sum(column * head, axis=0, keepdims=True)
        highest = jnp.max(logits, axis=1, keepdims=True)
        logsum = jnp.log(jnp.sum(jnp.exp(logits - highest), axis=1, keepdims=True)) + highest
        onehot = (classes == labels[tile]).astype(F32)
        loss = loss + logsum - jnp.sum(onehot * logits, axis=1, keepdims=True)
        dlogits = (jnp.exp(logits - logsum) - onehot) * (1.0 / NTILES)
        grad_head = grad_head + column * dlogits
        dpooled = jnp.sum(head * dlogits, axis=1, keepdims=True) / (TILE_ROWS * TILE_COLS)
        spread.append(dpooled.astype(BF).astype(F32))

    for start, size in CHUNKS:
        lanes = slice(start, start + size)
        upstream = spread[0] * mask_ref[0:1, lanes] + spread[1] * mask_ref[1:2, lanes]
        dz[:, lanes] = jnp.where(y2[:, lanes].astype(F32) > 0, upstream, 0.0).astype(BF)

    def pack_tall(value, row):
        count = value.shape[0]
        tall[0:count, :] = value
        half = count // 2
        flat_ref[row : row + half, 0:MID] = tall[pl.ds(0, half, stride=2), :]
        flat_ref[row : row + half, MID:] = tall[pl.ds(1, half, stride=2), :]

    def backward(inputs, wb, wout, h1, hs, h2, row, then):
        grad_out = nt(h2[...], dz[...])
        flat_ref[pl.ds(row + 416, MID, stride=2), :] = grad_out[:, :128]
        flat_ref[pl.ds(row + 417, MID, stride=2), :] = grad_out[:, 128:]
        for start, size in CHUNKS:
            lanes = slice(start, start + size)
            value = nn(wout[...], dz[:, lanes])
            value = jnp.where(h2[:, lanes].astype(F32) > 0, value, 0.0)
            dg2[:, GUARD + start : GUARD + start + size] = value.astype(BF)
        for start, size in CHUNKS:
            lanes = slice(start, start + size)
            for r in range(3):
                ds[r * MID : (r + 1) * MID, lanes] = shifted(
                    dg2, everything, start, size, (1 - r) * COLS
                )
            wide[:, GUARD + start : GUARD + start + size] = nn(wb[...], ds[:, lanes])
        grad_mid = nt(hs[...], ds[...])
        for r in range(3):
            pack_tall(grad_mid[:, r * MID : (r + 1) * MID], row + 128 + r * 96)
        for start, size in CHUNKS:
            lanes = slice(start, start + size)
            total = sum(
                shifted(wide, slice(s * MID, (s + 1) * MID), start, size, 1 - s) for s in range(3)
            )
            kept = h1[:, GUARD + start : GUARD + start + size].astype(F32) > 0
            value = jnp.where(kept, total, 0.0).astype(BF)
            dg1[:, lanes] = value
            if then is not None:
                then(lanes, value)
        pack_tall(nt(inputs[...], dg1[...]), row)

    def to_first(lanes, value):
        total = nn(win2[...], value) + dz[:, lanes].astype(F32)
        dz[:, lanes] = jnp.where(y1[:, lanes].astype(F32) > 0, total, 0.0).astype(BF)

    backward(y1, wb2, wout2, h1b, hs2, h2b, 544, to_first)
    backward(x_ref, wb1, wout1, h1a, hs1, h2a, 0, None)
    tall[:, 0:CLASSES] = grad_head
    for j in range(16):
        flat_ref[1088:1104, j * CLASSES : (j + 1) * CLASSES] = tall[
            pl.ds(j, 16, stride=16), 0:CLASSES
        ]

    row, col, core, far = place[0], place[1], place[2], place[3]
    lane = lax.broadcasted_iota(jnp.int32, (16, 128), 1)
    for m in range(16):
        m_col, m_far, m_core = m // 4, m // 2 % 2, m % 2
        first, offset = SHARE * m // 128, SHARE * m % 128
        lines = [
            pltpu.roll(flat_ref[pl.ds(first + j, 16, stride=69), :], (128 - offset) % 128, 1)
            for j in range(6)
        ]
        block = parts.at[m_core ^ core, m_col ^ col]
        for j in range(5):
            value = jnp.where(lane < 128 - offset, lines[j], lines[j + 1])
            if j == 4:
                value = jnp.where(lane < 40, value, jnp.where(lane == 40, loss, 0.0))
            block[m_far * 16 : m_far * 16 + 16, j * 128 : (j + 1) * 128] = value
    mine = far * 16 + row
    parts[0, 0, pl.ds(mine, 1), :] = parts[0, 0, pl.ds(mine, 1), :] + 9.0 * momentum_ref[...]
    keep_ref[...] = parts[0]
    send_ref[...] = parts[1]


def total_kernel(place, own, got_a, got_b, got_c, row_ref, size_ref):
    total = (own[...] + got_a[...]) + (got_b[...] + got_c[...])
    lane = lax.broadcasted_iota(jnp.int32, (SHARES, PAD), 1)
    kept = jnp.where(lane < SHARE, jnp.abs(total), 0.0)
    size = jnp.sum(jnp.sum(kept, axis=0, keepdims=True), axis=1, keepdims=True)
    size_ref[...] = jnp.broadcast_to(size, (1, PAD))
    mine = place[3] * 16 + place[0]
    line = lax.broadcasted_iota(jnp.int32, (SHARES, PAD), 0)
    row_ref[...] = jnp.sum(jnp.where(line == mine, total, 0.0), axis=0, keepdims=True)


VMEM = pl.BlockSpec(memory_space=pltpu.VMEM)
SMEM = pl.BlockSpec(memory_space=pltpu.SMEM)
PARAMS = pltpu.CompilerParams(vmem_limit_bytes=48 * 1024 * 1024)


def shape(dims, kind):
    return jax.ShapeDtypeStruct(dims, kind)


def split(image):
    return pl.pallas_call(
        split_kernel,
        out_shape=(shape((C, TILE_ROWS * 128), BF), shape((C, 128), BF)),
        in_specs=[VMEM],
        out_specs=(VMEM, VMEM),
        scratch_shapes=[
            pltpu.VMEM((C * TILE_ROWS, 128), F32),
            pltpu.VMEM((TILE_ROWS * 128, 128), BF),
        ],
        compiler_params=PARAMS,
    )(image)


def rim(place, own, even, odd):
    return pl.pallas_call(
        rim_kernel,
        out_shape=(shape((C, 128), BF), shape((C, 384), BF), shape((C, 384), BF)),
        in_specs=[SMEM] + [VMEM] * 3,
        out_specs=(VMEM,) * 3,
        compiler_params=PARAMS,
    )(place, own, even, odd)


def compute(labels, place, pieces, masks, momentum, blocks_list, head):
    (win1, wmid1, wout1), (win2, wmid2, wout2) = blocks_list
    wf = [w.transpose(0, 3, 1, 2).reshape(3 * MID, 3 * MID) for w in (wmid1, wmid2)]
    wb = [w.transpose(1, 2, 0, 3).reshape(3 * MID, 3 * MID) for w in (wmid1, wmid2)]
    return pl.pallas_call(
        kernel,
        out_shape=(shape((4, SHARES, PAD), F32), shape((4, SHARES, PAD), F32)),
        in_specs=[SMEM, SMEM] + [VMEM] * 18,
        out_specs=(VMEM, VMEM),
        scratch_shapes=[
            pltpu.VMEM((PARAM // 128 + 8, 128), F32),
            pltpu.VMEM((2, 4, SHARES, PAD), F32),
            pltpu.VMEM((C, LANES), BF),
            pltpu.VMEM((MID, WIDE), BF),
            pltpu.VMEM((MID, WIDE), BF),
            pltpu.VMEM((3 * MID, LANES), BF),
            pltpu.VMEM((3 * MID, LANES), BF),
            pltpu.VMEM((3 * MID, WIDE), F32),
            pltpu.VMEM((MID, LANES), BF),
            pltpu.VMEM((MID, LANES), BF),
            pltpu.VMEM((C, LANES), BF),
            pltpu.VMEM((C, LANES), BF),
            pltpu.VMEM((MID, WIDE), BF),
            pltpu.VMEM((3 * MID, LANES), BF),
            pltpu.VMEM((MID, LANES), BF),
            pltpu.VMEM((C, LANES), BF),
            pltpu.VMEM((C, MID), F32),
        ],
        compiler_params=PARAMS,
    )(
        labels,
        place,
        *pieces,
        masks,
        momentum,
        win1.T,
        wf[0],
        wb[0],
        wout1.T,
        wout1,
        win2.T,
        wf[1],
        wb[1],
        wout2.T,
        wout2,
        win2,
        head,
    )


def make_masks(row, col):
    pixel = np.arange(LANES)
    r, c = pixel // COLS - HALO, pixel % COLS - HALO
    real = pixel < PIX
    inside = real & (r >= 0) & (r < TILE_ROWS)
    tiles = [inside & (c >= t * TILE_COLS) & (c < (t + 1) * TILE_COLS) for t in range(2)]
    near = real & (r >= -1) & (r <= TILE_ROWS) & (c >= -1) & (c <= 2 * TILE_COLS)
    lane = np.where(c < 0, 2 * r + c + HALO, np.where(c >= 128, 64 + 2 * r + c - 128, -1000))
    sources = [
        np.where(inside, lane, -1000),
        np.where(real & (r < 0) & (lane > -500), lane + 2 * TILE_ROWS, -1000),
        np.where(real & (r >= TILE_ROWS) & (lane > -500), lane - 2 * TILE_ROWS, -1000),
    ]
    rows, cols = lax.axis_size("row"), lax.axis_size("col")
    image = (
        jnp.asarray(near)
        & (jnp.asarray(r >= 0) | (row > 0))
        & (jnp.asarray(r < TILE_ROWS) | (row < rows - 1))
        & (jnp.asarray(c >= 0) | (col > 0))
        & (jnp.asarray(c < 2 * TILE_COLS) | (col < cols - 1))
    )
    lines = [jnp.asarray(tiles[0], F32), jnp.asarray(tiles[1], F32), image.astype(F32)]
    lines += [jnp.asarray(source, F32) for source in sources]
    return jnp.stack(lines + [jnp.zeros((LANES,), F32)] * 2)


def local(image, labels, weights, momentum):
    row, col, dp = lax.axis_index("row"), lax.axis_index("col"), lax.axis_index("dp")
    place = jnp.stack([row, col, dp % 2, dp // 2]).astype(jnp.int32)
    blocks_list, head = unpack(weights)
    masks = make_masks(row, col)
    padded_momentum = jnp.pad(momentum, (0, PAD - SHARE)).reshape(1, PAD)

    own, edge = split(image[0])
    even = lax.ppermute(edge, "col", neighbours(4, False))
    odd = lax.ppermute(edge, "col", neighbours(4, True, True))
    beyond, up, down = rim(place, own, even, odd)
    even = lax.ppermute(up, "row", neighbours(16, False))
    odd = lax.ppermute(down, "row", neighbours(16, True))
    keep, send = compute(
        labels.reshape(2), place, (own, beyond, even, odd), masks, padded_momentum, blocks_list, head
    )

    parts = keep + received([send], CORE)[0]
    parts = paired_sum(parts[0], received([parts[1], parts[3], parts[2]], X_RING))
    for stage in (Y_RING, Z_PAIR):
        parts = stage_sum(parts, stage)
    got = received([parts] * 3, Z_RING)
    share, magnitude = pl.pallas_call(
        total_kernel,
        out_shape=(shape((1, PAD), F32), shape((1, PAD), F32)),
        in_specs=[SMEM] + [VMEM] * 4,
        out_specs=(VMEM, VMEM),
        compiler_params=PARAMS,
    )(place, parts, *got)
    for stage in (CORE, X_RING):
        magnitude = stage_sum(magnitude, stage)
    scale_tau = 0.1 * magnitude[0, :SHARE] / PARAM + 1e-06
    loss = share[0, SHARE] / NTILES
    share = share[0, :SHARE]
    mixed = 0.1 * share
    update = mixed / (jnp.abs(mixed) + scale_tau)
    start = (row * 16 + col * 4 + dp) * SHARE
    weight_share = lax.dynamic_slice_in_dim(weights, start, SHARE, 0)
    new_weights = weight_share - 0.0001 * (update + 0.1 * weight_share)
    new_momentum = 0.9 * momentum + 0.01 * share
    return (new_weights, new_momentum, update, loss)


def solution(mesh):
    in_specs = (P("dp", None, "row", "col"), P("dp", "row", "col"), P(), P(("row", "col", "dp")))
    out_specs = (P(("row", "col", "dp")), P(("row", "col", "dp")), P(("row", "col", "dp")), P())
    return jax.shard_map(local, mesh=mesh, in_specs=in_specs, out_specs=out_specs, check_vma=False)
```

```python
import numpy as np
import jax
import jax.numpy as jnp
from jax import lax
from jax.experimental import pallas as pl
from jax.experimental.pallas import tpu as pltpu
from jax.sharding import PartitionSpec as P

C = 256
MID = 64
CLASSES = 8
TILE_ROWS = 24
TILE_COLS = 64
NTILES = 512
PARAM = 141312
SHARE = 552

HALO = 2
ROWS = TILE_ROWS + 2 * HALO
COLS = 2 * TILE_COLS + 2 * HALO
PIX = ROWS * COLS
LANES = 3840
GUARD = 256
WIDE = LANES + 2 * GUARD
CHUNK = 768
INNER, OUTER = CHUNK, LANES - CHUNK

BF = jnp.bfloat16
F32 = jnp.float32
ZERO = np.zeros((), BF)

SHARES = 32
PAD = 640


def exchange(size, partner):
    return [(source, partner(source)) for source in range(size)]


def neighbours(size, odd, wrap=False):
    pairs = []
    for low in range(1 if odd else 0, size - 1, 2):
        pairs += [(low, low + 1), (low + 1, low)]
    if odd and wrap:
        pairs += [(0, size - 1), (size - 1, 0)]
    return pairs


def along_z(partner):
    pairs = []
    for row in range(16):
        for dp in range(4):
            z = partner(dp // 2 * 4 + row // 4)
            pairs.append((row * 4 + dp, (z % 4 * 4 + row % 4) * 4 + z // 4 * 2 + dp % 2))
    return pairs


def z_near(z):
    return (3, 2, 1, 0, 7, 6, 5, 4)[z]


CORE = ("dp", [exchange(4, lambda i: i ^ 1)])
X_RING = ("col", [exchange(4, lambda i, k=k: i ^ k) for k in (1, 3, 2)])
Y_RING = ("row", [exchange(16, lambda i, k=k: i ^ k) for k in (1, 3, 2)])
Z_PAIR = (("row", "dp"), [along_z(lambda z: z ^ 1)])
Z_RING = (
    ("row", "dp"),
    [along_z(z_near), along_z(lambda z: 7 - z), along_z(lambda z: z_near(7 - z))],
)


def received(values, stage):
    axis, exchanges = stage
    return [lax.ppermute(value, axis, pairs) for value, pairs in zip(values, exchanges)]


def paired_sum(own, got):
    if len(got) == 1:
        return own + got[0]
    return (own + got[0]) + (got[1] + got[2])


def stage_sum(value, stage):
    return paired_sum(value, received([value] * len(stage[1]), stage))


def nn(left, right):
    return lax.dot_general(left, right, (((1,), (0,)), ((), ())), preferred_element_type=F32)


def nt(left, right):
    return lax.dot_general(left, right, (((1,), (1,)), ((), ())), preferred_element_type=F32)


ALL_ROWS = slice(None)


def cut(start, stop, most=CHUNK):
    tiles = (stop - start) // 128
    count = -(-tiles // (most // 128))
    edges = [start + tiles * k // count * 128 for k in range(count + 1)]
    return list(zip(edges[:-1], edges[1:]))


class Lanes:
    def __init__(self, *segments):
        self.segments = segments

    def get(self, start, stop, rows=ALL_ROWS):
        found = []
        for low, high, ref, base in self.segments:
            a, b = max(start, low), min(stop, high)
            if a < b:
                found.append(ref[rows, a - base : b - base])
        return found[0] if len(found) == 1 else jnp.concatenate(found, axis=1)

    def shifted(self, start, stop, shift, rows=ALL_ROWS):
        low = (start + shift) // 128 * 128
        high = -(-(stop + shift) // 128) * 128
        return self.get(low, high, rows)[:, start + shift - low : stop + shift - low]

    def put(self, start, stop, value, rows=ALL_ROWS):
        for low, high, ref, base in self.segments:
            if low <= start and stop <= high:
                ref[rows, start - base : stop - base] = value
                return
        raise ValueError("no segment")


def whole(ref, base=0):
    return Lanes((base, base + ref.shape[1], ref, base))


def split_kernel(image_ref, own_ref, edge_ref, landed, tall, select, arrived):
    count = landed.shape[0]
    part = C // count
    copies = [
        pltpu.make_async_copy(
            image_ref.at[0, pl.ds(k * part, part)], landed.at[k], arrived.at[k]
        )
        for k in range(count)
    ]
    for copy in copies:
        copy.start()
    lane = lax.broadcasted_iota(jnp.int32, (128, 128), 1)
    col = lax.broadcasted_iota(jnp.int32, (128, 128), 0)
    wanted = jnp.where(col < HALO, col + 64, jnp.where(col >= 126, col - 126, -1000))
    for r in range(TILE_ROWS):
        select[r * 128 : (r + 1) * 128, :] = (lane - 2 * r == wanted).astype(F32).astype(BF)
    for k, copy in enumerate(copies):
        copy.wait()
        rows = slice(k * part, (k + 1) * part)
        tall[k] = landed[k].astype(F32).reshape(part * TILE_ROWS, 128)
        for r in range(TILE_ROWS):
            own_ref[rows, r * 128 : (r + 1) * 128] = tall[
                k, pl.ds(r, part, stride=TILE_ROWS), :
            ].astype(BF)
        edge_ref[rows, :] = nn(own_ref[rows, :], select[...]).astype(BF)


def prepare_kernel(
    own_ref,
    weights_ref,
    flat_ref,
    win_t1,
    wf1,
    wb1,
    wout_t1,
    wout1,
    win_t2,
    wf2,
    wb2,
    wout_t2,
    wout2,
    win2,
    head_ref,
    tall,
):
    for r in range(TILE_ROWS):
        lane = (r + HALO) * COLS + HALO
        flat_ref[:, lane : lane + 128] = own_ref[:, r * 128 : (r + 1) * 128]
        flat_ref[:, lane - 2 * HALO : lane] = jnp.zeros((C, 2 * HALO), BF)
    first = HALO * COLS - HALO
    flat_ref[:, 0:first] = jnp.zeros((C, first), BF)
    last = (ROWS - HALO) * COLS - HALO
    flat_ref[:, last:] = jnp.zeros((C, LANES - last), BF)

    def unpacked(row, count):
        half = count // 2
        lines = weights_ref[row : row + half, :]
        tall[pl.ds(0, half, stride=2), :] = lines[:, :MID]
        tall[pl.ds(1, half, stride=2), :] = lines[:, MID:]
        return tall[0:count, :]

    for row, win_t, wf, wb, wout_t, wout, win in (
        (0, win_t1, wf1, wb1, wout_t1, wout1, None),
        (544, win_t2, wf2, wb2, wout_t2, wout2, win2),
    ):
        value = unpacked(row, C)
        win_t[...] = value.T.astype(BF)
        if win is not None:
            win[...] = value.astype(BF)
        value = jnp.concatenate([unpacked(row + 128 + r * 96, 3 * MID) for r in range(3)], axis=1)
        wb[...] = value.astype(BF)
        wf[...] = value.T.astype(BF)
        value = jnp.concatenate(
            [weights_ref[pl.ds(row + 416 + k, MID, stride=2), :] for k in range(2)], axis=1
        )
        wout[...] = value.astype(BF)
        wout_t[...] = value.T.astype(BF)
    for j in range(16):
        tall[pl.ds(j, 16, stride=16), 0:CLASSES] = weights_ref[
            1088:1104, j * CLASSES : (j + 1) * CLASSES
        ]
    head_ref[...] = tall[:, 0:CLASSES]


def rim_kernel(place, own_ref, even_ref, odd_ref, _, rim_ref, up_ref, down_ref):
    row, col = place[0], place[1]
    lane = lax.broadcasted_iota(jnp.int32, (C, 128), 1)
    odd_col = lax.rem(col, 2)
    from_even = even_ref[...].astype(F32)
    from_odd = odd_ref[...].astype(F32)
    by_even = (lane < 64).astype(jnp.int32) == odd_col
    outside = ((lane < 64) & (col == 0)) | ((lane >= 64) & (col == 3))
    rim = jnp.where(outside, 0.0, jnp.where(by_even, from_even, from_odd)).astype(BF)
    rim_ref[...] = rim
    odd_row = lax.rem(row, 2)
    high = (TILE_ROWS - HALO) * 128
    first = pl.multiple_of((1 - odd_row) * high, 128)
    second = pl.multiple_of(odd_row * high, 128)
    up_ref[:, 0:256] = own_ref[:, pl.ds(first, 256)]
    up_ref[:, 256:384] = rim
    down_ref[:, 0:256] = own_ref[:, pl.ds(second, 256)]
    down_ref[:, 256:384] = rim


def placed(rim, table, k, start, stop):
    source = lax.broadcasted_iota(jnp.int32, (128, stop - start), 0).astype(F32)
    return nn(rim, (source == table[k : k + 1, start:stop]).astype(F32).astype(BF))


def in_image(place, table, start, stop):
    row, col = place[0], place[1]
    r, c = table[6:7, start:stop], table[7:8, start:stop]
    r_low = jnp.where(row > 0, -HALO, 0).astype(F32)
    r_high = jnp.where(row < 15, TILE_ROWS + HALO, TILE_ROWS).astype(F32)
    c_low = jnp.where(col > 0, -HALO, 0).astype(F32)
    c_high = jnp.where(col < 3, 2 * TILE_COLS + HALO, 2 * TILE_COLS).astype(F32)
    inside = (r >= r_low) & (r < r_high) & (c >= c_low) & (c < c_high)
    return jnp.where(inside, table[2:3, start:stop], 0.0)


def enter(inputs, win_t, h1, ranges, mask):
    for start, stop in ranges:
        value = jnp.maximum(nn(win_t[...], inputs.get(start, stop)).astype(BF), ZERO)
        if mask is not None:
            value = value * mask(start, stop).astype(BF)
        h1.put(start, stop, value)


def spread(h1, hs, ranges):
    for start, stop in ranges:
        for s in range(3):
            hs.put(start, stop, h1.shifted(start, stop, s - 1), slice(s * MID, (s + 1) * MID))


def widen(wf, hs, wide, ranges):
    for start, stop in ranges:
        wide.put(start, stop, nn(wf[...], hs.get(start, stop)))


def leave(inputs, wide, wout_t, h2, output, ranges):
    for start, stop in ranges:
        total = sum(
            wide.shifted(start, stop, (r - 1) * COLS, slice(r * MID, (r + 1) * MID))
            for r in range(3)
        )
        value = jnp.maximum(total.astype(BF), ZERO)
        h2.put(start, stop, value)
        total = nn(wout_t[...], value) + inputs.get(start, stop).astype(F32)
        output.put(start, stop, jnp.maximum(total.astype(BF), ZERO))


X_SPAN = (INNER - 512, OUTER + 512)
HS1_SPAN = (INNER - 384, OUTER + 384)
Y1_SPAN = (INNER - 256, OUTER + 256)
Y2_SPAN = (INNER, OUTER)


def inner_kernel(
    place,
    flat_ref,
    rim_ref,
    table,
    win_t1,
    wf1,
    wout_t1,
    win_t2,
    wf2,
    wout_t2,
    x_ref,
    h1a_ref,
    hs1_ref,
    h2a_ref,
    y1_ref,
    h1b_ref,
    hs2_ref,
    h2b_ref,
    y2_ref,
    wide_ref,
):
    x, h1a = whole(x_ref, X_SPAN[0]), whole(h1a_ref, X_SPAN[0])
    hs1 = whole(hs1_ref, HS1_SPAN[0])
    h2a, y1 = whole(h2a_ref, Y1_SPAN[0]), whole(y1_ref, Y1_SPAN[0])
    h1b, hs2 = whole(h1b_ref, Y1_SPAN[0] - 128), whole(hs2_ref, Y1_SPAN[0])
    h2b, y2 = whole(h2b_ref, Y2_SPAN[0]), whole(y2_ref, Y2_SPAN[0])
    wide = whole(wide_ref, X_SPAN[0])
    wide_ref[:, 0:128] = jnp.zeros((3 * MID, 128), F32)
    wide_ref[:, wide_ref.shape[1] - 128 :] = jnp.zeros((3 * MID, 128), F32)
    h1b_ref[:, 0:128] = jnp.zeros((MID, 128), BF)
    h1b_ref[:, h1b_ref.shape[1] - 128 :] = jnp.zeros((MID, 128), BF)
    for start, stop in cut(*X_SPAN):
        value = placed(rim_ref[...], table, 3, start, stop) + flat_ref[:, start:stop].astype(F32)
        x.put(start, stop, value.astype(BF))
    enter(x, win_t1, h1a, cut(*X_SPAN), None)
    spread(h1a, hs1, cut(*HS1_SPAN))
    widen(wf1, hs1, wide, cut(*HS1_SPAN))
    leave(x, wide, wout_t1, h2a, y1, cut(*Y1_SPAN))
    mask = lambda start, stop: in_image(place, table, start, stop)
    enter(y1, win_t2, h1b, cut(*Y1_SPAN), mask)
    spread(h1b, hs2, cut(*Y1_SPAN))
    widen(wf2, hs2, wide, cut(*Y1_SPAN))
    leave(y1, wide, wout_t2, h2b, y2, cut(*Y2_SPAN))


def kernel(
    labels,
    place,
    flat_ref,
    rim_ref,
    even_ref,
    odd_ref,
    table,
    momentum_ref,
    win_t1,
    wf1,
    wb1,
    wout_t1,
    wout1,
    win_t2,
    wf2,
    wb2,
    wout_t2,
    wout2,
    win2,
    head_ref,
    x_mid,
    h1a_mid,
    hs1_mid,
    h2a_mid,
    y1_mid,
    h1b_mid,
    hs2_mid,
    h2b_mid,
    y2_mid,
    keep_ref,
    send_ref,
    packed,
    parts,
    x_ends,
    h1a_ends,
    hs1_ends,
    h2a_ends,
    y1_ends,
    h1b_ends,
    hs2_ends,
    h2b_ends,
    y2_ends,
    wide_ref,
    dg2_ref,
    ds,
    dz,
    tall,
):
    def joined(ends, mid, base):
        pad = (ends.shape[2] - CHUNK) // 2
        return Lanes(
            (-pad, INNER, ends.at[0], -pad),
            (INNER, OUTER, mid, base),
            (OUTER, LANES + pad, ends.at[1], OUTER - pad),
        )

    x = joined(x_ends, x_mid, X_SPAN[0])
    h1a = joined(h1a_ends, h1a_mid, X_SPAN[0])
    hs1 = joined(hs1_ends, hs1_mid, HS1_SPAN[0])
    h2a = joined(h2a_ends, h2a_mid, Y1_SPAN[0])
    y1 = joined(y1_ends, y1_mid, Y1_SPAN[0])
    h1b = joined(h1b_ends, h1b_mid, Y1_SPAN[0] - 128)
    hs2 = joined(hs2_ends, hs2_mid, Y1_SPAN[0])
    h2b = joined(h2b_ends, h2b_mid, Y2_SPAN[0])
    y2 = joined(y2_ends, y2_mid, Y2_SPAN[0])
    wide, dg2 = whole(wide_ref, -GUARD), whole(dg2_ref, -GUARD)
    for ref in (wide_ref, dg2_ref):
        ref[:, :GUARD] = jnp.zeros((ref.shape[0], GUARD), ref.dtype)
        ref[:, GUARD + LANES :] = jnp.zeros((ref.shape[0], GUARD), ref.dtype)
    for ref in (h1a_ends, h1b_ends):
        ref[0, :, 0:128] = jnp.zeros((MID, 128), BF)
        ref[1, :, CHUNK + 128 :] = jnp.zeros((MID, 128), BF)

    odd_row = lax.rem(place[0], 2) == 1
    above = jnp.where(odd_row, even_ref[...].astype(F32), odd_ref[...].astype(F32)).astype(BF)
    below = jnp.where(odd_row, odd_ref[...].astype(F32), even_ref[...].astype(F32)).astype(BF)
    for end, start, stop, k, rows in ((0, 0, INNER, 4, above), (1, OUTER, LANES, 5, below)):
        value = placed(rim_ref[...], table, 3, start, stop) + flat_ref[:, start:stop].astype(F32)
        value = value + placed(rows[:, 256:], table, k, start, stop)
        x_ends[end] = value.astype(BF)
        for r in range(HALO):
            lane = (r if end == 0 else ROWS - HALO + r) * COLS + HALO - start
            x_ends[end, :, lane : lane + 128] = rows[:, r * 128 : (r + 1) * 128]
    ends = [(0, INNER), (OUTER, LANES)]
    wider = [(0, INNER + 256), (OUTER - 256, LANES)]
    mask = lambda start, stop: in_image(place, table, start, stop)
    enter(x, win_t1, h1a, ends, None)
    spread(h1a, hs1, ends)
    widen(wf1, hs1, wide, wider)
    leave(x, wide, wout_t1, h2a, y1, ends)
    enter(y1, win_t2, h1b, ends, mask)
    spread(h1b, hs2, ends)
    widen(wf2, hs2, wide, wider)
    leave(y1, wide, wout_t2, h2b, y2, ends)

    everything = cut(0, LANES)
    assert (0, INNER) in everything and (OUTER, LANES) in everything
    pooled = sum(
        nt(y2.get(start, stop), table[:, start:stop].astype(BF)) for start, stop in everything
    ) * (1.0 / (TILE_ROWS * TILE_COLS))
    head = head_ref[...]
    classes = lax.broadcasted_iota(jnp.int32, (1, CLASSES), 1)
    loss = jnp.zeros((1, 1), F32)
    grad_head = jnp.zeros((C, CLASSES), F32)
    upstream = []
    for tile in range(2):
        column = pooled[:, tile : tile + 1]
        logits = jnp.sum(column * head, axis=0, keepdims=True)
        highest = jnp.max(logits, axis=1, keepdims=True)
        logsum = jnp.log(jnp.sum(jnp.exp(logits - highest), axis=1, keepdims=True)) + highest
        onehot = (classes == labels[tile]).astype(F32)
        loss = loss + logsum - jnp.sum(onehot * logits, axis=1, keepdims=True)
        dlogits = (jnp.exp(logits - logsum) - onehot) * (1.0 / NTILES)
        grad_head = grad_head + column * dlogits
        dpooled = jnp.sum(head * dlogits, axis=1, keepdims=True) / (TILE_ROWS * TILE_COLS)
        upstream.append(dpooled.astype(BF))

    for start, stop in everything:
        first, second = (table[t : t + 1, start:stop].astype(BF) for t in range(2))
        value = upstream[0] * first + upstream[1] * second
        dz[:, start:stop] = jnp.where(y2.get(start, stop) > ZERO, value, ZERO)

    def pack_tall(value, row):
        count = value.shape[0]
        tall[0:count, :] = value
        half = count // 2
        packed[row : row + half, 0:MID] = tall[pl.ds(0, half, stride=2), :]
        packed[row : row + half, MID:] = tall[pl.ds(1, half, stride=2), :]

    def backward(inputs, wb, wout, h1, hs, h2, row, then):
        grad_out = jnp.zeros((C, MID), F32)
        for start, stop in everything:
            value = dz[:, start:stop]
            grad_out = grad_out + nt(value, h2.get(start, stop))
            value = nn(wout[...], value).astype(BF)
            dg2.put(start, stop, jnp.where(h2.get(start, stop) > ZERO, value, ZERO))
        grad_out = grad_out.T
        packed[pl.ds(row + 416, MID, stride=2), :] = grad_out[:, :128]
        packed[pl.ds(row + 417, MID, stride=2), :] = grad_out[:, 128:]
        grad_mid = jnp.zeros((3 * MID, 3 * MID), F32)
        for start, stop in everything:
            for r in range(3):
                ds[r * MID : (r + 1) * MID, start:stop] = dg2.shifted(start, stop, (1 - r) * COLS)
            value = ds[:, start:stop]
            wide.put(start, stop, nn(wb[...], value))
            grad_mid = grad_mid + nt(hs.get(start, stop), value)
        for r in range(3):
            pack_tall(grad_mid[:, r * MID : (r + 1) * MID], row + 128 + r * 96)
        grad_in = jnp.zeros((C, MID), F32)
        for start, stop in everything:
            total = sum(
                wide.shifted(start, stop, 1 - s, slice(s * MID, (s + 1) * MID)) for s in range(3)
            )
            value = jnp.where(h1.get(start, stop) > ZERO, total.astype(BF), ZERO)
            grad_in = grad_in + nt(inputs.get(start, stop), value)
            if then is not None:
                then(start, stop, value)
        pack_tall(grad_in, row)

    def to_first(start, stop, value):
        total = nn(win2[...], value) + dz[:, start:stop].astype(F32)
        dz[:, start:stop] = jnp.where(y1.get(start, stop) > ZERO, total.astype(BF), ZERO)

    backward(y1, wb2, wout2, h1b, hs2, h2b, 544, to_first)
    backward(x, wb1, wout1, h1a, hs1, h2a, 0, None)
    tall[:, 0:CLASSES] = grad_head
    for j in range(16):
        packed[1088:1104, j * CLASSES : (j + 1) * CLASSES] = tall[
            pl.ds(j, 16, stride=16), 0:CLASSES
        ]

    row, col, core, far = place[0], place[1], place[2], place[3]
    lane = lax.broadcasted_iota(jnp.int32, (16, 128), 1)
    for m in range(16):
        m_col, m_far, m_core = m // 4, m // 2 % 2, m % 2
        first, offset = SHARE * m // 128, SHARE * m % 128
        lines = [
            pltpu.roll(packed[pl.ds(first + j, 16, stride=69), :], (128 - offset) % 128, 1)
            for j in range(6)
        ]
        block = parts.at[m_core ^ core, m_col ^ col]
        for j in range(5):
            value = jnp.where(lane < 128 - offset, lines[j], lines[j + 1])
            if j == 4:
                value = jnp.where(lane < 40, value, jnp.where(lane == 40, loss, 0.0))
            block[m_far * 16 : m_far * 16 + 16, j * 128 : (j + 1) * 128] = value
    mine = far * 16 + row
    parts[0, 0, pl.ds(mine, 1), :] = parts[0, 0, pl.ds(mine, 1), :] + 9.0 * momentum_ref[...]
    keep_ref[...] = parts[0]
    send_ref[...] = parts[1]


def total_kernel(place, own, got_a, got_b, got_c, row_ref, size_ref):
    total = (own[...] + got_a[...]) + (got_b[...] + got_c[...])
    lane = lax.broadcasted_iota(jnp.int32, (SHARES, PAD), 1)
    kept = jnp.where(lane < SHARE, jnp.abs(total), 0.0)
    size = jnp.sum(jnp.sum(kept, axis=0, keepdims=True), axis=1, keepdims=True)
    size_ref[...] = jnp.broadcast_to(size, (1, PAD))
    mine = place[3] * 16 + place[0]
    line = lax.broadcasted_iota(jnp.int32, (SHARES, PAD), 0)
    row_ref[...] = jnp.sum(jnp.where(line == mine, total, 0.0), axis=0, keepdims=True)


VMEM = pl.BlockSpec(memory_space=pltpu.VMEM)
SMEM = pl.BlockSpec(memory_space=pltpu.SMEM)
PARAMS = pltpu.CompilerParams(vmem_limit_bytes=36 * 1024 * 1024)


def shape(dims, kind):
    return jax.ShapeDtypeStruct(dims, kind)


def split(image):
    parts = 4
    return pl.pallas_call(
        split_kernel,
        out_shape=(shape((C, TILE_ROWS * 128), BF), shape((C, 128), BF)),
        in_specs=[pl.BlockSpec(memory_space=pltpu.HBM)],
        out_specs=(VMEM, VMEM),
        scratch_shapes=[
            pltpu.VMEM((parts, C // parts, TILE_ROWS, 128), BF),
            pltpu.VMEM((parts, C // parts * TILE_ROWS, 128), F32),
            pltpu.VMEM((TILE_ROWS * 128, 128), BF),
            pltpu.SemaphoreType.DMA((parts,)),
        ],
        compiler_params=PARAMS,
    )(image)


def prepare(own, weights):
    square = shape((3 * MID, 3 * MID), BF)
    down, up = shape((MID, C), BF), shape((C, MID), BF)
    block = [down, square, square, up, down]
    return pl.pallas_call(
        prepare_kernel,
        out_shape=[shape((C, LANES), BF)] + block + block + [up, shape((C, CLASSES), F32)],
        in_specs=[VMEM] * 2,
        out_specs=[VMEM] * 13,
        scratch_shapes=[pltpu.VMEM((C, MID), F32)],
        compiler_params=PARAMS,
        cost_estimate=pl.CostEstimate(flops=0, bytes_accessed=6_000_000, transcendentals=0),
    )(own, weights.reshape(PARAM // 128, 128))


def rim(place, own, even, odd, after):
    return pl.pallas_call(
        rim_kernel,
        out_shape=(shape((C, 128), BF), shape((C, 384), BF), shape((C, 384), BF)),
        in_specs=[SMEM] + [VMEM] * 4,
        out_specs=(VMEM,) * 3,
        compiler_params=PARAMS,
    )(place, own, even, odd, after)


def inner(place, flat, beyond, table, mats):
    win_t1, wf1, _, wout_t1, _, win_t2, wf2, _, wout_t2 = mats[:9]
    spans = [
        (C, X_SPAN),
        (MID, X_SPAN),
        (3 * MID, HS1_SPAN),
        (MID, Y1_SPAN),
        (C, Y1_SPAN),
        (MID, (Y1_SPAN[0] - 128, Y1_SPAN[1] + 128)),
        (3 * MID, Y1_SPAN),
        (MID, Y2_SPAN),
        (C, Y2_SPAN),
    ]
    return pl.pallas_call(
        inner_kernel,
        out_shape=[shape((rows, stop - start), BF) for rows, (start, stop) in spans],
        in_specs=[SMEM] + [VMEM] * 9,
        out_specs=[VMEM] * 9,
        scratch_shapes=[pltpu.VMEM((3 * MID, X_SPAN[1] - X_SPAN[0]), F32)],
        compiler_params=PARAMS,
        cost_estimate=pl.CostEstimate(
            flops=1_000_000_000, bytes_accessed=12_000_000, transcendentals=0
        ),
    )(place, flat, beyond, table, win_t1, wf1, wout_t1, win_t2, wf2, wout_t2)


def compute(labels, place, flat, beyond, even, odd, table, momentum, mats, mids):
    return pl.pallas_call(
        kernel,
        out_shape=(shape((4, SHARES, PAD), F32), shape((4, SHARES, PAD), F32)),
        in_specs=[SMEM, SMEM] + [VMEM] * 27,
        out_specs=(VMEM, VMEM),
        scratch_shapes=[
            pltpu.VMEM((PARAM // 128 + 8, 128), F32),
            pltpu.VMEM((2, 4, SHARES, PAD), F32),
            pltpu.VMEM((2, C, CHUNK), BF),
            pltpu.VMEM((2, MID, CHUNK + 256), BF),
            pltpu.VMEM((2, 3 * MID, CHUNK), BF),
            pltpu.VMEM((2, MID, CHUNK), BF),
            pltpu.VMEM((2, C, CHUNK), BF),
            pltpu.VMEM((2, MID, CHUNK + 256), BF),
            pltpu.VMEM((2, 3 * MID, CHUNK), BF),
            pltpu.VMEM((2, MID, CHUNK), BF),
            pltpu.VMEM((2, C, CHUNK), BF),
            pltpu.VMEM((3 * MID, WIDE), F32),
            pltpu.VMEM((MID, WIDE), BF),
            pltpu.VMEM((3 * MID, LANES), BF),
            pltpu.VMEM((C, LANES), BF),
            pltpu.VMEM((C, MID), F32),
        ],
        compiler_params=PARAMS,
    )(labels, place, flat, beyond, even, odd, table, momentum, *mats, *mids)


def make_table():
    pixel = np.arange(LANES)
    r, c = pixel // COLS - HALO, pixel % COLS - HALO
    real = pixel < PIX
    inside = real & (r >= 0) & (r < TILE_ROWS)
    tiles = [inside & (c >= t * TILE_COLS) & (c < (t + 1) * TILE_COLS) for t in range(2)]
    near = real & (r >= -1) & (r <= TILE_ROWS) & (c >= -1) & (c <= 2 * TILE_COLS)
    lane = np.where(c < 0, 2 * r + c + HALO, np.where(c >= 128, 64 + 2 * r + c - 128, -1000))
    sources = [
        np.where(inside, lane, -1000),
        np.where(real & (r < 0) & (lane > -500), lane + 2 * TILE_ROWS, -1000),
        np.where(real & (r >= TILE_ROWS) & (lane > -500), lane - 2 * TILE_ROWS, -1000),
    ]
    return jnp.asarray(np.stack([*tiles, near, *sources, r, c]).astype(np.float32))


def local(image, labels, weights, momentum):
    row, col, dp = lax.axis_index("row"), lax.axis_index("col"), lax.axis_index("dp")
    place = jnp.stack([row, col, dp % 2, dp // 2]).astype(jnp.int32)
    table = make_table()
    padded_momentum = jnp.pad(momentum, (0, PAD - SHARE)).reshape(1, PAD)

    own, edge = split(image)
    even = lax.ppermute(edge, "col", neighbours(4, False))
    odd = lax.ppermute(edge, "col", neighbours(4, True, True))
    flat, *mats = prepare(own, weights)
    beyond, up, down = rim(place, own, even, odd, mats[-1])
    even = lax.ppermute(up, "row", neighbours(16, False))
    odd = lax.ppermute(down, "row", neighbours(16, True))
    mids = inner(place, flat, beyond, table, mats)
    keep, send = compute(
        labels.reshape(2), place, flat, beyond, even, odd, table, padded_momentum, mats, mids
    )

    parts = keep + received([send], CORE)[0]
    parts = paired_sum(parts[0], received([parts[1], parts[3], parts[2]], X_RING))
    for stage in (Y_RING, Z_PAIR):
        parts = stage_sum(parts, stage)
    got = received([parts] * 3, Z_RING)
    share, magnitude = pl.pallas_call(
        total_kernel,
        out_shape=(shape((1, PAD), F32), shape((1, PAD), F32)),
        in_specs=[SMEM] + [VMEM] * 4,
        out_specs=(VMEM, VMEM),
        compiler_params=PARAMS,
    )(place, parts, *got)
    for stage in (CORE, X_RING):
        magnitude = stage_sum(magnitude, stage)
    scale_tau = 0.1 * magnitude[0, :SHARE] / PARAM + 1e-06
    loss = share[0, SHARE] / NTILES
    share = share[0, :SHARE]
    mixed = 0.1 * share
    update = mixed / (jnp.abs(mixed) + scale_tau)
    start = (row * 16 + col * 4 + dp) * SHARE
    weight_share = lax.dynamic_slice_in_dim(weights, start, SHARE, 0)
    new_weights = weight_share - 0.0001 * (update + 0.1 * weight_share)
    new_momentum = 0.9 * momentum + 0.01 * share
    return (new_weights, new_momentum, update, loss)


def solution(mesh):
    in_specs = (P("dp", None, "row", "col"), P("dp", "row", "col"), P(), P(("row", "col", "dp")))
    out_specs = (P(("row", "col", "dp")), P(("row", "col", "dp")), P(("row", "col", "dp")), P())
    return jax.shard_map(local, mesh=mesh, in_specs=in_specs, out_specs=out_specs, check_vma=False)
```

```python
import numpy as np
import jax
import jax.numpy as jnp
from jax import lax
from jax.experimental import pallas as pl
from jax.experimental.pallas import tpu as pltpu
from jax.sharding import PartitionSpec as P

C = 256
MID = 64
CLASSES = 8
TILE_ROWS = 24
TILE_COLS = 64
NTILES = 512
PARAM = 141312
SHARE = 552

HALO = 2
ROWS = TILE_ROWS + 2 * HALO
COLS = 2 * TILE_COLS + 2 * HALO
PIX = ROWS * COLS
LANES = 3840
GUARD = 256
WIDE = LANES + 2 * GUARD
CHUNK = 768
INNER, OUTER = CHUNK, LANES - CHUNK

BF = jnp.bfloat16
F32 = jnp.float32
ZERO = np.zeros((), BF)

SHARES = 32
CORNERS = 16
MSG = (C + CORNERS, HALO * 128)
PAD = 640


def exchange(size, partner):
    return [(source, partner(source)) for source in range(size)]


def neighbours(size, odd, wrap=False):
    pairs = []
    for low in range(1 if odd else 0, size - 1, 2):
        pairs += [(low, low + 1), (low + 1, low)]
    if odd and wrap:
        pairs += [(0, size - 1), (size - 1, 0)]
    return pairs


def along_z(partner):
    pairs = []
    for row in range(16):
        for dp in range(4):
            z = partner(dp // 2 * 4 + row // 4)
            pairs.append((row * 4 + dp, (z % 4 * 4 + row % 4) * 4 + z // 4 * 2 + dp % 2))
    return pairs


def z_near(z):
    return (3, 2, 1, 0, 7, 6, 5, 4)[z]


CORE = ("dp", [exchange(4, lambda i: i ^ 1)])
X_RING = ("col", [exchange(4, lambda i, k=k: i ^ k) for k in (1, 3, 2)])
Y_RING = ("row", [exchange(16, lambda i, k=k: i ^ k) for k in (1, 3, 2)])
Z_PAIR = (("row", "dp"), [along_z(lambda z: z ^ 1)])
Z_RING = (
    ("row", "dp"),
    [along_z(z_near), along_z(lambda z: 7 - z), along_z(lambda z: z_near(7 - z))],
)


def received(values, stage):
    axis, exchanges = stage
    return [lax.ppermute(value, axis, pairs) for value, pairs in zip(values, exchanges)]


def paired_sum(own, got):
    if len(got) == 1:
        return own + got[0]
    return (own + got[0]) + (got[1] + got[2])


def stage_sum(value, stage):
    return paired_sum(value, received([value] * len(stage[1]), stage))


def nn(left, right):
    return lax.dot_general(left, right, (((1,), (0,)), ((), ())), preferred_element_type=F32)


def nt(left, right):
    return lax.dot_general(left, right, (((1,), (1,)), ((), ())), preferred_element_type=F32)


ALL_ROWS = slice(None)


def cut(start, stop, most=CHUNK):
    tiles = (stop - start) // 128
    count = -(-tiles // (most // 128))
    edges = [start + tiles * k // count * 128 for k in range(count + 1)]
    return list(zip(edges[:-1], edges[1:]))


class Lanes:
    def __init__(self, *segments):
        self.segments = segments

    def get(self, start, stop, rows=ALL_ROWS):
        found = []
        for low, high, ref, base in self.segments:
            a, b = max(start, low), min(stop, high)
            if a < b:
                found.append(ref[rows, a - base : b - base])
        return found[0] if len(found) == 1 else jnp.concatenate(found, axis=1)

    def shifted(self, start, stop, shift, rows=ALL_ROWS):
        low = (start + shift) // 128 * 128
        high = -(-(stop + shift) // 128) * 128
        return self.get(low, high, rows)[:, start + shift - low : stop + shift - low]

    def put(self, start, stop, value, rows=ALL_ROWS):
        for low, high, ref, base in self.segments:
            if low <= start and stop <= high:
                ref[rows, start - base : stop - base] = value
                return
        raise ValueError("no segment")


def whole(ref, base=0):
    return Lanes((base, base + ref.shape[1], ref, base))


def split_kernel(image_ref, own_ref, edge_ref, tall, select):
    tall[...] = image_ref[0].astype(F32).reshape(C * TILE_ROWS, 128)
    lane = lax.broadcasted_iota(jnp.int32, (128, 128), 1)
    col = lax.broadcasted_iota(jnp.int32, (128, 128), 0)
    wanted = jnp.where(col < HALO, col + 64, jnp.where(col >= 126, col - 126, -1000))
    for r in range(TILE_ROWS):
        own_ref[:, r * 128 : (r + 1) * 128] = tall[pl.ds(r, C, stride=TILE_ROWS), :].astype(BF)
        select[r * 128 : (r + 1) * 128, :] = (lane - 2 * r == wanted).astype(F32).astype(BF)
    edge_ref[...] = nn(own_ref[...], select[...]).astype(BF)


def prepare_kernel(
    labels,
    own_ref,
    weights_ref,
    flat_ref,
    win_t1,
    wf1,
    wb1,
    wout_t1,
    wout1,
    win_t2,
    wf2,
    wb2,
    wout_t2,
    wout2,
    win2,
    head_ref,
    target_ref,
    tall,
):
    for r in range(TILE_ROWS):
        lane = (r + HALO) * COLS + HALO
        flat_ref[:, lane : lane + 128] = own_ref[:, r * 128 : (r + 1) * 128]
        flat_ref[:, lane - 2 * HALO : lane] = jnp.zeros((C, 2 * HALO), BF)
    first = HALO * COLS - HALO
    flat_ref[:, 0:first] = jnp.zeros((C, first), BF)
    last = (ROWS - HALO) * COLS - HALO
    flat_ref[:, last:] = jnp.zeros((C, LANES - last), BF)

    def unpacked(row, count):
        half = count // 2
        lines = weights_ref[row : row + half, :]
        tall[pl.ds(0, half, stride=2), :] = lines[:, :MID]
        tall[pl.ds(1, half, stride=2), :] = lines[:, MID:]
        return tall[0:count, :]

    for row, win_t, wf, wb, wout_t, wout, win in (
        (0, win_t1, wf1, wb1, wout_t1, wout1, None),
        (544, win_t2, wf2, wb2, wout_t2, wout2, win2),
    ):
        value = unpacked(row, C)
        win_t[...] = value.T.astype(BF)
        if win is not None:
            win[...] = value.astype(BF)
        value = jnp.concatenate([unpacked(row + 128 + r * 96, 3 * MID) for r in range(3)], axis=1)
        wb[...] = value.astype(BF)
        wf[...] = value.T.astype(BF)
        value = jnp.concatenate(
            [weights_ref[pl.ds(row + 416 + k, MID, stride=2), :] for k in range(2)], axis=1
        )
        wout[...] = value.astype(BF)
        wout_t[...] = value.T.astype(BF)
    for j in range(16):
        tall[pl.ds(j, 16, stride=16), 0:CLASSES] = weights_ref[
            1088:1104, j * CLASSES : (j + 1) * CLASSES
        ]
    head_ref[...] = tall[:, 0:CLASSES]
    line = lax.broadcasted_iota(jnp.int32, (8, CLASSES), 0)
    label = jnp.where(line == 0, labels[0], labels[1])
    target_ref[...] = (lax.broadcasted_iota(jnp.int32, (8, CLASSES), 1) == label).astype(F32)


def rim_kernel(place, own_ref, even_ref, odd_ref, _, rim_ref, up_ref, down_ref):
    row, col = place[0], place[1]
    lane = lax.broadcasted_iota(jnp.int32, (C, 128), 1)
    odd_col = lax.rem(col, 2)
    from_even = even_ref[...].astype(F32)
    from_odd = odd_ref[...].astype(F32)
    by_even = (lane < 64).astype(jnp.int32) == odd_col
    outside = ((lane < 64) & (col == 0)) | ((lane >= 64) & (col == 3))
    rim = jnp.where(outside, 0.0, jnp.where(by_even, from_even, from_odd)).astype(BF)
    rim_ref[...] = rim
    odd_row = lax.rem(row, 2)
    corner = lax.broadcasted_iota(jnp.int32, (CORNERS, 128), 0)
    source = lax.broadcasted_iota(jnp.int32, (CORNERS, 128), 1)
    for ref, low in ((up_ref, odd_row), (down_ref, 1 - odd_row)):
        first = (1 - low) * (TILE_ROWS - HALO)
        ref[0:C, :] = own_ref[:, pl.ds(pl.multiple_of(first * 128, 128), HALO * 128)]
        wanted = 2 * first + jnp.where(corner < 4, corner, 64 + corner - 4)
        pick = ((source == wanted) & (corner < 8)).astype(F32).astype(BF)
        ref[C:, :] = nt(pick, rim).astype(BF)


def placed(rim, table, k, start, stop):
    source = lax.broadcasted_iota(jnp.int32, (rim.shape[1], stop - start), 0).astype(F32)
    return nn(rim, (source == table[k : k + 1, start:stop]).astype(F32).astype(BF))


def in_image(place, table, start, stop):
    row, col = place[0], place[1]
    r, c = table[6:7, start:stop], table[7:8, start:stop]
    r_low = jnp.where(row > 0, -HALO, 0).astype(F32)
    r_high = jnp.where(row < 15, TILE_ROWS + HALO, TILE_ROWS).astype(F32)
    c_low = jnp.where(col > 0, -HALO, 0).astype(F32)
    c_high = jnp.where(col < 3, 2 * TILE_COLS + HALO, 2 * TILE_COLS).astype(F32)
    inside = (r >= r_low) & (r < r_high) & (c >= c_low) & (c < c_high)
    return jnp.where(inside, table[2:3, start:stop], 0.0)


def enter(inputs, win_t, h1, ranges, mask):
    for start, stop in ranges:
        value = jnp.maximum(nn(win_t[...], inputs.get(start, stop)).astype(BF), ZERO)
        if mask is not None:
            value = value * mask(start, stop).astype(BF)
        h1.put(start, stop, value)


def spread(h1, hs, ranges):
    for start, stop in ranges:
        for s in range(3):
            hs.put(start, stop, h1.shifted(start, stop, s - 1), slice(s * MID, (s + 1) * MID))


def widen(wf, hs, wide, ranges):
    for start, stop in ranges:
        wide.put(start, stop, nn(wf[...], hs.get(start, stop)))


def leave(inputs, wide, wout_t, h2, output, ranges):
    for start, stop in ranges:
        total = sum(
            wide.shifted(start, stop, (r - 1) * COLS, slice(r * MID, (r + 1) * MID))
            for r in range(3)
        )
        value = jnp.maximum(total.astype(BF), ZERO)
        h2.put(start, stop, value)
        total = nn(wout_t[...], value) + inputs.get(start, stop).astype(F32)
        output.put(start, stop, jnp.maximum(total.astype(BF), ZERO))


X_SPAN = (INNER - 512, OUTER + 512)
HS1_SPAN = (INNER - 384, OUTER + 384)
Y1_SPAN = (INNER - 256, OUTER + 256)
Y2_SPAN = (INNER, OUTER)


def inner_kernel(
    place,
    flat_ref,
    rim_ref,
    table,
    win_t1,
    wf1,
    wout_t1,
    win_t2,
    wf2,
    wout_t2,
    x_ref,
    h1a_ref,
    hs1_ref,
    h2a_ref,
    y1_ref,
    h1b_ref,
    hs2_ref,
    h2b_ref,
    y2_ref,
    wide_ref,
):
    x, h1a = whole(x_ref, X_SPAN[0]), whole(h1a_ref, X_SPAN[0])
    hs1 = whole(hs1_ref, HS1_SPAN[0])
    h2a, y1 = whole(h2a_ref, Y1_SPAN[0]), whole(y1_ref, Y1_SPAN[0])
    h1b, hs2 = whole(h1b_ref, Y1_SPAN[0] - 128), whole(hs2_ref, Y1_SPAN[0])
    h2b, y2 = whole(h2b_ref, Y2_SPAN[0]), whole(y2_ref, Y2_SPAN[0])
    wide = whole(wide_ref, X_SPAN[0])
    wide_ref[:, 0:128] = jnp.zeros((3 * MID, 128), F32)
    wide_ref[:, wide_ref.shape[1] - 128 :] = jnp.zeros((3 * MID, 128), F32)
    h1b_ref[:, 0:128] = jnp.zeros((MID, 128), BF)
    h1b_ref[:, h1b_ref.shape[1] - 128 :] = jnp.zeros((MID, 128), BF)
    for start, stop in cut(*X_SPAN):
        value = placed(rim_ref[...], table, 3, start, stop) + flat_ref[:, start:stop].astype(F32)
        x.put(start, stop, value.astype(BF))
    enter(x, win_t1, h1a, cut(*X_SPAN), None)
    spread(h1a, hs1, cut(*HS1_SPAN))
    widen(wf1, hs1, wide, cut(*HS1_SPAN))
    leave(x, wide, wout_t1, h2a, y1, cut(*Y1_SPAN))
    mask = lambda start, stop: in_image(place, table, start, stop)
    enter(y1, win_t2, h1b, cut(*Y1_SPAN), mask)
    spread(h1b, hs2, cut(*Y1_SPAN))
    widen(wf2, hs2, wide, cut(*Y1_SPAN))
    leave(y1, wide, wout_t2, h2b, y2, cut(*Y2_SPAN))


def kernel(
    place,
    flat_ref,
    rim_ref,
    odd_ref,
    even_ref,
    table,
    momentum_ref,
    win_t1,
    wf1,
    wb1,
    wout_t1,
    wout1,
    win_t2,
    wf2,
    wb2,
    wout_t2,
    wout2,
    win2,
    head_ref,
    target_ref,
    x_mid,
    h1a_mid,
    hs1_mid,
    h2a_mid,
    y1_mid,
    h1b_mid,
    hs2_mid,
    h2b_mid,
    y2_mid,
    keep_ref,
    send_ref,
    packed,
    parts,
    x_ends,
    h1a_ends,
    hs1_ends,
    h2a_ends,
    y1_ends,
    h1b_ends,
    hs2_ends,
    h2b_ends,
    y2_ends,
    wide_ref,
    dg2_ref,
    ds,
    dz,
    tall,
):
    def joined(ends, mid, base):
        pad = (ends.shape[2] - CHUNK) // 2
        return Lanes(
            (-pad, INNER, ends.at[0], -pad),
            (INNER, OUTER, mid, base),
            (OUTER, LANES + pad, ends.at[1], OUTER - pad),
        )

    x = joined(x_ends, x_mid, X_SPAN[0])
    h1a = joined(h1a_ends, h1a_mid, X_SPAN[0])
    hs1 = joined(hs1_ends, hs1_mid, HS1_SPAN[0])
    h2a = joined(h2a_ends, h2a_mid, Y1_SPAN[0])
    y1 = joined(y1_ends, y1_mid, Y1_SPAN[0])
    h1b = joined(h1b_ends, h1b_mid, Y1_SPAN[0] - 128)
    hs2 = joined(hs2_ends, hs2_mid, Y1_SPAN[0])
    h2b = joined(h2b_ends, h2b_mid, Y2_SPAN[0])
    y2 = joined(y2_ends, y2_mid, Y2_SPAN[0])
    wide, dg2 = whole(wide_ref, -GUARD), whole(dg2_ref, -GUARD)
    for ref in (wide_ref, dg2_ref):
        ref[:, :GUARD] = jnp.zeros((ref.shape[0], GUARD), ref.dtype)
        ref[:, GUARD + LANES :] = jnp.zeros((ref.shape[0], GUARD), ref.dtype)
    for ref in (h1a_ends, h1b_ends):
        ref[0, :, 0:128] = jnp.zeros((MID, 128), BF)
        ref[1, :, CHUNK + 128 :] = jnp.zeros((MID, 128), BF)

    odd_row = lax.rem(place[0], 2) == 1
    above = jnp.where(odd_row, even_ref[...].astype(F32), odd_ref[...].astype(F32)).astype(BF)
    below = jnp.where(odd_row, odd_ref[...].astype(F32), even_ref[...].astype(F32)).astype(BF)
    for end, start, stop, k, rows in ((0, 0, INNER, 4, above), (1, OUTER, LANES, 5, below)):
        value = placed(rim_ref[...], table, 3, start, stop) + flat_ref[:, start:stop].astype(F32)
        corners = rows[C:, :].astype(F32).T.astype(BF)
        value = value + placed(corners, table, k, start, stop)
        x_ends[end] = value.astype(BF)
        for r in range(HALO):
            lane = (r if end == 0 else ROWS - HALO + r) * COLS + HALO - start
            x_ends[end, :, lane : lane + 128] = rows[0:C, r * 128 : (r + 1) * 128]
    ends = [(0, INNER), (OUTER, LANES)]
    wider = [(0, INNER + 256), (OUTER - 256, LANES)]
    mask = lambda start, stop: in_image(place, table, start, stop)
    enter(x, win_t1, h1a, ends, None)
    spread(h1a, hs1, ends)
    widen(wf1, hs1, wide, wider)
    leave(x, wide, wout_t1, h2a, y1, ends)
    enter(y1, win_t2, h1b, ends, mask)
    spread(h1b, hs2, ends)
    widen(wf2, hs2, wide, wider)
    leave(y1, wide, wout_t2, h2b, y2, ends)

    everything = cut(0, LANES)
    assert (0, INNER) in everything and (OUTER, LANES) in everything
    pooled = sum(
        nt(y2.get(start, stop), table[:, start:stop].astype(BF)) for start, stop in everything
    ) * (1.0 / (TILE_ROWS * TILE_COLS))
    head = head_ref[...]
    loss = jnp.zeros((1, 1), F32)
    grad_head = jnp.zeros((C, CLASSES), F32)
    upstream = []
    for tile in range(2):
        column = pooled[:, tile : tile + 1]
        logits = jnp.sum(column * head, axis=0, keepdims=True)
        highest = jnp.max(logits, axis=1, keepdims=True)
        logsum = jnp.log(jnp.sum(jnp.exp(logits - highest), axis=1, keepdims=True)) + highest
        onehot = target_ref[tile : tile + 1, :]
        loss = loss + logsum - jnp.sum(onehot * logits, axis=1, keepdims=True)
        dlogits = (jnp.exp(logits - logsum) - onehot) * (1.0 / NTILES)
        grad_head = grad_head + column * dlogits
        dpooled = jnp.sum(head * dlogits, axis=1, keepdims=True) / (TILE_ROWS * TILE_COLS)
        upstream.append(dpooled.astype(BF))

    own = [(256, 1024), (1024, 1792), (1792, 2560), (2560, 3584)]
    one = [(0, 768), (768, 1536), (1536, 2304), (2304, 3072), (3072, 3584)]
    dz[:, 0:256] = jnp.zeros((C, 256), BF)
    dg2_ref[:, GUARD : GUARD + 256] = jnp.zeros((MID, 256), BF)
    dg2_ref[:, GUARD + 3584 :] = jnp.zeros((MID, LANES - 3584 + GUARD), BF)
    for start, stop in own:
        first, second = (table[t : t + 1, start:stop].astype(BF) for t in range(2))
        value = upstream[0] * first + upstream[1] * second
        dz[:, start:stop] = jnp.where(y2.get(start, stop) > ZERO, value, ZERO)

    def pack_tall(value, row):
        count = value.shape[0]
        tall[0:count, :] = value
        half = count // 2
        packed[row : row + half, 0:MID] = tall[pl.ds(0, half, stride=2), :]
        packed[row : row + half, MID:] = tall[pl.ds(1, half, stride=2), :]

    def backward(inputs, wb, wout, h1, hs, h2, row, then, near, far):
        grad_out = jnp.zeros((C, MID), F32)
        for start, stop in near:
            value = dz[:, start:stop]
            grad_out = grad_out + nt(value, h2.get(start, stop))
            value = nn(wout[...], value).astype(BF)
            dg2.put(start, stop, jnp.where(h2.get(start, stop) > ZERO, value, ZERO))
        grad_out = grad_out.T
        packed[pl.ds(row + 416, MID, stride=2), :] = grad_out[:, :128]
        packed[pl.ds(row + 417, MID, stride=2), :] = grad_out[:, 128:]
        grad_mid = jnp.zeros((3 * MID, 3 * MID), F32)
        for start, stop in far:
            for r in range(3):
                ds[r * MID : (r + 1) * MID, start:stop] = dg2.shifted(start, stop, (1 - r) * COLS)
            value = ds[:, start:stop]
            wide.put(start, stop, nn(wb[...], value))
            grad_mid = grad_mid + nt(hs.get(start, stop), value)
        for r in range(3):
            pack_tall(grad_mid[:, r * MID : (r + 1) * MID], row + 128 + r * 96)
        grad_in = jnp.zeros((C, MID), F32)
        for start, stop in far:
            total = sum(
                wide.shifted(start, stop, 1 - s, slice(s * MID, (s + 1) * MID)) for s in range(3)
            )
            value = jnp.where(h1.get(start, stop) > ZERO, total.astype(BF), ZERO)
            grad_in = grad_in + nt(inputs.get(start, stop), value)
            if then is not None:
                then(start, stop, value)
        pack_tall(grad_in, row)

    def to_first(start, stop, value):
        total = nn(win2[...], value) + dz[:, start:stop].astype(F32)
        dz[:, start:stop] = jnp.where(y1.get(start, stop) > ZERO, total.astype(BF), ZERO)

    backward(y1, wb2, wout2, h1b, hs2, h2b, 544, to_first, own, one)
    tall[:, 0:CLASSES] = grad_head
    for j in range(16):
        packed[1088:1104, j * CLASSES : (j + 1) * CLASSES] = tall[
            pl.ds(j, 16, stride=16), 0:CLASSES
        ]

    row, col, core, far = place[0], place[1], place[2], place[3]
    lane = lax.broadcasted_iota(jnp.int32, (8, 128), 1)

    def pack_shares(low):
        for m in range(16):
            m_col, m_far, m_core = m // 4, m // 2 % 2, m % 2
            first, offset = 69 * low + SHARE * m // 128, SHARE * m % 128
            lines = [
                pltpu.roll(packed[pl.ds(first + j, 8, stride=69), :], (128 - offset) % 128, 1)
                for j in range(6)
            ]
            block = parts.at[m_core ^ core, m_col ^ col]
            for j in range(5):
                value = jnp.where(lane < 128 - offset, lines[j], lines[j + 1])
                if j == 4:
                    value = jnp.where(lane < 40, value, jnp.where(lane == 40, loss, 0.0))
                begin = m_far * 16 + low
                block[begin : begin + 8, j * 128 : (j + 1) * 128] = value

    pack_shares(8)
    backward(x, wb1, wout1, h1a, hs1, h2a, 0, None, one, everything)

    pack_shares(0)
    mine = far * 16 + row
    parts[0, 0, pl.ds(mine, 1), :] = parts[0, 0, pl.ds(mine, 1), :] + 9.0 * momentum_ref[...]
    keep_ref[...] = parts[0]
    send_ref[...] = parts[1]


def total_kernel(place, own, got_a, got_b, got_c, row_ref, size_ref):
    total = (own[...] + got_a[...]) + (got_b[...] + got_c[...])
    lane = lax.broadcasted_iota(jnp.int32, (SHARES, PAD), 1)
    kept = jnp.where(lane < SHARE, jnp.abs(total), 0.0)
    size = jnp.sum(jnp.sum(kept, axis=0, keepdims=True), axis=1, keepdims=True)
    size_ref[...] = jnp.broadcast_to(size, (1, PAD))
    mine = place[3] * 16 + place[0]
    line = lax.broadcasted_iota(jnp.int32, (SHARES, PAD), 0)
    row_ref[...] = jnp.sum(jnp.where(line == mine, total, 0.0), axis=0, keepdims=True)


VMEM = pl.BlockSpec(memory_space=pltpu.VMEM)
SMEM = pl.BlockSpec(memory_space=pltpu.SMEM)
PARAMS = pltpu.CompilerParams(vmem_limit_bytes=36 * 1024 * 1024)


def shape(dims, kind):
    return jax.ShapeDtypeStruct(dims, kind)


def split(image):
    return pl.pallas_call(
        split_kernel,
        out_shape=(shape((C, TILE_ROWS * 128), BF), shape((C, 128), BF)),
        in_specs=[VMEM],
        out_specs=(VMEM, VMEM),
        scratch_shapes=[
            pltpu.VMEM((C * TILE_ROWS, 128), F32),
            pltpu.VMEM((TILE_ROWS * 128, 128), BF),
        ],
        compiler_params=PARAMS,
    )(image)


def prepare(labels, own, weights):
    square = shape((3 * MID, 3 * MID), BF)
    down, up = shape((MID, C), BF), shape((C, MID), BF)
    block = [down, square, square, up, down]
    return pl.pallas_call(
        prepare_kernel,
        out_shape=[shape((C, LANES), BF)] + block + block + [up, shape((C, CLASSES), F32), shape((8, CLASSES), F32)],
        in_specs=[SMEM] + [VMEM] * 2,
        out_specs=[VMEM] * 14,
        scratch_shapes=[pltpu.VMEM((C, MID), F32)],
        compiler_params=PARAMS,
        cost_estimate=pl.CostEstimate(flops=0, bytes_accessed=6_000_000, transcendentals=0),
    )(labels, own, weights.reshape(PARAM // 128, 128))


def rim(place, own, even, odd, after):
    return pl.pallas_call(
        rim_kernel,
        out_shape=(shape((C, 128), BF), shape(MSG, BF), shape(MSG, BF)),
        in_specs=[SMEM] + [VMEM] * 4,
        out_specs=(VMEM,) * 3,
        compiler_params=PARAMS,
    )(place, own, even, odd, after)


def inner(place, flat, beyond, table, mats):
    win_t1, wf1, _, wout_t1, _, win_t2, wf2, _, wout_t2 = mats[:9]
    spans = [
        (C, X_SPAN),
        (MID, X_SPAN),
        (3 * MID, HS1_SPAN),
        (MID, Y1_SPAN),
        (C, Y1_SPAN),
        (MID, (Y1_SPAN[0] - 128, Y1_SPAN[1] + 128)),
        (3 * MID, Y1_SPAN),
        (MID, Y2_SPAN),
        (C, Y2_SPAN),
    ]
    return pl.pallas_call(
        inner_kernel,
        out_shape=[shape((rows, stop - start), BF) for rows, (start, stop) in spans],
        in_specs=[SMEM] + [VMEM] * 9,
        out_specs=[VMEM] * 9,
        scratch_shapes=[pltpu.VMEM((3 * MID, X_SPAN[1] - X_SPAN[0]), F32)],
        compiler_params=PARAMS,
        cost_estimate=pl.CostEstimate(
            flops=1_000_000_000, bytes_accessed=12_000_000, transcendentals=0
        ),
    )(place, flat, beyond, table, win_t1, wf1, wout_t1, win_t2, wf2, wout_t2)


def compute(place, flat, beyond, odd, even, table, momentum, mats, mids):
    return pl.pallas_call(
        kernel,
        out_shape=(shape((4, SHARES, PAD), F32), shape((4, SHARES, PAD), F32)),
        in_specs=[SMEM] + [VMEM] * 28,
        out_specs=(VMEM, VMEM),
        scratch_shapes=[
            pltpu.VMEM((PARAM // 128 + 8, 128), F32),
            pltpu.VMEM((2, 4, SHARES, PAD), F32),
            pltpu.VMEM((2, C, CHUNK), BF),
            pltpu.VMEM((2, MID, CHUNK + 256), BF),
            pltpu.VMEM((2, 3 * MID, CHUNK), BF),
            pltpu.VMEM((2, MID, CHUNK), BF),
            pltpu.VMEM((2, C, CHUNK), BF),
            pltpu.VMEM((2, MID, CHUNK + 256), BF),
            pltpu.VMEM((2, 3 * MID, CHUNK), BF),
            pltpu.VMEM((2, MID, CHUNK), BF),
            pltpu.VMEM((2, C, CHUNK), BF),
            pltpu.VMEM((3 * MID, WIDE), F32),
            pltpu.VMEM((MID, WIDE), BF),
            pltpu.VMEM((3 * MID, LANES), BF),
            pltpu.VMEM((C, LANES), BF),
            pltpu.VMEM((C, MID), F32),
        ],
        compiler_params=PARAMS,
    )(place, flat, beyond, odd, even, table, momentum, *mats, *mids)


def make_table():
    pixel = np.arange(LANES)
    r, c = pixel // COLS - HALO, pixel % COLS - HALO
    real = pixel < PIX
    inside = real & (r >= 0) & (r < TILE_ROWS)
    tiles = [inside & (c >= t * TILE_COLS) & (c < (t + 1) * TILE_COLS) for t in range(2)]
    near = real & (r >= -1) & (r <= TILE_ROWS) & (c >= -1) & (c <= 2 * TILE_COLS)
    lane = np.where(c < 0, 2 * r + c + HALO, np.where(c >= 128, 64 + 2 * r + c - 128, -1000))
    corner = lambda k: np.where(c < 0, 2 * k + c + HALO, np.where(c >= 128, 4 + 2 * k + c - 128, -1000))
    sources = [
        np.where(inside, lane, -1000),
        np.where(real & (r < 0), corner(r + HALO), -1000),
        np.where(real & (r >= TILE_ROWS), corner(r - TILE_ROWS), -1000),
    ]
    return jnp.asarray(np.stack([*tiles, near, *sources, r, c]).astype(np.float32))


def local(image, labels, weights, momentum):
    row, col, dp = lax.axis_index("row"), lax.axis_index("col"), lax.axis_index("dp")
    place = jnp.stack([row, col, dp % 2, dp // 2]).astype(jnp.int32)
    table = make_table()
    padded_momentum = jnp.pad(momentum, (0, PAD - SHARE)).reshape(1, PAD)

    own, edge = split(image)
    even = lax.ppermute(edge, "col", neighbours(4, False))
    odd = lax.ppermute(edge, "col", neighbours(4, True, True))
    flat, *mats = prepare(labels.reshape(2), own, weights)
    beyond, up, down = rim(place, own, even, odd, mats[-1])
    odd = lax.ppermute(down, "row", neighbours(16, True))
    even = lax.ppermute(up, "row", neighbours(16, False))
    mids = inner(place, flat, beyond, table, mats)
    keep, send = compute(
        place, flat, beyond, odd, even, table, padded_momentum, mats, mids
    )

    parts = keep + received([send], CORE)[0]
    parts = paired_sum(parts[0], received([parts[1], parts[3], parts[2]], X_RING))
    for stage in (Y_RING, Z_PAIR):
        parts = stage_sum(parts, stage)
    got = received([parts] * 3, Z_RING)
    share, magnitude = pl.pallas_call(
        total_kernel,
        out_shape=(shape((1, PAD), F32), shape((1, PAD), F32)),
        in_specs=[SMEM] + [VMEM] * 4,
        out_specs=(VMEM, VMEM),
        compiler_params=PARAMS,
    )(place, parts, *got)
    for stage in (CORE, X_RING):
        magnitude = stage_sum(magnitude, stage)
    scale_tau = 0.1 * magnitude[0, :SHARE] / PARAM + 1e-06
    loss = share[0, SHARE] / NTILES
    share = share[0, :SHARE]
    mixed = 0.1 * share
    update = mixed / (jnp.abs(mixed) + scale_tau)
    start = (row * 16 + col * 4 + dp) * SHARE
    weight_share = lax.dynamic_slice_in_dim(weights, start, SHARE, 0)
    new_weights = weight_share - 0.0001 * (update + 0.1 * weight_share)
    new_momentum = 0.9 * momentum + 0.01 * share
    return (new_weights, new_momentum, update, loss)


def solution(mesh):
    in_specs = (P("dp", None, "row", "col"), P("dp", "row", "col"), P(), P(("row", "col", "dp")))
    out_specs = (P(("row", "col", "dp")), P(("row", "col", "dp")), P(("row", "col", "dp")), P())
    return jax.shard_map(local, mesh=mesh, in_specs=in_specs, out_specs=out_specs, check_vma=False)
```

```python
import numpy as np
import jax
import jax.numpy as jnp
from jax import lax
from jax.experimental import pallas as pl
from jax.experimental.pallas import tpu as pltpu
from jax.sharding import PartitionSpec as P

C = 256
MID = 64
CLASSES = 8
TILE_ROWS = 24
TILE_COLS = 64
NTILES = 512
PARAM = 141312
SHARE = 552

HALO = 2
ROWS = TILE_ROWS + 2 * HALO
COLS = 2 * TILE_COLS + 2 * HALO
PIX = ROWS * COLS
LANES = 3840
GUARD = 256
WIDE = LANES + 2 * GUARD
CHUNK = 768
PIECE = 1024
INNER, OUTER = CHUNK, LANES - CHUNK

BF = jnp.bfloat16
F32 = jnp.float32
ZERO = np.zeros((), BF)

SHARES = 32
CORNERS = 16
MSG = (C + CORNERS, HALO * 128)
PAD = 640


def exchange(size, partner):
    return [(source, partner(source)) for source in range(size)]


def neighbours(size, odd, wrap=False):
    pairs = []
    for low in range(1 if odd else 0, size - 1, 2):
        pairs += [(low, low + 1), (low + 1, low)]
    if odd and wrap:
        pairs += [(0, size - 1), (size - 1, 0)]
    return pairs


def along_z(partner):
    pairs = []
    for row in range(16):
        for dp in range(4):
            z = partner(dp // 2 * 4 + row // 4)
            pairs.append((row * 4 + dp, (z % 4 * 4 + row % 4) * 4 + z // 4 * 2 + dp % 2))
    return pairs


def z_near(z):
    return (3, 2, 1, 0, 7, 6, 5, 4)[z]


CORE = ("dp", [exchange(4, lambda i: i ^ 1)])
X_RING = ("col", [exchange(4, lambda i, k=k: i ^ k) for k in (1, 3, 2)])
Y_RING = ("row", [exchange(16, lambda i, k=k: i ^ k) for k in (1, 3, 2)])
Z_PAIR = (("row", "dp"), [along_z(lambda z: z ^ 1)])
Z_RING = (
    ("row", "dp"),
    [along_z(z_near), along_z(lambda z: 7 - z), along_z(lambda z: z ^ 5)],
)


def received(values, stage):
    axis, exchanges = stage
    return [lax.ppermute(value, axis, pairs) for value, pairs in zip(values, exchanges)]


def paired_sum(own, got):
    if len(got) == 1:
        return own + got[0]
    return (own + got[0]) + (got[1] + got[2])


def stage_sum(value, stage):
    return paired_sum(value, received([value] * len(stage[1]), stage))


def nn(left, right):
    return lax.dot_general(left, right, (((1,), (0,)), ((), ())), preferred_element_type=F32)


def nt(left, right):
    return lax.dot_general(left, right, (((1,), (1,)), ((), ())), preferred_element_type=F32)


ALL_ROWS = slice(None)


def cut(start, stop):
    edges = list(range(start, stop, PIECE))
    if len(edges) > 1 and stop - edges[-1] <= 256:
        edges.pop()
    return list(zip(edges, edges[1:] + [stop]))


class Lanes:
    def __init__(self, *segments):
        self.segments = segments

    def get(self, start, stop, rows=ALL_ROWS):
        found = []
        for low, high, ref, base in self.segments:
            a, b = max(start, low), min(stop, high)
            if a < b:
                found.append(ref[rows, a - base : b - base])
        return found[0] if len(found) == 1 else jnp.concatenate(found, axis=1)

    def shifted(self, start, stop, shift, rows=ALL_ROWS):
        low = (start + shift) // 128 * 128
        high = -(-(stop + shift) // 128) * 128
        return self.get(low, high, rows)[:, start + shift - low : stop + shift - low]

    def put(self, start, stop, value, rows=ALL_ROWS):
        for low, high, ref, base in self.segments:
            if low <= start and stop <= high:
                ref[rows, start - base : stop - base] = value
                return
        raise ValueError("no segment")


def whole(ref, base=0):
    return Lanes((base, base + ref.shape[1], ref, base))


def split_kernel(image_ref, own_ref, edge_ref, tall, select):
    tall[...] = image_ref[0].astype(F32).reshape(C * TILE_ROWS, 128)
    lane = lax.broadcasted_iota(jnp.int32, (128, 128), 1)
    col = lax.broadcasted_iota(jnp.int32, (128, 128), 0)
    wanted = jnp.where(col < HALO, col + 64, jnp.where(col >= 126, col - 126, -1000))
    for r in range(TILE_ROWS):
        own_ref[:, r * 128 : (r + 1) * 128] = tall[pl.ds(r, C, stride=TILE_ROWS), :].astype(BF)
        select[r * 128 : (r + 1) * 128, :] = (lane - 2 * r == wanted).astype(F32).astype(BF)
    edge_ref[...] = nn(own_ref[...], select[...]).astype(BF)


def spots(count, table, k, start, stop):
    source = lax.broadcasted_iota(jnp.int32, (count, stop - start), 0).astype(F32)
    return (source == table[k : k + 1, start:stop]).astype(F32).astype(BF)


def prepare_kernel(
    labels,
    own_ref,
    weights_ref,
    table,
    flat_ref,
    spot_ref,
    win_t1,
    wf1,
    wb1,
    wout_t1,
    wout1,
    win_t2,
    wf2,
    wb2,
    wout_t2,
    wout2,
    win2,
    head_ref,
    target_ref,
    tall,
):
    for r in range(TILE_ROWS):
        lane = (r + HALO) * COLS + HALO
        flat_ref[:, lane : lane + 128] = own_ref[:, r * 128 : (r + 1) * 128]
        flat_ref[:, lane - 2 * HALO : lane] = jnp.zeros((C, 2 * HALO), BF)
    first = HALO * COLS - HALO
    flat_ref[:, 0:first] = jnp.zeros((C, first), BF)
    last = (ROWS - HALO) * COLS - HALO
    flat_ref[:, last:] = jnp.zeros((C, LANES - last), BF)

    def unpacked(row, count):
        half = count // 2
        lines = weights_ref[row : row + half, :]
        tall[pl.ds(0, half, stride=2), :] = lines[:, :MID]
        tall[pl.ds(1, half, stride=2), :] = lines[:, MID:]
        return tall[0:count, :]

    for row, win_t, wf, wb, wout_t, wout, win in (
        (0, win_t1, wf1, wb1, wout_t1, wout1, None),
        (544, win_t2, wf2, wb2, wout_t2, wout2, win2),
    ):
        value = unpacked(row, C)
        win_t[...] = value.T.astype(BF)
        if win is not None:
            win[...] = value.astype(BF)
        value = jnp.concatenate([unpacked(row + 128 + r * 96, 3 * MID) for r in range(3)], axis=1)
        wb[...] = value.astype(BF)
        wf[...] = value.T.astype(BF)
        value = jnp.concatenate(
            [weights_ref[pl.ds(row + 416 + k, MID, stride=2), :] for k in range(2)], axis=1
        )
        wout[...] = value.astype(BF)
        wout_t[...] = value.T.astype(BF)
    for j in range(16):
        tall[pl.ds(j, 16, stride=16), 0:CLASSES] = weights_ref[
            1088:1104, j * CLASSES : (j + 1) * CLASSES
        ]
    head_ref[...] = tall[:, 0:CLASSES]
    for start, stop in cut(0, LANES):
        spot_ref[:, start:stop] = spots(128, table, 3, start, stop)
    line = lax.broadcasted_iota(jnp.int32, (8, CLASSES), 0)
    label = jnp.where(line == 0, labels[0], labels[1])
    target_ref[...] = (lax.broadcasted_iota(jnp.int32, (8, CLASSES), 1) == label).astype(F32)


def rim_kernel(place, own_ref, even_ref, odd_ref, _, rim_ref, up_ref, down_ref):
    row, col = place[0], place[1]
    lane = lax.broadcasted_iota(jnp.int32, (C, 128), 1)
    odd_col = lax.rem(col, 2)
    from_even = even_ref[...].astype(F32)
    from_odd = odd_ref[...].astype(F32)
    by_even = (lane < 64).astype(jnp.int32) == odd_col
    outside = ((lane < 64) & (col == 0)) | ((lane >= 64) & (col == 3))
    rim = jnp.where(outside, 0.0, jnp.where(by_even, from_even, from_odd)).astype(BF)
    rim_ref[...] = rim
    odd_row = lax.rem(row, 2)
    corner = lax.broadcasted_iota(jnp.int32, (CORNERS, 128), 0)
    source = lax.broadcasted_iota(jnp.int32, (CORNERS, 128), 1)
    for ref, low in ((up_ref, odd_row), (down_ref, 1 - odd_row)):
        first = (1 - low) * (TILE_ROWS - HALO)
        ref[0:C, :] = own_ref[:, pl.ds(pl.multiple_of(first * 128, 128), HALO * 128)]
        wanted = 2 * first + jnp.where(corner < 4, corner, 64 + corner - 4)
        pick = ((source == wanted) & (corner < 8)).astype(F32).astype(BF)
        ref[C:, :] = nt(pick, rim).astype(BF)


def in_image(place, table, start, stop):
    row, col = place[0], place[1]
    r, c = table[6:7, start:stop], table[7:8, start:stop]
    r_low = jnp.where(row > 0, -HALO, 0).astype(F32)
    r_high = jnp.where(row < 15, TILE_ROWS + HALO, TILE_ROWS).astype(F32)
    c_low = jnp.where(col > 0, -HALO, 0).astype(F32)
    c_high = jnp.where(col < 3, 2 * TILE_COLS + HALO, 2 * TILE_COLS).astype(F32)
    inside = (r >= r_low) & (r < r_high) & (c >= c_low) & (c < c_high)
    return jnp.where(inside, table[2:3, start:stop], 0.0)


def emit(phases):
    for pieces, work in phases:
        for start, stop in pieces:
            work(start, stop)


def enter(inputs, win_t, h1, ranges, mask):
    def work(start, stop):
        value = jnp.maximum(nn(win_t[...], inputs.get(start, stop)).astype(BF), ZERO)
        if mask is not None:
            value = value * mask(start, stop).astype(BF)
        h1.put(start, stop, value)

    return ranges, work


def spread(h1, hs, ranges):
    def work(start, stop):
        for s in range(3):
            hs.put(start, stop, h1.shifted(start, stop, s - 1), slice(s * MID, (s + 1) * MID))

    return ranges, work


def widen(wf, hs, wide, ranges):
    def work(start, stop):
        wide.put(start, stop, nn(wf[...], hs.get(start, stop)))

    return ranges, work


def leave(inputs, wide, wout_t, h2, output, ranges):
    def work(start, stop):
        total = sum(
            wide.shifted(start, stop, (r - 1) * COLS, slice(r * MID, (r + 1) * MID))
            for r in range(3)
        )
        value = jnp.maximum(total.astype(BF), ZERO)
        h2.put(start, stop, value)
        total = nn(wout_t[...], value) + inputs.get(start, stop).astype(F32)
        output.put(start, stop, jnp.maximum(total.astype(BF), ZERO))

    return ranges, work


X_SPAN = (INNER - 512, OUTER + 512)
HS1_SPAN = (INNER - 384, OUTER + 384)
Y1_SPAN = (INNER - 256, OUTER + 256)
Y2_SPAN = (INNER, OUTER)


def inner_kernel(
    place,
    flat_ref,
    spot_ref,
    rim_ref,
    table,
    win_t1,
    wf1,
    wout_t1,
    win_t2,
    wf2,
    wout_t2,
    x_ref,
    h1a_ref,
    hs1_ref,
    h2a_ref,
    y1_ref,
    h1b_ref,
    hs2_ref,
    h2b_ref,
    y2_ref,
    wide_ref,
):
    x, h1a = whole(x_ref, X_SPAN[0]), whole(h1a_ref, X_SPAN[0])
    hs1 = whole(hs1_ref, HS1_SPAN[0])
    h2a, y1 = whole(h2a_ref, Y1_SPAN[0]), whole(y1_ref, Y1_SPAN[0])
    h1b, hs2 = whole(h1b_ref, Y1_SPAN[0] - 128), whole(hs2_ref, Y1_SPAN[0])
    h2b, y2 = whole(h2b_ref, Y2_SPAN[0]), whole(y2_ref, Y2_SPAN[0])
    wide = whole(wide_ref, X_SPAN[0])
    wide_ref[:, 0:128] = jnp.zeros((3 * MID, 128), F32)
    wide_ref[:, wide_ref.shape[1] - 128 :] = jnp.zeros((3 * MID, 128), F32)
    h1b_ref[:, 0:128] = jnp.zeros((MID, 128), BF)
    h1b_ref[:, h1b_ref.shape[1] - 128 :] = jnp.zeros((MID, 128), BF)

    def lay_out(start, stop):
        value = nn(rim_ref[...], spot_ref[:, start:stop]) + flat_ref[:, start:stop].astype(F32)
        x.put(start, stop, value.astype(BF))

    mask = lambda start, stop: in_image(place, table, start, stop)
    x_pieces, hs1_pieces = cut(*X_SPAN), cut(*HS1_SPAN)
    y1_pieces, y2_pieces = cut(*Y1_SPAN), cut(*Y2_SPAN)
    emit(
        [
            (x_pieces, lay_out),
            enter(x, win_t1, h1a, x_pieces, None),
            spread(h1a, hs1, hs1_pieces),
            widen(wf1, hs1, wide, hs1_pieces),
            leave(x, wide, wout_t1, h2a, y1, y1_pieces),
            enter(y1, win_t2, h1b, y1_pieces, mask),
            spread(h1b, hs2, y1_pieces),
            widen(wf2, hs2, wide, y1_pieces),
            leave(y1, wide, wout_t2, h2b, y2, y2_pieces),
        ]
    )


def kernel(
    place,
    flat_ref,
    spot_ref,
    rim_ref,
    odd_ref,
    even_ref,
    table,
    momentum_ref,
    win_t1,
    wf1,
    wb1,
    wout_t1,
    wout1,
    win_t2,
    wf2,
    wb2,
    wout_t2,
    wout2,
    win2,
    head_ref,
    target_ref,
    x_mid,
    h1a_mid,
    hs1_mid,
    h2a_mid,
    y1_mid,
    h1b_mid,
    hs2_mid,
    h2b_mid,
    y2_mid,
    keep_ref,
    send_ref,
    packed,
    parts,
    x_ends,
    h1a_ends,
    hs1_ends,
    h2a_ends,
    y1_ends,
    h1b_ends,
    hs2_ends,
    h2b_ends,
    y2_ends,
    wide_ref,
    dg2_ref,
    ds,
    dz,
    tall,
):
    def joined(ends, mid, base):
        pad = (ends.shape[2] - CHUNK) // 2
        return Lanes(
            (-pad, INNER, ends.at[0], -pad),
            (INNER, OUTER, mid, base),
            (OUTER, LANES + pad, ends.at[1], OUTER - pad),
        )

    x = joined(x_ends, x_mid, X_SPAN[0])
    h1a = joined(h1a_ends, h1a_mid, X_SPAN[0])
    hs1 = joined(hs1_ends, hs1_mid, HS1_SPAN[0])
    h2a = joined(h2a_ends, h2a_mid, Y1_SPAN[0])
    y1 = joined(y1_ends, y1_mid, Y1_SPAN[0])
    h1b = joined(h1b_ends, h1b_mid, Y1_SPAN[0] - 128)
    hs2 = joined(hs2_ends, hs2_mid, Y1_SPAN[0])
    h2b = joined(h2b_ends, h2b_mid, Y2_SPAN[0])
    y2 = joined(y2_ends, y2_mid, Y2_SPAN[0])
    wide, dg2 = whole(wide_ref, -GUARD), whole(dg2_ref, -GUARD)
    for ref in (wide_ref, dg2_ref):
        ref[:, :GUARD] = jnp.zeros((ref.shape[0], GUARD), ref.dtype)
        ref[:, GUARD + LANES :] = jnp.zeros((ref.shape[0], GUARD), ref.dtype)
    for ref in (h1a_ends, h1b_ends):
        ref[0, :, 0:128] = jnp.zeros((MID, 128), BF)
        ref[1, :, CHUNK + 128 :] = jnp.zeros((MID, 128), BF)

    odd_row = lax.rem(place[0], 2) == 1
    above = jnp.where(odd_row, even_ref[...].astype(F32), odd_ref[...].astype(F32)).astype(BF)
    below = jnp.where(odd_row, odd_ref[...].astype(F32), even_ref[...].astype(F32)).astype(BF)
    for end, start, stop, k, rows in ((0, 0, INNER, 4, above), (1, OUTER, LANES, 5, below)):
        value = nn(rim_ref[...], spot_ref[:, start:stop]) + flat_ref[:, start:stop].astype(F32)
        corners = rows[C:, :].astype(F32).T.astype(BF)
        value = value + nn(corners, spots(CORNERS, table, k, start, stop))
        x_ends[end] = value.astype(BF)
        for r in range(HALO):
            lane = (r if end == 0 else ROWS - HALO + r) * COLS + HALO - start
            x_ends[end, :, lane : lane + 128] = rows[0:C, r * 128 : (r + 1) * 128]
    ends = [(0, INNER), (OUTER, LANES)]
    wider = [(0, INNER + 256), (OUTER - 256, LANES)]
    mask = lambda start, stop: in_image(place, table, start, stop)
    everything = cut(0, LANES)
    sums = {"pooled": jnp.zeros((C, 8), F32)}

    def pool(start, stop):
        sums["pooled"] += nt(y2.get(start, stop), table[:, start:stop].astype(BF))

    for start, stop in cut(INNER, OUTER):
        pool(start, stop)
    emit(
        [
            enter(x, win_t1, h1a, ends, None),
            spread(h1a, hs1, ends),
            widen(wf1, hs1, wide, wider),
            leave(x, wide, wout_t1, h2a, y1, ends),
            enter(y1, win_t2, h1b, ends, mask),
            spread(h1b, hs2, ends),
            widen(wf2, hs2, wide, wider),
            leave(y1, wide, wout_t2, h2b, y2, ends),
            (ends, pool),
        ]
    )
    pooled = sums["pooled"] * (1.0 / (TILE_ROWS * TILE_COLS))
    head = head_ref[...]
    loss = jnp.zeros((1, 1), F32)
    grad_head = jnp.zeros((C, CLASSES), F32)
    upstream = []
    for tile in range(2):
        column = pooled[:, tile : tile + 1]
        logits = jnp.sum(column * head, axis=0, keepdims=True)
        highest = jnp.max(logits, axis=1, keepdims=True)
        logsum = jnp.log(jnp.sum(jnp.exp(logits - highest), axis=1, keepdims=True)) + highest
        onehot = target_ref[tile : tile + 1, :]
        loss = loss + logsum - jnp.sum(onehot * logits, axis=1, keepdims=True)
        dlogits = (jnp.exp(logits - logsum) - onehot) * (1.0 / NTILES)
        grad_head = grad_head + column * dlogits
        dpooled = jnp.sum(head * dlogits, axis=1, keepdims=True) / (TILE_ROWS * TILE_COLS)
        upstream.append(dpooled.astype(BF))

    own, one = cut(256, 3584), cut(0, 3584)
    dz[:, 0:256] = jnp.zeros((C, 256), BF)
    dg2_ref[:, GUARD : GUARD + 256] = jnp.zeros((MID, 256), BF)
    dg2_ref[:, GUARD + 3584 :] = jnp.zeros((MID, LANES - 3584 + GUARD), BF)

    def seed(start, stop):
        first, second = (table[t : t + 1, start:stop].astype(BF) for t in range(2))
        value = upstream[0] * first + upstream[1] * second
        dz[:, start:stop] = jnp.where(y2.get(start, stop) > ZERO, value, ZERO)

    def pack_tall(value, row):
        count = value.shape[0]
        tall[0:count, :] = value
        half = count // 2
        packed[row : row + half, 0:MID] = tall[pl.ds(0, half, stride=2), :]
        packed[row : row + half, MID:] = tall[pl.ds(1, half, stride=2), :]

    def backward(inputs, wb, wout, h1, hs, h2, row, then, near, far):
        grads = {
            "out": jnp.zeros((C, MID), F32),
            "mid": jnp.zeros((3 * MID, 3 * MID), F32),
            "in": jnp.zeros((C, MID), F32),
        }

        def to_mid(start, stop):
            value = dz[:, start:stop]
            grads["out"] += nt(value, h2.get(start, stop))
            value = nn(wout[...], value).astype(BF)
            dg2.put(start, stop, jnp.where(h2.get(start, stop) > ZERO, value, ZERO))
            if (start, stop) == near[-1]:
                total = grads["out"].T
                packed[pl.ds(row + 416, MID, stride=2), :] = total[:, :128]
                packed[pl.ds(row + 417, MID, stride=2), :] = total[:, 128:]

        def through_taps(start, stop):
            for r in range(3):
                ds[r * MID : (r + 1) * MID, start:stop] = dg2.shifted(start, stop, (1 - r) * COLS)
            value = ds[:, start:stop]
            wide.put(start, stop, nn(wb[...], value))
            grads["mid"] += nt(hs.get(start, stop), value)
            if (start, stop) == far[-1]:
                for r in range(3):
                    pack_tall(grads["mid"][:, r * MID : (r + 1) * MID], row + 128 + r * 96)

        def to_inputs(start, stop):
            total = sum(
                wide.shifted(start, stop, 1 - s, slice(s * MID, (s + 1) * MID)) for s in range(3)
            )
            value = jnp.where(h1.get(start, stop) > ZERO, total.astype(BF), ZERO)
            grads["in"] += nt(inputs.get(start, stop), value)
            if then is not None:
                then(start, stop, value)
            if (start, stop) == far[-1]:
                pack_tall(grads["in"], row)
                if then is not None:
                    pack_shares(8)

        return [(near, to_mid), (far, through_taps), (far, to_inputs)]

    def to_first(start, stop, value):
        total = nn(win2[...], value) + dz[:, start:stop].astype(F32)
        dz[:, start:stop] = jnp.where(y1.get(start, stop) > ZERO, total.astype(BF), ZERO)

    tall[:, 0:CLASSES] = grad_head
    for j in range(16):
        packed[1088:1104, j * CLASSES : (j + 1) * CLASSES] = tall[
            pl.ds(j, 16, stride=16), 0:CLASSES
        ]

    row, col, core, far = place[0], place[1], place[2], place[3]
    lane = lax.broadcasted_iota(jnp.int32, (8, 128), 1)

    def pack_shares(low):
        for m in range(16):
            m_col, m_far, m_core = m // 4, m // 2 % 2, m % 2
            first, offset = 69 * low + SHARE * m // 128, SHARE * m % 128
            lines = [
                pltpu.roll(packed[pl.ds(first + j, 8, stride=69), :], (128 - offset) % 128, 1)
                for j in range(6)
            ]
            block = parts.at[m_core ^ core, m_col ^ col]
            for j in range(5):
                value = jnp.where(lane < 128 - offset, lines[j], lines[j + 1])
                if j == 4:
                    value = jnp.where(lane < 40, value, jnp.where(lane == 40, loss, 0.0))
                begin = m_far * 16 + low
                block[begin : begin + 8, j * 128 : (j + 1) * 128] = value

    emit(
        [(own, seed)]
        + backward(y1, wb2, wout2, h1b, hs2, h2b, 544, to_first, own, one)
        + backward(x, wb1, wout1, h1a, hs1, h2a, 0, None, one, everything)
    )

    pack_shares(0)
    mine = far * 16 + row
    parts[0, 0, pl.ds(mine, 1), :] = parts[0, 0, pl.ds(mine, 1), :] + 9.0 * momentum_ref[...]
    keep_ref[...] = parts[0]
    send_ref[...] = parts[1]


def total_kernel(place, own, got_a, got_b, got_c, row_ref, size_ref):
    total = (own[...] + got_a[...]) + (got_b[...] + got_c[...])
    lane = lax.broadcasted_iota(jnp.int32, (SHARES, PAD), 1)
    kept = jnp.where(lane < SHARE, jnp.abs(total), 0.0)
    size = jnp.sum(jnp.sum(kept, axis=0, keepdims=True), axis=1, keepdims=True)
    size_ref[...] = jnp.broadcast_to(size, (1, PAD))
    mine = place[3] * 16 + place[0]
    line = lax.broadcasted_iota(jnp.int32, (SHARES, PAD), 0)
    row_ref[...] = jnp.sum(jnp.where(line == mine, total, 0.0), axis=0, keepdims=True)


VMEM = pl.BlockSpec(memory_space=pltpu.VMEM)
SMEM = pl.BlockSpec(memory_space=pltpu.SMEM)
PARAMS = pltpu.CompilerParams(vmem_limit_bytes=36 * 1024 * 1024)


def shape(dims, kind):
    return jax.ShapeDtypeStruct(dims, kind)


def split(image):
    return pl.pallas_call(
        split_kernel,
        out_shape=(shape((C, TILE_ROWS * 128), BF), shape((C, 128), BF)),
        in_specs=[VMEM],
        out_specs=(VMEM, VMEM),
        scratch_shapes=[
            pltpu.VMEM((C * TILE_ROWS, 128), F32),
            pltpu.VMEM((TILE_ROWS * 128, 128), BF),
        ],
        compiler_params=PARAMS,
    )(image)


def prepare(labels, own, weights, table):
    square = shape((3 * MID, 3 * MID), BF)
    down, up = shape((MID, C), BF), shape((C, MID), BF)
    block = [down, square, square, up, down]
    return pl.pallas_call(
        prepare_kernel,
        out_shape=[shape((C, LANES), BF), shape((128, LANES), BF)] + block + block + [up, shape((C, CLASSES), F32), shape((8, CLASSES), F32)],
        in_specs=[SMEM] + [VMEM] * 3,
        out_specs=[VMEM] * 15,
        scratch_shapes=[pltpu.VMEM((C, MID), F32)],
        compiler_params=PARAMS,
        cost_estimate=pl.CostEstimate(flops=0, bytes_accessed=6_000_000, transcendentals=0),
    )(labels, own, weights.reshape(PARAM // 128, 128), table)


def rim(place, own, even, odd, after):
    return pl.pallas_call(
        rim_kernel,
        out_shape=(shape((C, 128), BF), shape(MSG, BF), shape(MSG, BF)),
        in_specs=[SMEM] + [VMEM] * 4,
        out_specs=(VMEM,) * 3,
        compiler_params=PARAMS,
    )(place, own, even, odd, after)


def inner(place, flat, spot, beyond, table, mats):
    win_t1, wf1, _, wout_t1, _, win_t2, wf2, _, wout_t2 = mats[:9]
    spans = [
        (C, X_SPAN),
        (MID, X_SPAN),
        (3 * MID, HS1_SPAN),
        (MID, Y1_SPAN),
        (C, Y1_SPAN),
        (MID, (Y1_SPAN[0] - 128, Y1_SPAN[1] + 128)),
        (3 * MID, Y1_SPAN),
        (MID, Y2_SPAN),
        (C, Y2_SPAN),
    ]
    return pl.pallas_call(
        inner_kernel,
        out_shape=[shape((rows, stop - start), BF) for rows, (start, stop) in spans],
        in_specs=[SMEM] + [VMEM] * 10,
        out_specs=[VMEM] * 9,
        scratch_shapes=[pltpu.VMEM((3 * MID, X_SPAN[1] - X_SPAN[0]), F32)],
        compiler_params=PARAMS,
        cost_estimate=pl.CostEstimate(
            flops=1_000_000_000, bytes_accessed=12_000_000, transcendentals=0
        ),
    )(place, flat, spot, beyond, table, win_t1, wf1, wout_t1, win_t2, wf2, wout_t2)


def compute(place, flat, spot, beyond, odd, even, table, momentum, mats, mids):
    return pl.pallas_call(
        kernel,
        out_shape=(shape((4, SHARES, PAD), F32), shape((4, SHARES, PAD), F32)),
        in_specs=[SMEM] + [VMEM] * 29,
        out_specs=(VMEM, VMEM),
        scratch_shapes=[
            pltpu.VMEM((PARAM // 128 + 8, 128), F32),
            pltpu.VMEM((2, 4, SHARES, PAD), F32),
            pltpu.VMEM((2, C, CHUNK), BF),
            pltpu.VMEM((2, MID, CHUNK + 256), BF),
            pltpu.VMEM((2, 3 * MID, CHUNK), BF),
            pltpu.VMEM((2, MID, CHUNK), BF),
            pltpu.VMEM((2, C, CHUNK), BF),
            pltpu.VMEM((2, MID, CHUNK + 256), BF),
            pltpu.VMEM((2, 3 * MID, CHUNK), BF),
            pltpu.VMEM((2, MID, CHUNK), BF),
            pltpu.VMEM((2, C, CHUNK), BF),
            pltpu.VMEM((3 * MID, WIDE), F32),
            pltpu.VMEM((MID, WIDE), BF),
            pltpu.VMEM((3 * MID, LANES), BF),
            pltpu.VMEM((C, LANES), BF),
            pltpu.VMEM((C, MID), F32),
        ],
        compiler_params=PARAMS,
    )(place, flat, spot, beyond, odd, even, table, momentum, *mats, *mids)


def make_table():
    pixel = np.arange(LANES)
    r, c = pixel // COLS - HALO, pixel % COLS - HALO
    real = pixel < PIX
    inside = real & (r >= 0) & (r < TILE_ROWS)
    tiles = [inside & (c >= t * TILE_COLS) & (c < (t + 1) * TILE_COLS) for t in range(2)]
    near = real & (r >= -1) & (r <= TILE_ROWS) & (c >= -1) & (c <= 2 * TILE_COLS)
    lane = np.where(c < 0, 2 * r + c + HALO, np.where(c >= 128, 64 + 2 * r + c - 128, -1000))
    corner = lambda k: np.where(c < 0, 2 * k + c + HALO, np.where(c >= 128, 4 + 2 * k + c - 128, -1000))
    sources = [
        np.where(inside, lane, -1000),
        np.where(real & (r < 0), corner(r + HALO), -1000),
        np.where(real & (r >= TILE_ROWS), corner(r - TILE_ROWS), -1000),
    ]
    return jnp.asarray(np.stack([*tiles, near, *sources, r, c]).astype(np.float32))


def local(image, labels, weights, momentum):
    row, col, dp = lax.axis_index("row"), lax.axis_index("col"), lax.axis_index("dp")
    place = jnp.stack([row, col, dp % 2, dp // 2]).astype(jnp.int32)
    table = make_table()
    padded_momentum = jnp.pad(momentum, (0, PAD - SHARE)).reshape(1, PAD)

    own, edge = split(image)
    even = lax.ppermute(edge, "col", neighbours(4, False))
    odd = lax.ppermute(edge, "col", neighbours(4, True, True))
    flat, spot, *mats = prepare(labels.reshape(2), own, weights, table)
    beyond, up, down = rim(place, own, even, odd, mats[-1])
    odd = lax.ppermute(down, "row", neighbours(16, True))
    even = lax.ppermute(up, "row", neighbours(16, False))
    mids = inner(place, flat, spot, beyond, table, mats)
    keep, send = compute(
        place, flat, spot, beyond, odd, even, table, padded_momentum, mats, mids
    )

    parts = keep + received([send], CORE)[0]
    parts = paired_sum(parts[0], received([parts[1], parts[3], parts[2]], X_RING))
    for stage in (Y_RING, Z_PAIR):
        parts = stage_sum(parts, stage)
    got = received([parts] * 3, Z_RING)
    share, magnitude = pl.pallas_call(
        total_kernel,
        out_shape=(shape((1, PAD), F32), shape((1, PAD), F32)),
        in_specs=[SMEM] + [VMEM] * 4,
        out_specs=(VMEM, VMEM),
        compiler_params=PARAMS,
    )(place, parts, *got)
    for stage in (CORE, X_RING):
        magnitude = stage_sum(magnitude, stage)
    scale_tau = 0.1 * magnitude[0, :SHARE] / PARAM + 1e-06
    loss = share[0, SHARE] / NTILES
    share = share[0, :SHARE]
    mixed = 0.1 * share
    update = mixed / (jnp.abs(mixed) + scale_tau)
    start = (row * 16 + col * 4 + dp) * SHARE
    weight_share = lax.dynamic_slice_in_dim(weights, start, SHARE, 0)
    new_weights = weight_share - 0.0001 * (update + 0.1 * weight_share)
    new_momentum = 0.9 * momentum + 0.01 * share
    return (new_weights, new_momentum, update, loss)


def solution(mesh):
    in_specs = (P("dp", None, "row", "col"), P("dp", "row", "col"), P(), P(("row", "col", "dp")))
    out_specs = (P(("row", "col", "dp")), P(("row", "col", "dp")), P(("row", "col", "dp")), P())
    return jax.shard_map(local, mesh=mesh, in_specs=in_specs, out_specs=out_specs, check_vma=False)
```

```python
import numpy as np
import jax
import jax.numpy as jnp
from jax import lax
from jax.experimental import pallas as pl
from jax.experimental.pallas import tpu as pltpu
from jax.sharding import PartitionSpec as P

C = 256
MID = 64
CLASSES = 8
TILE_ROWS = 24
TILE_COLS = 64
NTILES = 512
PARAM = 141312
SHARE = 552

HALO = 2
ROWS = TILE_ROWS + 2 * HALO
COLS = 2 * TILE_COLS + 2 * HALO
PIX = ROWS * COLS
LANES = 3840
GUARD = 256
WIDE = LANES + 2 * GUARD
CHUNK = 768
PIECE = 1024
INNER, OUTER = CHUNK, LANES - CHUNK

BF = jnp.bfloat16
F32 = jnp.float32
ZERO = np.zeros((), BF)

SHARES = 32
CORNERS = 16
MSG = (C + CORNERS, HALO * 128)
PAD = 640


def exchange(size, partner):
    return [(source, partner(source)) for source in range(size)]


def neighbours(size, odd, wrap=False):
    pairs = []
    for low in range(1 if odd else 0, size - 1, 2):
        pairs += [(low, low + 1), (low + 1, low)]
    if odd and wrap:
        pairs += [(0, size - 1), (size - 1, 0)]
    return pairs


def along_z(partner):
    pairs = []
    for row in range(16):
        for dp in range(4):
            z = partner(dp // 2 * 4 + row // 4)
            pairs.append((row * 4 + dp, (z % 4 * 4 + row % 4) * 4 + z // 4 * 2 + dp % 2))
    return pairs


def z_near(z):
    return (3, 2, 1, 0, 7, 6, 5, 4)[z]


CORE = ("dp", [exchange(4, lambda i: i ^ 1)])
X_RING = ("col", [exchange(4, lambda i, k=k: i ^ k) for k in (2, 3, 1)])
Y_RING = ("row", [exchange(16, lambda i, k=k: i ^ k) for k in (3, 1, 2)])
Z_PAIR = (("row", "dp"), [along_z(lambda z: z ^ 1)])
Z_RING = (
    ("row", "dp"),
    [along_z(lambda z: z ^ 5), along_z(lambda z: 7 - z), along_z(z_near)],
)


def received(values, stage):
    axis, exchanges = stage
    return [lax.ppermute(value, axis, pairs) for value, pairs in zip(values, exchanges)]


def paired_sum(own, got):
    if len(got) == 1:
        return own + got[0]
    return (own + got[0]) + (got[1] + got[2])


def stage_sum(value, stage):
    return paired_sum(value, received([value] * len(stage[1]), stage))


def nn(left, right):
    return lax.dot_general(left, right, (((1,), (0,)), ((), ())), preferred_element_type=F32)


def nt(left, right):
    return lax.dot_general(left, right, (((1,), (1,)), ((), ())), preferred_element_type=F32)


ALL_ROWS = slice(None)


def cut(start, stop):
    edges = list(range(start, stop, PIECE))
    if len(edges) > 1 and stop - edges[-1] <= 256:
        edges.pop()
    return list(zip(edges, edges[1:] + [stop]))


class Lanes:
    def __init__(self, *segments):
        self.segments = segments

    def get(self, start, stop, rows=ALL_ROWS):
        found = []
        for low, high, ref, base in self.segments:
            a, b = max(start, low), min(stop, high)
            if a < b:
                found.append(ref[rows, a - base : b - base])
        return found[0] if len(found) == 1 else jnp.concatenate(found, axis=1)

    def shifted(self, start, stop, shift, rows=ALL_ROWS):
        low = (start + shift) // 128 * 128
        high = -(-(stop + shift) // 128) * 128
        return self.get(low, high, rows)[:, start + shift - low : stop + shift - low]

    def put(self, start, stop, value, rows=ALL_ROWS):
        for low, high, ref, base in self.segments:
            if low <= start and stop <= high:
                ref[rows, start - base : stop - base] = value
                return
        raise ValueError("no segment")


def whole(ref, base=0):
    return Lanes((base, base + ref.shape[1], ref, base))


def split_kernel(image_ref, own_ref, edge_ref, tall, select):
    tall[...] = image_ref[0].astype(F32).reshape(C * TILE_ROWS, 128)
    lane = lax.broadcasted_iota(jnp.int32, (128, 128), 1)
    col = lax.broadcasted_iota(jnp.int32, (128, 128), 0)
    wanted = jnp.where(col < HALO, col + 4, jnp.where(col >= 126, col - 124, -1000))
    for r in range(TILE_ROWS):
        own_ref[:, r * 128 : (r + 1) * 128] = tall[pl.ds(r, C, stride=TILE_ROWS), :].astype(BF)
        select[r * 128 : (r + 1) * 128, :] = (lane - 4 * r == wanted).astype(F32).astype(BF)
    edge_ref[...] = nn(own_ref[...], select[...]).astype(BF)


def prepare_kernel(
    own_ref,
    weights_ref,
    table,
    flat_ref,
    spot_ref,
    win_t1,
    wf1,
    wb1,
    wout_t1,
    wout1,
    win_t2,
    wf2,
    wb2,
    wout_t2,
    wout2,
    win2,
    head_ref,
    tall,
):
    for start, stop in cut(*X_SPAN):
        source = lax.broadcasted_iota(jnp.int32, (128, stop - start), 0).astype(F32)
        spot_ref[:, start:stop] = (source == table[5:6, start:stop]).astype(F32).astype(BF)
    for r in range(TILE_ROWS):
        lane = (r + HALO) * COLS + HALO
        flat_ref[:, lane : lane + 128] = own_ref[:, r * 128 : (r + 1) * 128]
        flat_ref[:, lane - 2 * HALO : lane] = jnp.zeros((C, 2 * HALO), BF)
    first = HALO * COLS - HALO
    flat_ref[:, 0:first] = jnp.zeros((C, first), BF)
    last = (ROWS - HALO) * COLS - HALO
    flat_ref[:, last:] = jnp.zeros((C, LANES - last), BF)

    def unpacked(row, count):
        half = count // 2
        lines = weights_ref[row : row + half, :]
        tall[pl.ds(0, half, stride=2), :] = lines[:, :MID]
        tall[pl.ds(1, half, stride=2), :] = lines[:, MID:]
        return tall[0:count, :]

    for row, win_t, wf, wb, wout_t, wout, win in (
        (0, win_t1, wf1, wb1, wout_t1, wout1, None),
        (544, win_t2, wf2, wb2, wout_t2, wout2, win2),
    ):
        value = unpacked(row, C)
        win_t[...] = value.T.astype(BF)
        if win is not None:
            win[...] = value.astype(BF)
        value = jnp.concatenate([unpacked(row + 128 + r * 96, 3 * MID) for r in range(3)], axis=1)
        wb[...] = value.astype(BF)
        wf[...] = value.T.astype(BF)
        value = jnp.concatenate(
            [weights_ref[pl.ds(row + 416 + k, MID, stride=2), :] for k in range(2)], axis=1
        )
        wout[...] = value.astype(BF)
        wout_t[...] = value.T.astype(BF)
    for j in range(16):
        tall[pl.ds(j, 16, stride=16), 0:CLASSES] = weights_ref[
            1088:1104, j * CLASSES : (j + 1) * CLASSES
        ]
    head_ref[...] = tall[:, 0:CLASSES]


def rim_kernel(place, own_ref, odd_ref, even_ref, _, rim_ref, up_ref, down_ref):
    row, col = place[0], place[1]
    on_left = lax.rem(lax.broadcasted_iota(jnp.int32, (C, 128), 1), 4) >= 2
    odd_col = lax.rem(col, 2)
    from_even = even_ref[...].astype(F32)
    from_odd = odd_ref[...].astype(F32)
    by_even = on_left.astype(jnp.int32) == odd_col
    outside = (on_left & (col == 0)) | (~on_left & (col == 3))
    rim = jnp.where(outside, 0.0, jnp.where(by_even, from_even, from_odd)).astype(BF)
    rim_ref[...] = rim
    odd_row = lax.rem(row, 2)
    corner = lax.broadcasted_iota(jnp.int32, (CORNERS, 128), 0)
    source = lax.broadcasted_iota(jnp.int32, (CORNERS, 128), 1)
    for ref, low in ((up_ref, odd_row), (down_ref, 1 - odd_row)):
        first = (1 - low) * (TILE_ROWS - HALO)
        ref[0:C, :] = own_ref[:, pl.ds(pl.multiple_of(first * 128, 128), HALO * 128)]
        row_of, pixel = lax.rem(corner, 4) // 2, lax.rem(corner, 2)
        wanted = 4 * (first + row_of) + pixel + jnp.where(corner < 4, 2, 4)
        pick = ((source == wanted) & (corner < 8)).astype(F32).astype(BF)
        ref[C:, :] = nt(pick, rim).astype(BF)


def in_image(place, table, start, stop):
    row, col = place[0], place[1]
    r, c = table[3:4, start:stop], table[4:5, start:stop]
    r_low = jnp.where(row > 0, -HALO, 0).astype(F32)
    r_high = jnp.where(row < 15, TILE_ROWS + HALO, TILE_ROWS).astype(F32)
    c_low = jnp.where(col > 0, -HALO, 0).astype(F32)
    c_high = jnp.where(col < 3, 2 * TILE_COLS + HALO, 2 * TILE_COLS).astype(F32)
    inside = (r >= r_low) & (r < r_high) & (c >= c_low) & (c < c_high)
    return jnp.where(inside, table[2:3, start:stop], 0.0)


def emit(phases):
    for pieces, work in phases:
        for start, stop in pieces:
            work(start, stop)


def put_rim(ref, rim, start, stop):
    for b in range(TILE_ROWS + 1):
        lane = (b + HALO) * COLS - HALO
        if start <= lane and lane + 2 * HALO <= stop:
            ref[:, lane - start : lane - start + 2 * HALO] = rim[:, 4 * b : 4 * b + 4]


def enter(inputs, win_t, h1, ranges, mask):
    def work(start, stop):
        value = jnp.maximum(nn(win_t[...], inputs.get(start, stop)).astype(BF), ZERO)
        if mask is not None:
            value = value * mask(start, stop).astype(BF)
        h1.put(start, stop, value)

    return ranges, work


def spread(h1, hs, ranges):
    def work(start, stop):
        for s in range(3):
            hs.put(start, stop, h1.shifted(start, stop, s - 1), slice(s * MID, (s + 1) * MID))

    return ranges, work


def widen(wf, hs, wide, ranges):
    def work(start, stop):
        wide.put(start, stop, nn(wf[...], hs.get(start, stop)))

    return ranges, work


def leave(inputs, wide, wout_t, h2, output, ranges):
    def work(start, stop):
        total = sum(
            wide.shifted(start, stop, (r - 1) * COLS, slice(r * MID, (r + 1) * MID))
            for r in range(3)
        )
        value = jnp.maximum(total.astype(BF), ZERO)
        h2.put(start, stop, value)
        total = nn(wout_t[...], value) + inputs.get(start, stop).astype(F32)
        output.put(start, stop, jnp.maximum(total.astype(BF), ZERO))

    return ranges, work


X_SPAN = (INNER - 512, OUTER + 512)
HS1_SPAN = (INNER - 384, OUTER + 384)
Y1_SPAN = (INNER - 256, OUTER + 256)
Y2_SPAN = (INNER, OUTER)


def inner_kernel(
    place,
    flat_ref,
    spot_ref,
    rim_ref,
    table,
    win_t1,
    wf1,
    wout_t1,
    win_t2,
    wf2,
    wout_t2,
    x_ref,
    h1a_ref,
    hs1_ref,
    h2a_ref,
    y1_ref,
    h1b_ref,
    hs2_ref,
    h2b_ref,
    y2_ref,
    wide_ref,
):
    x, h1a = whole(x_ref, X_SPAN[0]), whole(h1a_ref, X_SPAN[0])
    hs1 = whole(hs1_ref, HS1_SPAN[0])
    h2a, y1 = whole(h2a_ref, Y1_SPAN[0]), whole(y1_ref, Y1_SPAN[0])
    h1b, hs2 = whole(h1b_ref, Y1_SPAN[0] - 128), whole(hs2_ref, Y1_SPAN[0])
    h2b, y2 = whole(h2b_ref, Y2_SPAN[0]), whole(y2_ref, Y2_SPAN[0])
    wide = whole(wide_ref, X_SPAN[0])
    wide_ref[:, 0:128] = jnp.zeros((3 * MID, 128), F32)
    wide_ref[:, wide_ref.shape[1] - 128 :] = jnp.zeros((3 * MID, 128), F32)
    h1b_ref[:, 0:128] = jnp.zeros((MID, 128), BF)
    h1b_ref[:, h1b_ref.shape[1] - 128 :] = jnp.zeros((MID, 128), BF)

    def lay_out(start, stop):
        value = nn(rim_ref[...], spot_ref[:, start:stop]) + flat_ref[:, start:stop].astype(F32)
        x.put(start, stop, value.astype(BF))

    mask = lambda start, stop: in_image(place, table, start, stop)
    x_pieces, hs1_pieces = cut(*X_SPAN), cut(*HS1_SPAN)
    y1_pieces, y2_pieces = cut(*Y1_SPAN), cut(*Y2_SPAN)
    emit(
        [
            (x_pieces, lay_out),
            enter(x, win_t1, h1a, x_pieces, None),
            spread(h1a, hs1, hs1_pieces),
            widen(wf1, hs1, wide, hs1_pieces),
            leave(x, wide, wout_t1, h2a, y1, y1_pieces),
            enter(y1, win_t2, h1b, y1_pieces, mask),
            spread(h1b, hs2, y1_pieces),
            widen(wf2, hs2, wide, y1_pieces),
            leave(y1, wide, wout_t2, h2b, y2, y2_pieces),
        ]
    )


def kernel(
    place,
    flat_ref,
    rim_ref,
    odd_ref,
    even_ref,
    table,
    momentum_ref,
    win_t1,
    wf1,
    wb1,
    wout_t1,
    wout1,
    win_t2,
    wf2,
    wb2,
    wout_t2,
    wout2,
    win2,
    head_ref,
    target_ref,
    x_mid,
    h1a_mid,
    hs1_mid,
    h2a_mid,
    y1_mid,
    h1b_mid,
    hs2_mid,
    h2b_mid,
    y2_mid,
    keep_ref,
    send_ref,
    packed,
    parts,
    x_ends,
    h1a_ends,
    hs1_ends,
    h2a_ends,
    y1_ends,
    h1b_ends,
    hs2_ends,
    h2b_ends,
    y2_ends,
    wide_ref,
    dg2_ref,
    ds,
    dz,
    tall,
):
    def joined(ends, mid, base):
        pad = (ends.shape[2] - CHUNK) // 2
        return Lanes(
            (-pad, INNER, ends.at[0], -pad),
            (INNER, OUTER, mid, base),
            (OUTER, LANES + pad, ends.at[1], OUTER - pad),
        )

    x = joined(x_ends, x_mid, X_SPAN[0])
    h1a = joined(h1a_ends, h1a_mid, X_SPAN[0])
    hs1 = joined(hs1_ends, hs1_mid, HS1_SPAN[0])
    h2a = joined(h2a_ends, h2a_mid, Y1_SPAN[0])
    y1 = joined(y1_ends, y1_mid, Y1_SPAN[0])
    h1b = joined(h1b_ends, h1b_mid, Y1_SPAN[0] - 128)
    hs2 = joined(hs2_ends, hs2_mid, Y1_SPAN[0])
    h2b = joined(h2b_ends, h2b_mid, Y2_SPAN[0])
    y2 = joined(y2_ends, y2_mid, Y2_SPAN[0])
    wide, dg2 = whole(wide_ref, -GUARD), whole(dg2_ref, -GUARD)
    for ref in (wide_ref, dg2_ref):
        ref[:, :GUARD] = jnp.zeros((ref.shape[0], GUARD), ref.dtype)
        ref[:, GUARD + LANES :] = jnp.zeros((ref.shape[0], GUARD), ref.dtype)
    for ref in (h1a_ends, h1b_ends):
        ref[0, :, 0:128] = jnp.zeros((MID, 128), BF)
        ref[1, :, CHUNK + 128 :] = jnp.zeros((MID, 128), BF)

    odd_row = lax.rem(place[0], 2) == 1
    above = jnp.where(odd_row, even_ref[...].astype(F32), odd_ref[...].astype(F32)).astype(BF)
    below = jnp.where(odd_row, odd_ref[...].astype(F32), even_ref[...].astype(F32)).astype(BF)
    for end, start, stop, rows in ((0, 0, INNER, above), (1, OUTER, LANES, below)):
        ref = x_ends.at[end]
        ref[...] = flat_ref[:, start:stop]
        put_rim(ref, rim_ref, start, stop)
        corners = rows[C:, :].astype(F32).T.astype(BF)
        for k in range(HALO):
            lane = (k if end == 0 else ROWS - HALO + k) * COLS - start
            ref[:, lane : lane + HALO] = corners[:, 2 * k : 2 * k + 2]
            ref[:, lane + HALO : lane + HALO + 128] = rows[0:C, k * 128 : (k + 1) * 128]
            ref[:, lane + HALO + 128 : lane + COLS] = corners[:, 4 + 2 * k : 6 + 2 * k]
    ends = [(0, INNER), (OUTER, LANES)]
    wider = [(0, INNER + 256), (OUTER - 256, LANES)]
    mask = lambda start, stop: in_image(place, table, start, stop)
    everything = cut(0, LANES)
    sums = {"pooled": jnp.zeros((C, 8), F32)}

    def pool(start, stop):
        sums["pooled"] += nt(y2.get(start, stop), table[:, start:stop].astype(BF))

    for start, stop in cut(INNER, OUTER):
        pool(start, stop)
    emit(
        [
            enter(x, win_t1, h1a, ends, None),
            spread(h1a, hs1, ends),
            widen(wf1, hs1, wide, wider),
            leave(x, wide, wout_t1, h2a, y1, ends),
            enter(y1, win_t2, h1b, ends, mask),
            spread(h1b, hs2, ends),
            widen(wf2, hs2, wide, wider),
            leave(y1, wide, wout_t2, h2b, y2, ends),
            (ends, pool),
        ]
    )
    pooled = sums["pooled"] * (1.0 / (TILE_ROWS * TILE_COLS))
    head = head_ref[...]
    loss = jnp.zeros((1, 1), F32)
    grad_head = jnp.zeros((C, CLASSES), F32)
    upstream = []
    for tile in range(2):
        column = pooled[:, tile : tile + 1]
        logits = jnp.sum(column * head, axis=0, keepdims=True)
        highest = jnp.max(logits, axis=1, keepdims=True)
        logsum = jnp.log(jnp.sum(jnp.exp(logits - highest), axis=1, keepdims=True)) + highest
        onehot = target_ref[tile : tile + 1, :]
        loss = loss + logsum - jnp.sum(onehot * logits, axis=1, keepdims=True)
        dlogits = (jnp.exp(logits - logsum) - onehot) * (1.0 / NTILES)
        grad_head = grad_head + column * dlogits
        dpooled = jnp.sum(head * dlogits, axis=1, keepdims=True) / (TILE_ROWS * TILE_COLS)
        upstream.append(dpooled.astype(BF))

    own, one = cut(256, 3584), cut(0, 3584)
    dz[:, 0:256] = jnp.zeros((C, 256), BF)
    dg2_ref[:, GUARD : GUARD + 256] = jnp.zeros((MID, 256), BF)
    dg2_ref[:, GUARD + 3584 :] = jnp.zeros((MID, LANES - 3584 + GUARD), BF)

    def seed(start, stop):
        first, second = (table[t : t + 1, start:stop].astype(BF) for t in range(2))
        value = upstream[0] * first + upstream[1] * second
        dz[:, start:stop] = jnp.where(y2.get(start, stop) > ZERO, value, ZERO)

    def pack_tall(value, row):
        count = value.shape[0]
        tall[0:count, :] = value
        half = count // 2
        packed[row : row + half, 0:MID] = tall[pl.ds(0, half, stride=2), :]
        packed[row : row + half, MID:] = tall[pl.ds(1, half, stride=2), :]

    def backward(inputs, wb, wout, h1, hs, h2, row, then, near, far):
        grads = {
            "out": jnp.zeros((C, MID), F32),
            "mid": jnp.zeros((3 * MID, 3 * MID), F32),
            "in": jnp.zeros((C, MID), F32),
        }

        def to_mid(start, stop):
            value = dz[:, start:stop]
            grads["out"] += nt(value, h2.get(start, stop))
            value = nn(wout[...], value).astype(BF)
            dg2.put(start, stop, jnp.where(h2.get(start, stop) > ZERO, value, ZERO))
            if (start, stop) == near[-1]:
                total = grads["out"].T
                packed[pl.ds(row + 416, MID, stride=2), :] = total[:, :128]
                packed[pl.ds(row + 417, MID, stride=2), :] = total[:, 128:]

        def through_taps(start, stop):
            for r in range(3):
                ds[r * MID : (r + 1) * MID, start:stop] = dg2.shifted(start, stop, (1 - r) * COLS)
            value = ds[:, start:stop]
            wide.put(start, stop, nn(wb[...], value))
            grads["mid"] += nt(hs.get(start, stop), value)
            if (start, stop) == far[-1]:
                for r in range(3):
                    pack_tall(grads["mid"][:, r * MID : (r + 1) * MID], row + 128 + r * 96)

        def to_inputs(start, stop):
            total = sum(
                wide.shifted(start, stop, 1 - s, slice(s * MID, (s + 1) * MID)) for s in range(3)
            )
            value = jnp.where(h1.get(start, stop) > ZERO, total.astype(BF), ZERO)
            grads["in"] += nt(inputs.get(start, stop), value)
            if then is not None:
                then(start, stop, value)
            if (start, stop) == far[-1]:
                pack_tall(grads["in"], row)
                if then is not None:
                    pack_shares(8)

        return [(near, to_mid), (far, through_taps), (far, to_inputs)]

    def to_first(start, stop, value):
        total = nn(win2[...], value) + dz[:, start:stop].astype(F32)
        dz[:, start:stop] = jnp.where(y1.get(start, stop) > ZERO, total.astype(BF), ZERO)

    tall[:, 0:CLASSES] = grad_head
    for j in range(16):
        packed[1088:1104, j * CLASSES : (j + 1) * CLASSES] = tall[
            pl.ds(j, 16, stride=16), 0:CLASSES
        ]

    row, col, core, far = place[0], place[1], place[2], place[3]
    lane = lax.broadcasted_iota(jnp.int32, (8, 128), 1)

    def pack_shares(low):
        for m in range(16):
            m_col, m_far, m_core = m // 4, m // 2 % 2, m % 2
            first, offset = 69 * low + SHARE * m // 128, SHARE * m % 128
            lines = [
                pltpu.roll(packed[pl.ds(first + j, 8, stride=69), :], (128 - offset) % 128, 1)
                for j in range(6)
            ]
            block = parts.at[m_core ^ core, m_col ^ col]
            for j in range(5):
                value = jnp.where(lane < 128 - offset, lines[j], lines[j + 1])
                if j == 4:
                    value = jnp.where(lane < 40, value, jnp.where(lane == 40, loss, 0.0))
                begin = m_far * 16 + low
                block[begin : begin + 8, j * 128 : (j + 1) * 128] = value

    emit(
        [(own, seed)]
        + backward(y1, wb2, wout2, h1b, hs2, h2b, 544, to_first, own, one)
        + backward(x, wb1, wout1, h1a, hs1, h2a, 0, None, one, everything)
    )

    pack_shares(0)
    mine = far * 16 + row
    parts[0, 0, pl.ds(mine, 1), :] = parts[0, 0, pl.ds(mine, 1), :] + 9.0 * momentum_ref[...]
    keep_ref[...] = parts[0]
    send_ref[...] = parts[1]


def total_kernel(place, own, got_a, got_b, got_c, row_ref, size_ref):
    total = (own[...] + got_a[...]) + (got_b[...] + got_c[...])
    lane = lax.broadcasted_iota(jnp.int32, (SHARES, PAD), 1)
    kept = jnp.where(lane < SHARE, jnp.abs(total), 0.0)
    size = jnp.sum(jnp.sum(kept, axis=0, keepdims=True), axis=1, keepdims=True)
    size_ref[...] = jnp.broadcast_to(size, (1, PAD))
    mine = place[3] * 16 + place[0]
    line = lax.broadcasted_iota(jnp.int32, (SHARES, PAD), 0)
    row_ref[...] = jnp.sum(jnp.where(line == mine, total, 0.0), axis=0, keepdims=True)


VMEM = pl.BlockSpec(memory_space=pltpu.VMEM)
SMEM = pl.BlockSpec(memory_space=pltpu.SMEM)
PARAMS = pltpu.CompilerParams(vmem_limit_bytes=36 * 1024 * 1024)


def shape(dims, kind):
    return jax.ShapeDtypeStruct(dims, kind)


def split(image):
    return pl.pallas_call(
        split_kernel,
        out_shape=(shape((C, TILE_ROWS * 128), BF), shape((C, 128), BF)),
        in_specs=[VMEM],
        out_specs=(VMEM, VMEM),
        scratch_shapes=[
            pltpu.VMEM((C * TILE_ROWS, 128), F32),
            pltpu.VMEM((TILE_ROWS * 128, 128), BF),
        ],
        compiler_params=PARAMS,
    )(image)


def prepare(own, weights, table):
    square = shape((3 * MID, 3 * MID), BF)
    down, up = shape((MID, C), BF), shape((C, MID), BF)
    block = [down, square, square, up, down]
    return pl.pallas_call(
        prepare_kernel,
        out_shape=[shape((C, LANES), BF), shape((128, LANES), BF)] + block + block + [up, shape((C, CLASSES), F32)],
        in_specs=[VMEM] * 3,
        out_specs=[VMEM] * 14,
        scratch_shapes=[pltpu.VMEM((C, MID), F32)],
        compiler_params=PARAMS,
        cost_estimate=pl.CostEstimate(flops=0, bytes_accessed=6_000_000, transcendentals=0),
    )(own, weights.reshape(PARAM // 128, 128), table)


def rim(place, own, odd, even, after):
    return pl.pallas_call(
        rim_kernel,
        out_shape=(shape((C, 128), BF), shape(MSG, BF), shape(MSG, BF)),
        in_specs=[SMEM] + [VMEM] * 4,
        out_specs=(VMEM,) * 3,
        compiler_params=PARAMS,
    )(place, own, odd, even, after)


def inner(place, flat, spot, beyond, table, mats):
    win_t1, wf1, _, wout_t1, _, win_t2, wf2, _, wout_t2 = mats[:9]
    spans = [
        (C, X_SPAN),
        (MID, X_SPAN),
        (3 * MID, HS1_SPAN),
        (MID, Y1_SPAN),
        (C, Y1_SPAN),
        (MID, (Y1_SPAN[0] - 128, Y1_SPAN[1] + 128)),
        (3 * MID, Y1_SPAN),
        (MID, Y2_SPAN),
        (C, Y2_SPAN),
    ]
    return pl.pallas_call(
        inner_kernel,
        out_shape=[shape((rows, stop - start), BF) for rows, (start, stop) in spans],
        in_specs=[SMEM] + [VMEM] * 10,
        out_specs=[VMEM] * 9,
        scratch_shapes=[pltpu.VMEM((3 * MID, X_SPAN[1] - X_SPAN[0]), F32)],
        compiler_params=PARAMS,
        cost_estimate=pl.CostEstimate(
            flops=1_000_000_000, bytes_accessed=12_000_000, transcendentals=0
        ),
    )(place, flat, spot, beyond, table, win_t1, wf1, wout_t1, win_t2, wf2, wout_t2)


def compute(place, flat, beyond, odd, even, table, momentum, mats, mids):
    return pl.pallas_call(
        kernel,
        out_shape=(shape((4, SHARES, PAD), F32), shape((4, SHARES, PAD), F32)),
        in_specs=[SMEM] + [VMEM] * 28,
        out_specs=(VMEM, VMEM),
        scratch_shapes=[
            pltpu.VMEM((PARAM // 128 + 8, 128), F32),
            pltpu.VMEM((2, 4, SHARES, PAD), F32),
            pltpu.VMEM((2, C, CHUNK), BF),
            pltpu.VMEM((2, MID, CHUNK + 256), BF),
            pltpu.VMEM((2, 3 * MID, CHUNK), BF),
            pltpu.VMEM((2, MID, CHUNK), BF),
            pltpu.VMEM((2, C, CHUNK), BF),
            pltpu.VMEM((2, MID, CHUNK + 256), BF),
            pltpu.VMEM((2, 3 * MID, CHUNK), BF),
            pltpu.VMEM((2, MID, CHUNK), BF),
            pltpu.VMEM((2, C, CHUNK), BF),
            pltpu.VMEM((3 * MID, WIDE), F32),
            pltpu.VMEM((MID, WIDE), BF),
            pltpu.VMEM((3 * MID, LANES), BF),
            pltpu.VMEM((C, LANES), BF),
            pltpu.VMEM((C, MID), F32),
        ],
        compiler_params=PARAMS,
    )(place, flat, beyond, odd, even, table, momentum, *mats, *mids)


def make_table():
    pixel = np.arange(LANES)
    r, c = pixel // COLS - HALO, pixel % COLS - HALO
    real = pixel < PIX
    inside = real & (r >= 0) & (r < TILE_ROWS)
    tiles = [inside & (c >= t * TILE_COLS) & (c < (t + 1) * TILE_COLS) for t in range(2)]
    near = real & (r >= -1) & (r <= TILE_ROWS) & (c >= -1) & (c <= 2 * TILE_COLS)
    lane = np.where(c < 0, 4 * r + c + 4, np.where(c >= 128, 4 * r + c - 124, -1000))
    lane = np.where(real & (r >= 0) & (r < TILE_ROWS), lane, -1000)
    return jnp.asarray(np.stack([*tiles, near, r, c, lane, 0 * r, 0 * r]).astype(np.float32))


def local(image, labels, weights, momentum):
    row, col, dp = lax.axis_index("row"), lax.axis_index("col"), lax.axis_index("dp")
    place = jnp.stack([row, col, dp % 2, dp // 2]).astype(jnp.int32)
    table = make_table()
    targets = (labels.reshape(2, 1) == jnp.arange(CLASSES, dtype=jnp.int32)).astype(F32)
    padded_momentum = jnp.pad(momentum, (0, PAD - SHARE)).reshape(1, PAD)

    own, edge = split(image)
    odd = lax.ppermute(edge, "col", neighbours(4, True, True))
    even = lax.ppermute(edge, "col", neighbours(4, False))
    flat, spot, *mats = prepare(own, weights, table)
    beyond, up, down = rim(place, own, odd, even, mats[-1])
    odd = lax.ppermute(down, "row", neighbours(16, True))
    even = lax.ppermute(up, "row", neighbours(16, False))
    mids = inner(place, flat, spot, beyond, table, mats)
    keep, send = compute(
        place, flat, beyond, odd, even, table, padded_momentum, [*mats, targets], mids
    )

    parts = keep + received([send], CORE)[0]
    parts = paired_sum(parts[0], received([parts[2], parts[3], parts[1]], X_RING))
    for stage in (Y_RING, Z_PAIR):
        parts = stage_sum(parts, stage)
    got = received([parts] * 3, Z_RING)
    share, magnitude = pl.pallas_call(
        total_kernel,
        out_shape=(shape((1, PAD), F32), shape((1, PAD), F32)),
        in_specs=[SMEM] + [VMEM] * 4,
        out_specs=(VMEM, VMEM),
        compiler_params=PARAMS,
    )(place, parts, *got)
    for stage in (CORE, X_RING):
        magnitude = stage_sum(magnitude, stage)
    scale_tau = 0.1 * magnitude[0, :SHARE] / PARAM + 1e-06
    loss = share[0, SHARE] / NTILES
    share = share[0, :SHARE]
    mixed = 0.1 * share
    update = mixed / (jnp.abs(mixed) + scale_tau)
    start = (row * 16 + col * 4 + dp) * SHARE
    weight_share = lax.dynamic_slice_in_dim(weights, start, SHARE, 0)
    new_weights = weight_share - 0.0001 * (update + 0.1 * weight_share)
    new_momentum = 0.9 * momentum + 0.01 * share
    return (new_weights, new_momentum, update, loss)


def solution(mesh):
    in_specs = (P("dp", None, "row", "col"), P("dp", "row", "col"), P(), P(("row", "col", "dp")))
    out_specs = (P(("row", "col", "dp")), P(("row", "col", "dp")), P(("row", "col", "dp")), P())
    return jax.shard_map(local, mesh=mesh, in_specs=in_specs, out_specs=out_specs, check_vma=False)
```

```python
import numpy as np
import jax
import jax.numpy as jnp
from jax import lax
from jax.experimental import pallas as pl
from jax.experimental.pallas import tpu as pltpu
from jax.sharding import PartitionSpec as P

C = 256
MID = 64
CLASSES = 8
TILE_ROWS = 24
TILE_COLS = 64
NTILES = 512
PARAM = 141312
SHARE = 552

HALO = 2
ROWS = TILE_ROWS + 2 * HALO
COLS = 2 * TILE_COLS + 2 * HALO
PIX = ROWS * COLS
LANES = 3840
GUARD = 256
WIDE = LANES + 2 * GUARD
CHUNK = 768
PIECE = 1024
INNER, OUTER = CHUNK, LANES - CHUNK

BF = jnp.bfloat16
F32 = jnp.float32
ZERO = np.zeros((), BF)

REST = 40
LINES = 144
CORNERS = 16
MSG = (C + CORNERS, HALO * 128)
PAD = 640


def exchange(size, partner):
    return [(source, partner(source)) for source in range(size)]


def neighbours(size, odd, wrap=False):
    pairs = []
    for low in range(1 if odd else 0, size - 1, 2):
        pairs += [(low, low + 1), (low + 1, low)]
    if odd and wrap:
        pairs += [(0, size - 1), (size - 1, 0)]
    return pairs


def along_z(partner):
    pairs = []
    for row in range(16):
        for dp in range(4):
            z = partner(dp // 2 * 4 + row // 4)
            pairs.append((row * 4 + dp, (z % 4 * 4 + row % 4) * 4 + z // 4 * 2 + dp % 2))
    return pairs


def z_near(z):
    return (3, 2, 1, 0, 7, 6, 5, 4)[z]


CORE = ("dp", [exchange(4, lambda i: i ^ 1)])
X_RING = ("col", [exchange(4, lambda i, k=k: i ^ k) for k in (2, 3, 1)])
Y_RING = ("row", [exchange(16, lambda i, k=k: i ^ k) for k in (3, 1, 2)])
Z_PAIR = (("row", "dp"), [along_z(lambda z: z ^ 1)])
Z_RING = (
    ("row", "dp"),
    [along_z(lambda z: z ^ 5), along_z(lambda z: 7 - z), along_z(z_near)],
)


def received(values, stage):
    axis, exchanges = stage
    return [lax.ppermute(value, axis, pairs) for value, pairs in zip(values, exchanges)]


def paired_sum(own, got):
    if len(got) == 1:
        return own + got[0]
    return (own + got[0]) + (got[1] + got[2])


def stage_sum(value, stage):
    return paired_sum(value, received([value] * len(stage[1]), stage))


def nn(left, right):
    return lax.dot_general(left, right, (((1,), (0,)), ((), ())), preferred_element_type=F32)


def nt(left, right):
    return lax.dot_general(left, right, (((1,), (1,)), ((), ())), preferred_element_type=F32)


ALL_ROWS = slice(None)


def cut(start, stop):
    edges = list(range(start, stop, PIECE))
    if len(edges) > 1 and stop - edges[-1] <= 256:
        edges.pop()
    return list(zip(edges, edges[1:] + [stop]))


class Lanes:
    def __init__(self, *segments):
        self.segments = segments

    def get(self, start, stop, rows=ALL_ROWS):
        found = []
        for low, high, ref, base in self.segments:
            a, b = max(start, low), min(stop, high)
            if a < b:
                found.append(ref[rows, a - base : b - base])
        return found[0] if len(found) == 1 else jnp.concatenate(found, axis=1)

    def shifted(self, start, stop, shift, rows=ALL_ROWS):
        low = (start + shift) // 128 * 128
        high = -(-(stop + shift) // 128) * 128
        return self.get(low, high, rows)[:, start + shift - low : stop + shift - low]

    def put(self, start, stop, value, rows=ALL_ROWS):
        for low, high, ref, base in self.segments:
            if low <= start and stop <= high:
                ref[rows, start - base : stop - base] = value
                return
        raise ValueError("no segment")


def whole(ref, base=0):
    return Lanes((base, base + ref.shape[1], ref, base))


def split_kernel(image_ref, own_ref, left_ref, right_ref, tall, select):
    tall[...] = image_ref[0].astype(F32).reshape(C * TILE_ROWS, 128)
    lane = lax.broadcasted_iota(jnp.int32, (128, 128), 1)
    col = lax.broadcasted_iota(jnp.int32, (128, 128), 0)
    wanted = jnp.where(col < HALO, col + 64, jnp.where(col >= 126, col - 126, -1000))
    for r in range(TILE_ROWS):
        own_ref[:, r * 128 : (r + 1) * 128] = tall[pl.ds(r, C, stride=TILE_ROWS), :].astype(BF)
        select[r * 128 : (r + 1) * 128, :] = (lane - 2 * r == wanted).astype(F32).astype(BF)
    edges = nn(own_ref[...], select[...])
    low, high = edges[:128], edges[128:]
    right_ref[...] = jnp.where(lane < 64, low, pltpu.roll(high, 64, 1)).astype(BF)
    left_ref[...] = jnp.where(lane < 64, pltpu.roll(low, 64, 1), high).astype(BF)


def prepare_kernel(
    own_ref,
    weights_ref,
    table,
    flat_ref,
    spot_ref,
    win_t1,
    wf1,
    wb1,
    wout_t1,
    wout1,
    win_t2,
    wf2,
    wb2,
    wout_t2,
    wout2,
    win2,
    head_ref,
    tall,
):
    for start, stop in cut(*X_SPAN):
        source = lax.broadcasted_iota(jnp.int32, (128, stop - start), 0).astype(F32)
        spot_ref[:, start:stop] = (source == table[5:6, start:stop]).astype(F32).astype(BF)
    for r in range(TILE_ROWS):
        lane = (r + HALO) * COLS + HALO
        flat_ref[:, lane : lane + 128] = own_ref[:, r * 128 : (r + 1) * 128]
        flat_ref[:, lane - 2 * HALO : lane] = jnp.zeros((C, 2 * HALO), BF)
    first = HALO * COLS - HALO
    flat_ref[:, 0:first] = jnp.zeros((C, first), BF)
    last = (ROWS - HALO) * COLS - HALO
    flat_ref[:, last:] = jnp.zeros((C, LANES - last), BF)

    def unpacked(row, count):
        half = count // 2
        lines = weights_ref[row : row + half, :]
        tall[pl.ds(0, half, stride=2), :] = lines[:, :MID]
        tall[pl.ds(1, half, stride=2), :] = lines[:, MID:]
        return tall[0:count, :]

    for row, win_t, wf, wb, wout_t, wout, win in (
        (0, win_t1, wf1, wb1, wout_t1, wout1, None),
        (544, win_t2, wf2, wb2, wout_t2, wout2, win2),
    ):
        value = unpacked(row, C)
        win_t[...] = value.T.astype(BF)
        if win is not None:
            win[...] = value.astype(BF)
        value = jnp.concatenate([unpacked(row + 128 + r * 96, 3 * MID) for r in range(3)], axis=1)
        wb[...] = value.astype(BF)
        wf[...] = value.T.astype(BF)
        value = jnp.concatenate(
            [weights_ref[pl.ds(row + 416 + k, MID, stride=2), :] for k in range(2)], axis=1
        )
        wout[...] = value.astype(BF)
        wout_t[...] = value.T.astype(BF)
    for j in range(16):
        tall[pl.ds(j, 16, stride=16), 0:CLASSES] = weights_ref[
            1088:1104, j * CLASSES : (j + 1) * CLASSES
        ]
    head_ref[...] = tall[:, 0:CLASSES]


def rim_kernel(place, own_ref, odd_ref, even_ref, _, rim_ref, up_ref, down_ref):
    row, col = place[0], place[1]
    lane = lax.broadcasted_iota(jnp.int32, (128, 128), 1)
    odd_col = lax.rem(col, 2) == 1
    odd, even = odd_ref[...].astype(F32), even_ref[...].astype(F32)
    from_left = jnp.where(col == 0, 0.0, jnp.where(odd_col, even, odd))
    from_right = jnp.where(col == 3, 0.0, jnp.where(odd_col, odd, even))
    low = jnp.where(lane < 64, from_left, pltpu.roll(from_right, 64, 1))
    high = jnp.where(lane < 64, pltpu.roll(from_left, 64, 1), from_right)
    rim = jnp.concatenate([low, high], axis=0).astype(BF)
    rim_ref[...] = rim
    odd_row = lax.rem(row, 2)
    corner = lax.broadcasted_iota(jnp.int32, (CORNERS, 128), 0)
    source = lax.broadcasted_iota(jnp.int32, (CORNERS, 128), 1)
    for ref, low in ((up_ref, odd_row), (down_ref, 1 - odd_row)):
        first = (1 - low) * (TILE_ROWS - HALO)
        ref[0:C, :] = own_ref[:, pl.ds(pl.multiple_of(first * 128, 128), HALO * 128)]
        wanted = 2 * first + jnp.where(corner < 4, corner, 64 + corner - 4)
        pick = ((source == wanted) & (corner < 8)).astype(F32).astype(BF)
        ref[C:, :] = nt(pick, rim).astype(BF)


def in_image(place, table, start, stop):
    row, col = place[0], place[1]
    r, c = table[3:4, start:stop], table[4:5, start:stop]
    r_low = jnp.where(row > 0, -HALO, 0).astype(F32)
    r_high = jnp.where(row < 15, TILE_ROWS + HALO, TILE_ROWS).astype(F32)
    c_low = jnp.where(col > 0, -HALO, 0).astype(F32)
    c_high = jnp.where(col < 3, 2 * TILE_COLS + HALO, 2 * TILE_COLS).astype(F32)
    inside = (r >= r_low) & (r < r_high) & (c >= c_low) & (c < c_high)
    return jnp.where(inside, table[2:3, start:stop], 0.0)


def emit(phases):
    for pieces, work in phases:
        for start, stop in pieces:
            work(start, stop)


def put_rim(ref, rim, start, stop):
    for r in range(TILE_ROWS):
        for source, lane in (
            (2 * r, (r + HALO) * COLS),
            (64 + 2 * r, (r + HALO + 1) * COLS - HALO),
        ):
            if start <= lane and lane + HALO <= stop:
                ref[:, lane - start : lane - start + HALO] = rim[:, source : source + HALO]


def enter(inputs, win_t, h1, ranges, mask):
    def work(start, stop):
        value = jnp.maximum(nn(win_t[...], inputs.get(start, stop)).astype(BF), ZERO)
        if mask is not None:
            value = value * mask(start, stop).astype(BF)
        h1.put(start, stop, value)

    return ranges, work


def spread(h1, hs, ranges):
    def work(start, stop):
        for s in range(3):
            hs.put(start, stop, h1.shifted(start, stop, s - 1), slice(s * MID, (s + 1) * MID))

    return ranges, work


def widen(wf, hs, wide, ranges):
    def work(start, stop):
        wide.put(start, stop, nn(wf[...], hs.get(start, stop)))

    return ranges, work


def leave(inputs, wide, wout_t, h2, output, ranges):
    def work(start, stop):
        total = sum(
            wide.shifted(start, stop, (r - 1) * COLS, slice(r * MID, (r + 1) * MID))
            for r in range(3)
        )
        value = jnp.maximum(total.astype(BF), ZERO)
        h2.put(start, stop, value)
        total = nn(wout_t[...], value) + inputs.get(start, stop).astype(F32)
        output.put(start, stop, jnp.maximum(total.astype(BF), ZERO))

    return ranges, work


X_SPAN = (INNER - 512, OUTER + 512)
HS1_SPAN = (INNER - 384, OUTER + 384)
Y1_SPAN = (INNER - 256, OUTER + 256)
Y2_SPAN = (INNER, OUTER)


def inner_kernel(
    place,
    flat_ref,
    spot_ref,
    rim_ref,
    table,
    win_t1,
    wf1,
    wout_t1,
    win_t2,
    wf2,
    wout_t2,
    x_ref,
    h1a_ref,
    hs1_ref,
    h2a_ref,
    y1_ref,
    h1b_ref,
    hs2_ref,
    h2b_ref,
    y2_ref,
    wide_ref,
):
    x, h1a = whole(x_ref, X_SPAN[0]), whole(h1a_ref, X_SPAN[0])
    hs1 = whole(hs1_ref, HS1_SPAN[0])
    h2a, y1 = whole(h2a_ref, Y1_SPAN[0]), whole(y1_ref, Y1_SPAN[0])
    h1b, hs2 = whole(h1b_ref, Y1_SPAN[0] - 128), whole(hs2_ref, Y1_SPAN[0])
    h2b, y2 = whole(h2b_ref, Y2_SPAN[0]), whole(y2_ref, Y2_SPAN[0])
    wide = whole(wide_ref, X_SPAN[0])
    wide_ref[:, 0:128] = jnp.zeros((3 * MID, 128), F32)
    wide_ref[:, wide_ref.shape[1] - 128 :] = jnp.zeros((3 * MID, 128), F32)
    h1b_ref[:, 0:128] = jnp.zeros((MID, 128), BF)
    h1b_ref[:, h1b_ref.shape[1] - 128 :] = jnp.zeros((MID, 128), BF)

    def lay_out(start, stop):
        value = nn(rim_ref[...], spot_ref[:, start:stop]) + flat_ref[:, start:stop].astype(F32)
        x.put(start, stop, value.astype(BF))

    mask = lambda start, stop: in_image(place, table, start, stop)
    x_pieces, hs1_pieces = cut(*X_SPAN), cut(*HS1_SPAN)
    y1_pieces, y2_pieces = cut(*Y1_SPAN), cut(*Y2_SPAN)
    emit(
        [
            (x_pieces, lay_out),
            enter(x, win_t1, h1a, x_pieces, None),
            spread(h1a, hs1, hs1_pieces),
            widen(wf1, hs1, wide, hs1_pieces),
            leave(x, wide, wout_t1, h2a, y1, y1_pieces),
            enter(y1, win_t2, h1b, y1_pieces, mask),
            spread(h1b, hs2, y1_pieces),
            widen(wf2, hs2, wide, y1_pieces),
            leave(y1, wide, wout_t2, h2b, y2, y2_pieces),
        ]
    )


def rest_of(share):
    group = lax.div(share, 8)
    return 128 + 8 * lax.div(group, 3) + lax.rem(share, 8), lax.rem(group, 3)


def kernel(
    place,
    flat_ref,
    rim_ref,
    odd_ref,
    even_ref,
    table,
    momentum_ref,
    win_t1,
    wf1,
    wb1,
    wout_t1,
    wout1,
    win_t2,
    wf2,
    wb2,
    wout_t2,
    wout2,
    win2,
    head_ref,
    target_ref,
    x_mid,
    h1a_mid,
    hs1_mid,
    h2a_mid,
    y1_mid,
    h1b_mid,
    hs2_mid,
    h2b_mid,
    y2_mid,
    keep_ref,
    send_ref,
    packed,
    parts,
    x_ends,
    h1a_ends,
    hs1_ends,
    h2a_ends,
    y1_ends,
    h1b_ends,
    hs2_ends,
    h2b_ends,
    y2_ends,
    wide_ref,
    dg2_ref,
    ds,
    dz,
    tall,
):
    def joined(ends, mid, base):
        pad = (ends.shape[2] - CHUNK) // 2
        return Lanes(
            (-pad, INNER, ends.at[0], -pad),
            (INNER, OUTER, mid, base),
            (OUTER, LANES + pad, ends.at[1], OUTER - pad),
        )

    x = joined(x_ends, x_mid, X_SPAN[0])
    h1a = joined(h1a_ends, h1a_mid, X_SPAN[0])
    hs1 = joined(hs1_ends, hs1_mid, HS1_SPAN[0])
    h2a = joined(h2a_ends, h2a_mid, Y1_SPAN[0])
    y1 = joined(y1_ends, y1_mid, Y1_SPAN[0])
    h1b = joined(h1b_ends, h1b_mid, Y1_SPAN[0] - 128)
    hs2 = joined(hs2_ends, hs2_mid, Y1_SPAN[0])
    h2b = joined(h2b_ends, h2b_mid, Y2_SPAN[0])
    y2 = joined(y2_ends, y2_mid, Y2_SPAN[0])
    wide, dg2 = whole(wide_ref, -GUARD), whole(dg2_ref, -GUARD)
    for ref in (wide_ref, dg2_ref):
        ref[:, :GUARD] = jnp.zeros((ref.shape[0], GUARD), ref.dtype)
        ref[:, GUARD + LANES :] = jnp.zeros((ref.shape[0], GUARD), ref.dtype)
    for ref in (h1a_ends, h1b_ends):
        ref[0, :, 0:128] = jnp.zeros((MID, 128), BF)
        ref[1, :, CHUNK + 128 :] = jnp.zeros((MID, 128), BF)

    odd_row = lax.rem(place[0], 2) == 1
    above = jnp.where(odd_row, even_ref[...].astype(F32), odd_ref[...].astype(F32)).astype(BF)
    below = jnp.where(odd_row, odd_ref[...].astype(F32), even_ref[...].astype(F32)).astype(BF)
    for end, start, stop, rows in ((0, 0, INNER, above), (1, OUTER, LANES, below)):
        ref = x_ends.at[end]
        ref[...] = flat_ref[:, start:stop]
        put_rim(ref, rim_ref, start, stop)
        corners = rows[C:, :].astype(F32).T.astype(BF)
        for k in range(HALO):
            lane = (k if end == 0 else ROWS - HALO + k) * COLS - start
            ref[:, lane : lane + HALO] = corners[:, 2 * k : 2 * k + 2]
            ref[:, lane + HALO : lane + HALO + 128] = rows[0:C, k * 128 : (k + 1) * 128]
            ref[:, lane + HALO + 128 : lane + COLS] = corners[:, 4 + 2 * k : 6 + 2 * k]
    ends = [(0, INNER), (OUTER, LANES)]
    wider = [(0, INNER + 256), (OUTER - 256, LANES)]
    mask = lambda start, stop: in_image(place, table, start, stop)
    everything = cut(0, LANES)
    sums = {"pooled": jnp.zeros((C, 8), F32)}

    def pool(start, stop):
        sums["pooled"] += nt(y2.get(start, stop), table[:, start:stop].astype(BF))

    for start, stop in cut(INNER, OUTER):
        pool(start, stop)
    emit(
        [
            enter(x, win_t1, h1a, ends, None),
            spread(h1a, hs1, ends),
            widen(wf1, hs1, wide, wider),
            leave(x, wide, wout_t1, h2a, y1, ends),
            enter(y1, win_t2, h1b, ends, mask),
            spread(h1b, hs2, ends),
            widen(wf2, hs2, wide, wider),
            leave(y1, wide, wout_t2, h2b, y2, ends),
            (ends, pool),
        ]
    )
    pooled = sums["pooled"] * (1.0 / (TILE_ROWS * TILE_COLS))
    head = head_ref[...]
    loss = jnp.zeros((1, 1), F32)
    grad_head = jnp.zeros((C, CLASSES), F32)
    upstream = []
    for tile in range(2):
        column = pooled[:, tile : tile + 1]
        logits = jnp.sum(column * head, axis=0, keepdims=True)
        highest = jnp.max(logits, axis=1, keepdims=True)
        logsum = jnp.log(jnp.sum(jnp.exp(logits - highest), axis=1, keepdims=True)) + highest
        onehot = target_ref[tile : tile + 1, :]
        loss = loss + logsum - jnp.sum(onehot * logits, axis=1, keepdims=True)
        dlogits = (jnp.exp(logits - logsum) - onehot) * (1.0 / NTILES)
        grad_head = grad_head + column * dlogits
        dpooled = jnp.sum(head * dlogits, axis=1, keepdims=True) / (TILE_ROWS * TILE_COLS)
        upstream.append(dpooled.astype(BF))

    own, one = cut(256, 3584), cut(0, 3584)
    dz[:, 0:256] = jnp.zeros((C, 256), BF)
    dg2_ref[:, GUARD : GUARD + 256] = jnp.zeros((MID, 256), BF)
    dg2_ref[:, GUARD + 3584 :] = jnp.zeros((MID, LANES - 3584 + GUARD), BF)

    def seed(start, stop):
        first, second = (table[t : t + 1, start:stop].astype(BF) for t in range(2))
        value = upstream[0] * first + upstream[1] * second
        dz[:, start:stop] = jnp.where(y2.get(start, stop) > ZERO, value, ZERO)

    def pack_tall(value, row):
        count = value.shape[0]
        tall[0:count, :] = value
        half = count // 2
        packed[row : row + half, 0:MID] = tall[pl.ds(0, half, stride=2), :]
        packed[row : row + half, MID:] = tall[pl.ds(1, half, stride=2), :]

    def backward(inputs, wb, wout, h1, hs, h2, row, then, near, far):
        grads = {
            "out": jnp.zeros((C, MID), F32),
            "mid": jnp.zeros((3 * MID, 3 * MID), F32),
            "in": jnp.zeros((C, MID), F32),
        }

        def to_mid(start, stop):
            value = dz[:, start:stop]
            grads["out"] += nt(value, h2.get(start, stop))
            value = nn(wout[...], value).astype(BF)
            dg2.put(start, stop, jnp.where(h2.get(start, stop) > ZERO, value, ZERO))
            if (start, stop) == near[-1]:
                total = grads["out"].T
                packed[pl.ds(row + 416, MID, stride=2), :] = total[:, :128]
                packed[pl.ds(row + 417, MID, stride=2), :] = total[:, 128:]

        def through_taps(start, stop):
            for r in range(3):
                ds[r * MID : (r + 1) * MID, start:stop] = dg2.shifted(start, stop, (1 - r) * COLS)
            value = ds[:, start:stop]
            wide.put(start, stop, nn(wb[...], value))
            grads["mid"] += nt(hs.get(start, stop), value)
            if (start, stop) == far[-1]:
                for r in range(3):
                    pack_tall(grads["mid"][:, r * MID : (r + 1) * MID], row + 128 + r * 96)

        def to_inputs(start, stop):
            total = sum(
                wide.shifted(start, stop, 1 - s, slice(s * MID, (s + 1) * MID)) for s in range(3)
            )
            value = jnp.where(h1.get(start, stop) > ZERO, total.astype(BF), ZERO)
            grads["in"] += nt(inputs.get(start, stop), value)
            if then is not None:
                then(start, stop, value)
            if (start, stop) == far[-1]:
                pack_tall(grads["in"], row)
                if then is not None:
                    pack_shares(8)

        return [(near, to_mid), (far, through_taps), (far, to_inputs)]

    def to_first(start, stop, value):
        total = nn(win2[...], value) + dz[:, start:stop].astype(F32)
        dz[:, start:stop] = jnp.where(y1.get(start, stop) > ZERO, total.astype(BF), ZERO)

    tall[:, 0:CLASSES] = grad_head
    for j in range(16):
        packed[1088:1104, j * CLASSES : (j + 1) * CLASSES] = tall[
            pl.ds(j, 16, stride=16), 0:CLASSES
        ]

    row, col, core, far = place[0], place[1], place[2], place[3]
    lane = lax.broadcasted_iota(jnp.int32, (8, 128), 1)

    def pack_shares(low):
        for m in range(16):
            m_col, m_far, m_core = m // 4, m // 2 % 2, m % 2
            first, offset = 69 * low + SHARE * m // 128, SHARE * m % 128
            lines = [
                pltpu.roll(packed[pl.ds(first + j, 8, stride=69), :], (128 - offset) % 128, 1)
                for j in range(6)
            ]
            block = parts.at[m_core ^ core, m_col ^ col]
            for j in range(4):
                begin = 32 * j + 16 * m_far + low
                block[begin : begin + 8, :] = jnp.where(lane < 128 - offset, lines[j], lines[j + 1])
            group = 2 * m_far + low // 8
            begin, at = 128 + 8 * (group // 3), REST * (group % 3)
            rest = [pltpu.roll(line, at, 1) if at else line for line in lines[4:6]]
            value = jnp.where(lane - at < 128 - offset, rest[0], rest[1])
            if group == 3:
                value = jnp.where(lane < REST, value, jnp.where(lane == 127, loss, 0.0))
                block[begin : begin + 8, :] = value
            elif group == 2:
                value = jnp.where(lane < at + REST, value, 0.0)
                block[begin : begin + 8, at:] = value[:, at:]
            else:
                block[begin : begin + 8, at : at + REST] = value[:, at : at + REST]

    emit(
        [(own, seed)]
        + backward(y1, wb2, wout2, h1b, hs2, h2b, 544, to_first, own, one)
        + backward(x, wb1, wout1, h1a, hs1, h2a, 0, None, one, everything)
    )

    pack_shares(0)
    mine = far * 16 + row
    for j in range(4):
        line = pl.ds(32 * j + mine, 1)
        parts[0, 0, line, :] += 9.0 * momentum_ref[:, j * 128 : (j + 1) * 128]
    line, turn = rest_of(mine)
    rest = 9.0 * momentum_ref[:, 512:]
    for k in range(3):
        parts[0, 0, pl.ds(line, 1), :] += jnp.where(turn == k, pltpu.roll(rest, REST * k, 1) if k else rest, 0.0)
    keep_ref[...] = parts[0]
    send_ref[...] = parts[1]


def total_kernel(place, own, got_a, got_b, got_c, row_ref, size_ref, total):
    total[...] = (own[...] + got_a[...]) + (got_b[...] + got_c[...])
    lane = lax.broadcasted_iota(jnp.int32, (LINES, 128), 1)
    line = lax.broadcasted_iota(jnp.int32, (LINES, 128), 0)
    kept = jnp.where((line >= LINES - 8) & (lane >= REST), 0.0, jnp.abs(total[...]))
    size = jnp.sum(jnp.sum(kept, axis=0, keepdims=True), axis=1, keepdims=True)
    size_ref[...] = jnp.broadcast_to(size, (1, PAD))
    mine = place[3] * 16 + place[0]
    for j in range(4):
        row_ref[:, j * 128 : (j + 1) * 128] = total[pl.ds(32 * j + mine, 1), :]
    at, turn = rest_of(mine)
    rest = total[pl.ds(at, 1), :]
    value = jnp.where(turn == 0, rest, 0.0)
    for k in (1, 2):
        value = value + jnp.where(turn == k, pltpu.roll(rest, 128 - REST * k, 1), 0.0)
    lane = lax.broadcasted_iota(jnp.int32, (1, 128), 1)
    loss = total[LINES - 1 : LINES, 127:128]
    row_ref[:, 512:] = jnp.where(lane < REST, value, jnp.where(lane == REST, loss, 0.0))


VMEM = pl.BlockSpec(memory_space=pltpu.VMEM)
SMEM = pl.BlockSpec(memory_space=pltpu.SMEM)
PARAMS = pltpu.CompilerParams(vmem_limit_bytes=36 * 1024 * 1024)


def shape(dims, kind):
    return jax.ShapeDtypeStruct(dims, kind)


def split(image):
    return pl.pallas_call(
        split_kernel,
        out_shape=(shape((C, TILE_ROWS * 128), BF), shape((C // 2, 128), BF), shape((C // 2, 128), BF)),
        in_specs=[VMEM],
        out_specs=(VMEM,) * 3,
        scratch_shapes=[
            pltpu.VMEM((C * TILE_ROWS, 128), F32),
            pltpu.VMEM((TILE_ROWS * 128, 128), BF),
        ],
        compiler_params=PARAMS,
    )(image)


def prepare(own, weights, table):
    square = shape((3 * MID, 3 * MID), BF)
    down, up = shape((MID, C), BF), shape((C, MID), BF)
    block = [down, square, square, up, down]
    return pl.pallas_call(
        prepare_kernel,
        out_shape=[shape((C, LANES), BF), shape((128, LANES), BF)] + block + block + [up, shape((C, CLASSES), F32)],
        in_specs=[VMEM] * 3,
        out_specs=[VMEM] * 14,
        scratch_shapes=[pltpu.VMEM((C, MID), F32)],
        compiler_params=PARAMS,
        cost_estimate=pl.CostEstimate(flops=0, bytes_accessed=6_000_000, transcendentals=0),
    )(own, weights.reshape(PARAM // 128, 128), table)


def rim(place, own, odd, even, after):
    return pl.pallas_call(
        rim_kernel,
        out_shape=(shape((C, 128), BF), shape(MSG, BF), shape(MSG, BF)),
        in_specs=[SMEM] + [VMEM] * 4,
        out_specs=(VMEM,) * 3,
        compiler_params=PARAMS,
    )(place, own, odd, even, after)


def inner(place, flat, spot, beyond, table, mats):
    win_t1, wf1, _, wout_t1, _, win_t2, wf2, _, wout_t2 = mats[:9]
    spans = [
        (C, X_SPAN),
        (MID, X_SPAN),
        (3 * MID, HS1_SPAN),
        (MID, Y1_SPAN),
        (C, Y1_SPAN),
        (MID, (Y1_SPAN[0] - 128, Y1_SPAN[1] + 128)),
        (3 * MID, Y1_SPAN),
        (MID, Y2_SPAN),
        (C, Y2_SPAN),
    ]
    return pl.pallas_call(
        inner_kernel,
        out_shape=[shape((rows, stop - start), BF) for rows, (start, stop) in spans],
        in_specs=[SMEM] + [VMEM] * 10,
        out_specs=[VMEM] * 9,
        scratch_shapes=[pltpu.VMEM((3 * MID, X_SPAN[1] - X_SPAN[0]), F32)],
        compiler_params=PARAMS,
        cost_estimate=pl.CostEstimate(
            flops=1_000_000_000, bytes_accessed=12_000_000, transcendentals=0
        ),
    )(place, flat, spot, beyond, table, win_t1, wf1, wout_t1, win_t2, wf2, wout_t2)


def compute(place, flat, beyond, odd, even, table, momentum, mats, mids):
    return pl.pallas_call(
        kernel,
        out_shape=(shape((4, LINES, 128), F32), shape((4, LINES, 128), F32)),
        in_specs=[SMEM] + [VMEM] * 28,
        out_specs=(VMEM, VMEM),
        scratch_shapes=[
            pltpu.VMEM((PARAM // 128 + 8, 128), F32),
            pltpu.VMEM((2, 4, LINES, 128), F32),
            pltpu.VMEM((2, C, CHUNK), BF),
            pltpu.VMEM((2, MID, CHUNK + 256), BF),
            pltpu.VMEM((2, 3 * MID, CHUNK), BF),
            pltpu.VMEM((2, MID, CHUNK), BF),
            pltpu.VMEM((2, C, CHUNK), BF),
            pltpu.VMEM((2, MID, CHUNK + 256), BF),
            pltpu.VMEM((2, 3 * MID, CHUNK), BF),
            pltpu.VMEM((2, MID, CHUNK), BF),
            pltpu.VMEM((2, C, CHUNK), BF),
            pltpu.VMEM((3 * MID, WIDE), F32),
            pltpu.VMEM((MID, WIDE), BF),
            pltpu.VMEM((3 * MID, LANES), BF),
            pltpu.VMEM((C, LANES), BF),
            pltpu.VMEM((C, MID), F32),
        ],
        compiler_params=PARAMS,
    )(place, flat, beyond, odd, even, table, momentum, *mats, *mids)


def make_table():
    pixel = np.arange(LANES)
    r, c = pixel // COLS - HALO, pixel % COLS - HALO
    real = pixel < PIX
    inside = real & (r >= 0) & (r < TILE_ROWS)
    tiles = [inside & (c >= t * TILE_COLS) & (c < (t + 1) * TILE_COLS) for t in range(2)]
    near = real & (r >= -1) & (r <= TILE_ROWS) & (c >= -1) & (c <= 2 * TILE_COLS)
    lane = np.where(c < 0, 2 * r + c + HALO, np.where(c >= 128, 64 + 2 * r + c - 128, -1000))
    lane = np.where(real & (r >= 0) & (r < TILE_ROWS), lane, -1000)
    return jnp.asarray(np.stack([*tiles, near, r, c, lane, 0 * r, 0 * r]).astype(np.float32))


def local(image, labels, weights, momentum):
    row, col, dp = lax.axis_index("row"), lax.axis_index("col"), lax.axis_index("dp")
    place = jnp.stack([row, col, dp % 2, dp // 2]).astype(jnp.int32)
    table = make_table()
    targets = (labels.reshape(2, 1) == jnp.arange(CLASSES, dtype=jnp.int32)).astype(F32)
    padded_momentum = jnp.pad(momentum, (0, PAD - SHARE)).reshape(1, PAD)

    own, left, right = split(image)
    odd_col = col % 2 == 1
    odd = lax.ppermute(jnp.where(odd_col, right, left), "col", neighbours(4, True, True))
    even = lax.ppermute(jnp.where(odd_col, left, right), "col", neighbours(4, False))
    flat, spot, *mats = prepare(own, weights, table)
    beyond, up, down = rim(place, own, odd, even, mats[-1])
    odd = lax.ppermute(down, "row", neighbours(16, True))
    even = lax.ppermute(up, "row", neighbours(16, False))
    mids = inner(place, flat, spot, beyond, table, mats)
    keep, send = compute(
        place, flat, beyond, odd, even, table, padded_momentum, [*mats, targets], mids
    )

    parts = keep + received([send], CORE)[0]
    parts = paired_sum(parts[0], received([parts[2], parts[3], parts[1]], X_RING))
    for stage in (Y_RING, Z_PAIR):
        parts = stage_sum(parts, stage)
    got = received([parts] * 3, Z_RING)
    share, magnitude = pl.pallas_call(
        total_kernel,
        out_shape=(shape((1, PAD), F32), shape((1, PAD), F32)),
        in_specs=[SMEM] + [VMEM] * 4,
        out_specs=(VMEM, VMEM),
        scratch_shapes=[pltpu.VMEM((LINES, 128), F32)],
        compiler_params=PARAMS,
    )(place, parts, *got)
    for stage in (CORE, X_RING):
        magnitude = stage_sum(magnitude, stage)
    scale_tau = 0.1 * magnitude[0, :SHARE] / PARAM + 1e-06
    loss = share[0, SHARE] / NTILES
    share = share[0, :SHARE]
    mixed = 0.1 * share
    update = mixed / (jnp.abs(mixed) + scale_tau)
    start = (row * 16 + col * 4 + dp) * SHARE
    weight_share = lax.dynamic_slice_in_dim(weights, start, SHARE, 0)
    new_weights = weight_share - 0.0001 * (update + 0.1 * weight_share)
    new_momentum = 0.9 * momentum + 0.01 * share
    return (new_weights, new_momentum, update, loss)


def solution(mesh):
    in_specs = (P("dp", None, "row", "col"), P("dp", "row", "col"), P(), P(("row", "col", "dp")))
    out_specs = (P(("row", "col", "dp")), P(("row", "col", "dp")), P(("row", "col", "dp")), P())
    return jax.shard_map(local, mesh=mesh, in_specs=in_specs, out_specs=out_specs, check_vma=False)
```
